32 devices in a mesh: gx: 4 (over z), gy: 4 (over x, core), gz: 2 (over y).
Axes of the slice: x: 2, y: 2, z: 4, core: 2. Of those that a mesh axis runs over, the one named last changes fastest.
Arguments:
- conductivity: float32 [16, 64, 512], P('gx', 'gz', 'gy'), may hold values from 0.2 to 5
- initial_guess: float32 [16, 64, 512], P('gx', 'gz', 'gy'), may hold values from -6 to 6
- right_side: float32 [16, 64, 512], P('gx', 'gz', 'gy')
Outputs:
- fine_solution: float32 [16, 64, 512], P('gx', 'gz', 'gy')
- level_one_solution: float32 [8, 32, 256], P('gx', 'gz', 'gy')
- level_two_solution: float32 [4, 16, 128], P(None, 'gz', 'gy')
- level_three_solution: float32 [2, 8, 64], P(None, 'gz', 'gy')
- level_three_residual: float32 [2, 8, 64], P(None, 'gz', 'gy')
The draws below stay inside these ranges and needn't reach their ends.
All inputs are finite; a program needn't handle non-finite values.
Results may differ from the reference program's by a relative error of at most 0.000034.
Values sent between devices are 32-bit elements; how exact they have to be, the bound alone decides.
A program may use at most 64 MiB of HBM per device.

```python
import math
import jax
import jax.numpy as jnp

SWEEPS = 3
NX = 16
NZ = 64
NY = 512


def draw_right_side(key, part):
    rough = jax.random.normal(key, (NX, NZ, NY), jnp.float32)
    rough = jnp.clip(rough, -6.0, 6.0)
    return rough


def block_scale(rng, dims, pieces, smallest, high):
    gain, own = 1.0, jax.random.fold_in(rng, 6)
    for position, shards_of in pieces:
        draws = jnp.exp(jax.random.uniform(jax.random.fold_in(own, position), (shards_of,), jnp.float32, smallest / len(pieces), high / len(pieces)))
        gain = gain * jnp.repeat(draws, dims[position] // shards_of).reshape([-1 if axis == position else 1 for axis in range(len(dims))])
    return gain


def normal_values(own_key, dims, scale, most, shards=(), kind=jnp.bfloat16):
    entries = jax.random.normal(own_key, dims, jnp.float32) * scale
    if len(shards) > 0:
        entries = block_scale(own_key, dims, shards, -0.22, 0.18) * entries
    return jnp.clip(entries, min=-most, max=most).astype(kind)


def setup_inputs(seed: int = 0) -> dict:
    key_list = jax.random.split(jax.random.key(seed), 4)
    return {
        "conductivity": jnp.clip(jnp.exp(math.log(5.0) - 3.218876 * jax.random.uniform(key_list[0], (NX, NZ, NY), jnp.float32) ** block_scale(key_list[0], (NX, NZ, NY), ((0, 4), (1, 2), (2, 4)), -0.2, 0.2)), 0.2, 5.0),
        "initial_guess": normal_values(key_list[1], (NX, NZ, NY), 1.0, 6.0, ((0, 4), (1, 2), (2, 4)), jnp.float32),
        "right_side": draw_right_side(jax.random.fold_in(key_list[3], 71), 0),
    }


lower_bound = 0.25
upper_bound = 2.0


def neighbours(padded):
    return [padded[:-2, 1:-1, 1:-1], padded[2:, 1:-1, 1:-1],
            padded[1:-1, :-2, 1:-1], padded[1:-1, 2:, 1:-1],
            padded[1:-1, 1:-1, :-2], padded[1:-1, 1:-1, 2:]]


def face_terms(conduct):
    others = neighbours(jnp.pad(conduct, 1))
    weights = [0.5 * (conduct + other) for other in others]
    diagonal = weights[0] + weights[1] + weights[2] + weights[3] + weights[4] + weights[5]
    return weights, diagonal


def operate(field, weights, diagonal):
    others = neighbours(jnp.pad(field, 1))
    result = diagonal * field
    for face_index in range(6):
        result = result - weights[face_index] * others[face_index]
    return result


def smooth(source, start, conduct):
    theta = 0.5 * (upper_bound + lower_bound)
    delta = 0.5 * (upper_bound - lower_bound)
    sigma = theta / delta
    weights, diagonal = face_terms(conduct)
    if start is None:
        solution = jnp.zeros_like(source)
        residual = source
    else:
        solution = start
        residual = source - operate(start, weights, diagonal)
    direction = residual / (theta * diagonal)
    ratio_now = 1.0 / sigma
    for sweep_index in range(SWEEPS):
        solution = solution + direction
        residual = residual - operate(direction, weights, diagonal)
        if sweep_index + 1 < SWEEPS:
            ratio_next = 1.0 / (2.0 * sigma - ratio_now)
            direction = (ratio_next * ratio_now) * direction + (2.0 * ratio_next / delta) * residual / diagonal
            ratio_now = ratio_next
    return solution, residual


def coarse_sum(field):
    first, second, third = field.shape
    blocks = field.reshape(first // 2, 2, second // 2, 2, third // 2, 2)
    return jnp.sum(blocks, axis=(1, 3, 5))


def reference(conductivity, initial_guess, right_side):
    fine_solution, residual_zero = smooth(right_side, initial_guess, conductivity)
    conduct_one = 0.125 * coarse_sum(conductivity)
    level_one_solution, residual_one = smooth(0.25 * coarse_sum(residual_zero), None, conduct_one)
    conduct_two = 0.125 * coarse_sum(conduct_one)
    level_two_solution, residual_two = smooth(0.25 * coarse_sum(residual_one), None, conduct_two)
    conduct_three = 0.125 * coarse_sum(conduct_two)
    level_three_solution, level_three_residual = smooth(0.25 * coarse_sum(residual_two), None, conduct_three)
    return fine_solution, level_one_solution, level_two_solution, level_three_solution, level_three_residual
```

```python
import functools

import jax
import jax.numpy as jnp
from jax import lax
from jax.experimental import pallas as pl
from jax.experimental.pallas import tpu as pltpu
from jax.sharding import PartitionSpec as P

SWEEPS = 3


lower_bound = 0.25
upper_bound = 2.0


def with_halo(block, sides, width):
    for axis, dim in sides:
        count = lax.axis_size(axis)
        forward = [(i, i + 1) for i in range(count - 1)]
        backward = [(target, source) for source, target in forward]
        low = lax.ppermute(
            lax.slice_in_dim(block, block.shape[dim] - width, None, axis=dim), axis, forward
        )
        high = lax.ppermute(lax.slice_in_dim(block, 0, width, axis=dim), axis, backward)
        block = jnp.concatenate([low, block, high], axis=dim)
    return block


def extend(bundle):
    return with_halo(bundle, (("gx", 1), ("gy", 3), ("gz", 2)), 1)


def deep_extend(bundle, merged):
    if merged:
        grown = with_halo(bundle, (("gy", 3), ("gz", 2)), 4)
        return jnp.pad(grown, ((0, 0), (4, 4), (0, 0), (0, 0)))
    return with_halo(bundle, (("gx", 1), ("gy", 3), ("gz", 2)), 4)


def neighbours(padded):
    return [
        padded[:-2, 1:-1, 1:-1],
        padded[2:, 1:-1, 1:-1],
        padded[1:-1, :-2, 1:-1],
        padded[1:-1, 2:, 1:-1],
        padded[1:-1, 1:-1, :-2],
        padded[1:-1, 1:-1, 2:],
    ]


def face_terms(conduct):
    others = neighbours(extend(conduct[None])[0])
    weights = [0.5 * (conduct + other) for other in others]
    diagonal = weights[0] + weights[1] + weights[2] + weights[3] + weights[4] + weights[5]
    return (weights, diagonal)


def operate(field, weights, diagonal):
    others = neighbours(extend(field[None])[0])
    result = diagonal * field
    for face_index in range(6):
        result = result - weights[face_index] * others[face_index]
    return result


def smooth(source, conduct):
    theta = 0.5 * (upper_bound + lower_bound)
    delta = 0.5 * (upper_bound - lower_bound)
    sigma = theta / delta
    weights, diagonal = face_terms(conduct)
    solution = jnp.zeros_like(source)
    residual = source
    direction = residual / (theta * diagonal)
    ratio_now = 1.0 / sigma
    for sweep_index in range(SWEEPS):
        solution = solution + direction
        residual = residual - operate(direction, weights, diagonal)
        if sweep_index + 1 < SWEEPS:
            ratio_next = 1.0 / (2.0 * sigma - ratio_now)
            direction = (
                ratio_next * ratio_now * direction + 2.0 * ratio_next / delta * residual / diagonal
            )
            ratio_now = ratio_next
    return (solution, residual)


def local_operate(field, weights, diagonal):
    others = neighbours(jnp.pad(field, 1))
    result = diagonal * field
    for face_index in range(6):
        result = result - weights[face_index] * others[face_index]
    return result


def smooth_deep(source, start, conduct, merged):
    theta = 0.5 * (upper_bound + lower_bound)
    delta = 0.5 * (upper_bound - lower_bound)
    sigma = theta / delta
    members = [conduct, source, jnp.ones_like(source)]
    if start is not None:
        members.append(start)
    grown = deep_extend(jnp.stack(members), merged)
    padded_conduct = grown[0]
    padded_source = grown[1]
    inside = grown[2]
    others = neighbours(jnp.pad(padded_conduct, 1))
    weights = [0.5 * (padded_conduct + other) for other in others]
    diagonal = weights[0] + weights[1] + weights[2] + weights[3] + weights[4] + weights[5]
    safe_diagonal = jnp.where(inside > 0.5, diagonal, 1.0)
    if start is None:
        solution = jnp.zeros_like(padded_source)
        residual = padded_source
    else:
        solution = grown[3]
        residual = padded_source - local_operate(solution, weights, diagonal)
    direction = inside * (residual / (theta * safe_diagonal))
    ratio_now = 1.0 / sigma
    for sweep_index in range(SWEEPS):
        solution = solution + direction
        residual = residual - local_operate(direction, weights, diagonal)
        if sweep_index + 1 < SWEEPS:
            ratio_next = 1.0 / (2.0 * sigma - ratio_now)
            direction = inside * (
                ratio_next * ratio_now * direction
                + 2.0 * ratio_next / delta * residual / safe_diagonal
            )
            ratio_now = ratio_next
    return (solution[4:-4, 4:-4, 4:-4], residual[4:-4, 4:-4, 4:-4])


def level_smooth(source, start, conduct, merged):
    extents = source.shape[1:] if merged else source.shape
    if min(extents) >= 4:
        return smooth_deep(source, start, conduct, merged)
    return smooth(source, conduct)


def coarse_sum(field):
    first, second, third = field.shape
    blocks = field.reshape(first // 2, 2, second // 2, 2, third // 2, 2)
    return jnp.sum(blocks, axis=(1, 3, 5))


def shards(conductivity, initial_guess, right_side):
    fine_solution, residual_zero = level_smooth(right_side, initial_guess, conductivity, False)
    conduct_one = 0.125 * coarse_sum(conductivity)
    level_one_solution, residual_one = level_smooth(
        0.25 * coarse_sum(residual_zero), None, conduct_one, False
    )
    conduct_two = 0.125 * coarse_sum(conduct_one)
    source_two = 0.25 * coarse_sum(residual_one)
    bundle = jnp.stack([source_two, conduct_two])
    bundle = lax.all_gather(bundle, "gx", axis=1, tiled=True)
    level_two_solution, residual_two = level_smooth(bundle[0], None, bundle[1], True)
    conduct_three = 0.125 * coarse_sum(bundle[1])
    level_three_solution, level_three_residual = level_smooth(
        0.25 * coarse_sum(residual_two), None, conduct_three, True
    )
    return (
        fine_solution,
        level_one_solution,
        level_two_solution,
        level_three_solution,
        level_three_residual,
    )


FIELDS = 3
WIDTH = 4
ROWS = 8
LANES = 128


def in_range(index, count):
    return (index >= 0) & (index < count)


def shift(value, amount, axis):
    return pltpu.roll(value, amount % value.shape[axis], axis)


def smooth_planes(conduct, source, start, grown):
    theta = 0.5 * (upper_bound + lower_bound)
    delta = 0.5 * (upper_bound - lower_bound)
    sigma = theta / delta
    count = len(conduct)
    edge = 1 if grown else 0
    weight_x = [None] * (count + 1)
    for i in range(1, count):
        weight_x[i] = 0.5 * (conduct[i - 1] + conduct[i])
    if not grown:
        weight_x[0] = 0.5 * conduct[0]
        weight_x[count] = 0.5 * conduct[count - 1]
    weight_z = [None] * count
    weight_y = [None] * count
    inverse = [None] * count
    for i in range(edge, count - edge):
        weight_z[i] = 0.5 * (conduct[i] + shift(conduct[i], -1, 0))
        weight_y[i] = 0.5 * (conduct[i] + shift(conduct[i], -1, 1))
        diagonal = weight_x[i] + weight_x[i + 1]
        diagonal = diagonal + (weight_z[i] + shift(weight_z[i], 1, 0))
        diagonal = diagonal + (weight_y[i] + shift(weight_y[i], 1, 1))
        inside = conduct[i] > 0.0
        inverse[i] = jnp.where(inside, 1.0 / jnp.where(inside, diagonal, 1.0), 0.0)

    def operate_planes(field, low, high):
        flux_x = [None] * (count + 1)
        for i in range(low, high + 1):
            if i == 0:
                flux_x[i] = weight_x[i] * field[i]
            elif i == count:
                flux_x[i] = -(weight_x[i] * field[i - 1])
            else:
                flux_x[i] = weight_x[i] * (field[i] - field[i - 1])
        result = [None] * count
        for i in range(low, high):
            flux_z = weight_z[i] * (field[i] - shift(field[i], -1, 0))
            flux_y = weight_y[i] * (field[i] - shift(field[i], -1, 1))
            result[i] = (
                (flux_x[i] - flux_x[i + 1])
                + (flux_z - shift(flux_z, 1, 0))
                + (flux_y - shift(flux_y, 1, 1))
            )
        return result

    low, high = edge, count - edge
    residual = list(source)
    if start is not None:
        applied = operate_planes(start, low, high)
        for i in range(low, high):
            residual[i] = source[i] - applied[i]
    direction = [None] * count
    for i in range(low, high):
        direction[i] = residual[i] * (inverse[i] * (1.0 / theta))
    ratio_now = 1.0 / sigma
    solution = list(start) if start is not None else [None] * count
    for sweep_index in range(SWEEPS):
        for i in range(low, high):
            solution[i] = direction[i] if solution[i] is None else solution[i] + direction[i]
        low, high = low + edge, high - edge
        applied = operate_planes(direction, low, high)
        for i in range(low, high):
            residual[i] = residual[i] - applied[i]
        if sweep_index + 1 < SWEEPS:
            ratio_next = 1.0 / (2.0 * sigma - ratio_now)
            turned = [None] * count
            for i in range(low, high):
                turned[i] = (ratio_next * ratio_now) * direction[i] + (
                    2.0 * ratio_next / delta
                ) * (residual[i] * inverse[i])
            direction = turned
            ratio_now = ratio_next
    return solution, residual


def split_dot(value, matrix):
    parts = []
    rest = value
    for _ in range(3):
        part = rest.astype(jnp.bfloat16)
        parts.append(part.astype(jnp.float32))
        rest = rest - parts[-1]
    rows = value.shape[0]
    stacked = jnp.concatenate(parts, axis=0).astype(jnp.bfloat16)
    product = jnp.dot(stacked, matrix, preferred_element_type=jnp.float32)
    return product[:rows] + product[rows : 2 * rows] + product[2 * rows :]


def pair_matrix(keep_low, keep_high, offset):
    source = lax.broadcasted_iota(jnp.int32, (LANES, LANES), 0)
    target = lax.broadcasted_iota(jnp.int32, (LANES, LANES), 1)
    low = (source < keep_low) & (target == offset + source // 2)
    high = (source >= LANES - keep_high) & (target == LANES // 2 + source // 2)
    return jnp.where(low | high, 1.0, 0.0).astype(jnp.bfloat16)


def pair_rows(value, hold):
    rows = value.shape[0]
    hold[0:rows, :] = value
    return hold[pl.ds(0, rows // 2, stride=2), :] + hold[pl.ds(1, rows // 2, stride=2), :]


def kernel(sizes, *refs):
    count_x, count_y, count_z = sizes
    inputs = refs[0:3]
    out_fine, out_one, out_two, out_three, out_rest = refs[3:8]
    grown = refs[8:11]
    (pack_full, pack_edge, pack_rows, got_full, got_edge, got_rows, own_one, own_half, all_one,
     all_half, hold, solved_one, solved_fine, load_sem, face_send, face_recv, row_send, row_recv,
     full_send, full_recv, edge_send, edge_recv, one_send, one_recv, store_sem) = refs[11:]
    planes, rows = inputs[0].shape[0], inputs[0].shape[1]
    x = lax.axis_index("gx")
    y = lax.axis_index("gy")
    z = lax.axis_index("gz")
    first_z = z == 0

    loads = []
    for f in range(FIELDS):
        loads.append(pltpu.make_async_copy(
            inputs[f], grown[f].at[planes : 2 * planes, 0:rows, 0:LANES], load_sem.at[f]))
        loads[-1].start()

    def other(step, turn, dy):
        return {"gx": lax.rem(x + step, count_x), "gy": y + dy, "gz": lax.rem(z + turn, count_z)}

    partners = [
        (step, turn, dy)
        for step in range(count_x)
        for turn in range(count_z)
        for dy in (0, -1, 1)
        if (step, turn, dy) != (0, 0, 0)
    ]
    barrier = pltpu.get_barrier_semaphore()
    for dy in (0, -1, 1):
        @pl.when(in_range(y + dy, count_y))
        def _():
            chosen = [p for p in partners if p[2] == dy]
            for step, turn, _dy in chosen:
                pl.semaphore_signal(
                    barrier, inc=1, device_id=other(step, turn, dy),
                    device_id_type=pl.DeviceIdType.MESH)

    for f in range(FIELDS):
        @pl.when(x == 0)
        def _():
            grown[f][0:planes, 0:rows, 0:LANES] = jnp.zeros((planes, rows, LANES), jnp.float32)

        @pl.when(x == count_x - 1)
        def _():
            grown[f][2 * planes : 3 * planes, 0:rows, 0:LANES] = jnp.zeros(
                (planes, rows, LANES), jnp.float32)

    for slot in range(3):
        for side in range(2):
            there = in_range(x + (slot - 1), count_x) & in_range(y + (2 * side - 1), count_y)

            @pl.when(jnp.logical_not(there))
            def _():
                got_full[slot, side] = jnp.zeros((rows, LANES), jnp.float32)
                got_edge[slot, side] = jnp.zeros((ROWS, LANES), jnp.float32)

        if slot != 1:
            @pl.when(jnp.logical_not(in_range(x + (slot - 1), count_x)))
            def _():
                got_rows[slot] = jnp.zeros((FIELDS * planes, ROWS, LANES), jnp.float32)

    for side in range(2):
        @pl.when(jnp.logical_not(in_range(y + (2 * side - 1), count_y)))
        def _():
            for part in range(2):
                all_half[part, side] = jnp.zeros(all_half.shape[2:], jnp.float32)

    for load in loads:
        load.wait()

    lane = lax.broadcasted_iota(jnp.int32, (rows, LANES), 1)
    packed = jnp.zeros((rows, LANES), jnp.float32)
    for f in range(FIELDS):
        for q in range(planes):
            k = f * planes + q
            piece = grown[f][planes + q, 0:rows, 0:LANES]
            pack_rows[k] = jnp.where(first_z, piece[rows - ROWS :], piece[0:ROWS])
            moved = shift(piece, 2 * WIDTH * k, 1)
            window = lax.rem(lane - 2 * WIDTH * k + WIDTH + LANES, LANES) < 2 * WIDTH
            packed = jnp.where(window, moved, packed)
    pack_full[...] = packed
    pack_edge[...] = jnp.where(first_z, packed[rows - ROWS :], packed[0:ROWS])

    wanted = (count_x * count_z - 1) + count_x * count_z * (
        jnp.where(y > 0, 1, 0) + jnp.where(y < count_y - 1, 1, 0))
    pl.semaphore_wait(barrier, wanted)

    started = []

    def send(src, dst, send_sem, recv_sem, device, to, back):
        copy = pltpu.make_async_remote_copy(
            src_ref=src, dst_ref=dst, send_sem=send_sem, recv_sem=recv_sem,
            device_id=device, device_id_type=pl.DeviceIdType.MESH)
        if to is None:
            copy.start()
        else:
            pl.when(to)(copy.start)
        return copy, to, back

    def wait_recv(entry):
        copy, _, back = entry
        if back is None:
            copy.wait_recv()
        else:
            pl.when(back)(copy.wait_recv)

    def wait_send(entry):
        copy, to, _ = entry
        if to is None:
            copy.wait_send()
        else:
            pl.when(to)(copy.wait_send)

    fine = []
    for dx in (1, -1):
        to, back = in_range(x + dx, count_x), in_range(x - dx, count_x)
        for f in range(FIELDS):
            low, high = 0, planes
            if f == 2:
                low, high = (1, planes) if dx == 1 else (0, planes - 1)
            base = 0 if dx == 1 else 2 * planes
            fine.append(send(
                grown[f].at[planes + low : planes + high, 0:rows, 0:LANES],
                grown[f].at[base + low : base + high, 0:rows, 0:LANES],
                face_send.at[(dx + 1) // 2 * FIELDS + f], face_recv.at[(dx + 1) // 2 * FIELDS + f],
                {"gx": x + dx, "gy": y, "gz": z}, to, back))
    for dx in (0, 1, -1):
        slot = 1 - dx
        to, back = (in_range(x + dx, count_x), in_range(x - dx, count_x)) if dx else (None, None)
        fine.append(send(
            pack_rows, got_rows.at[slot], row_send.at[slot], row_recv.at[slot],
            {"gx": x + dx, "gy": y, "gz": 1 - z}, to, back))
    for dy in (1, -1):
        side = (1 - dy) // 2
        for dx in (0, 1, -1):
            slot = 1 - dx
            to = in_range(x + dx, count_x) & in_range(y + dy, count_y)
            back = in_range(x - dx, count_x) & in_range(y - dy, count_y)
            fine.append(send(
                pack_full, got_full.at[slot, side], full_send.at[slot * 2 + side],
                full_recv.at[slot * 2 + side], {"gx": x + dx, "gy": y + dy, "gz": z}, to, back))
            fine.append(send(
                pack_edge, got_edge.at[slot, side], edge_send.at[slot * 2 + side],
                edge_recv.at[slot * 2 + side], {"gx": x + dx, "gy": y + dy, "gz": 1 - z}, to, back))

    to_one = [pair_matrix(LANES, 0, 0), pair_matrix(LANES, 0, LANES // 2)]
    matrix_one = jnp.concatenate(to_one, axis=0)
    quarter = lax.broadcasted_iota(jnp.int32, (ROWS, LANES), 1) % (LANES // 2) < LANES // 4

    def restrict_fine(blocks, scale):
        pairs = [pair_rows(blocks[2 * q] + blocks[2 * q + 1], hold) for q in range(planes // 2)]
        return scale * split_dot(jnp.concatenate(pairs, axis=1), matrix_one)

    def spread(part, value):
        own_one[part] = value
        top, bottom = value[0:ROWS], value[ROWS : 2 * ROWS]
        own_half[part, 0] = jnp.where(quarter, top, shift(bottom, LANES // 4, 1))
        own_half[part, 1] = jnp.where(quarter, shift(bottom, -(LANES // 4), 1), top)
        all_one[part, x, z] = value
        entries = []
        for index, (step, turn, dy) in enumerate(partners):
            from_x, from_z = lax.rem(x + count_x - step, count_x), lax.rem(z + turn, count_z)
            here = (part, x, z)
            sems = (one_send.at[part, index], one_recv.at[part, index])
            device = other(step, turn, dy)
            if dy == 0:
                entry = send(own_one.at[part], all_one.at[part, x, z], *sems, device, None, None)
                landed = all_one.at[part, from_x, from_z]
                source = own_one.at[part]
                back = None
            else:
                side = (1 - dy) // 2
                source = own_half.at[part, 0 if dy < 0 else 1]
                entry = send(
                    source, all_half.at[part, side, x, z], *sems, device,
                    in_range(y + dy, count_y), None)
                landed = all_half.at[part, side, from_x, from_z]
                back = in_range(y - dy, count_y)
            arrival = pltpu.make_async_remote_copy(
                src_ref=source, dst_ref=landed, send_sem=sems[0], recv_sem=sems[1],
                device_id=device, device_id_type=pl.DeviceIdType.MESH)
            entries.append((entry, (arrival, None, back)))
        return entries

    conduct_entries = spread(
        0, restrict_fine([grown[0][planes + q, 0:rows, 0:LANES] for q in range(planes)], 0.125))

    for entry in fine:
        wait_recv(entry)

    row_index = lax.broadcasted_iota(jnp.int32, (ROWS, LANES), 0)
    row_keep = (row_index < WIDTH) == first_z
    lane_edge = lax.broadcasted_iota(jnp.int32, (rows + ROWS, LANES), 1)
    lane_keep = (lane_edge < WIDTH) | (lane_edge >= LANES - WIDTH)
    from_high = lax.rem(lane_edge, 2 * WIDTH) < WIDTH
    for slot in range(3):
        halves = []
        for side in range(2):
            halves.append(jnp.concatenate(
                [got_full[slot, side], jnp.where(row_keep, got_edge[slot, side], 0.0)], axis=0))
        joined = jnp.where(from_high, halves[1], halves[0])
        for f in range(FIELDS):
            for q in range(planes):
                k = f * planes + q
                p = slot * planes + q
                grown[f][p, rows : rows + ROWS, 0:LANES] = jnp.where(row_keep, got_rows[slot, k], 0.0)
                grown[f][p, :, LANES : 2 * LANES] = jnp.where(
                    lane_keep, shift(joined, -2 * WIDTH * k, 1), 0.0)

    solved, residual = smooth_planes(
        [grown[0][p] for p in range(3 * planes)],
        [None] + [grown[2][p] for p in range(1, 3 * planes - 1)] + [None],
        [grown[1][p] for p in range(3 * planes)],
        True,
    )
    source_entries = spread(
        1, restrict_fine([residual[planes + q][0:rows, 0:LANES] for q in range(planes)], 0.25))
    for q in range(planes):
        solved_fine[q] = solved[planes + q][0:rows, 0:LANES]
    store = pltpu.make_async_copy(solved_fine, out_fine, store_sem)
    store.start()

    lane_one = lax.broadcasted_iota(jnp.int32, (2 * ROWS, LANES), 1)
    lower = lane_one < LANES // 2
    empty = jnp.zeros((ROWS, LANES), jnp.float32)

    def assemble(part):
        level = []
        for from_x in range(count_x):
            blocks = [[], []]
            for from_z in range(count_z):
                own = all_one[part, from_x, from_z]
                low, high = all_half[part, 0, from_x, from_z], all_half[part, 1, from_x, from_z]
                beside = jnp.concatenate(
                    [jnp.where(quarter, high, low),
                     jnp.where(quarter, shift(high, -(LANES // 4), 1), shift(low, LANES // 4, 1))],
                    axis=0)
                blocks[0].append(jnp.where(lower, own, shift(beside, LANES // 2, 1)))
                blocks[1].append(jnp.where(lower, shift(own, LANES // 2, 1), beside))
            for q in range(2):
                level.append(jnp.concatenate(blocks[q] + [empty], axis=0))
        return level

    def restrict(level, matrix, scale):
        length = level[0].shape[0] - ROWS
        summed = []
        for q in range(len(level) // 2):
            both = level[2 * q] + level[2 * q + 1]
            summed.append(pair_rows(both[0:length], hold))
        joined = scale * split_dot(jnp.concatenate(summed, axis=0), matrix)
        half = length // 2
        return [
            jnp.concatenate([joined[q * half : (q + 1) * half], empty], axis=0)
            for q in range(len(summed))
        ]

    matrix_two = pair_matrix(3 * LANES // 4, LANES // 4, 0)
    matrix_three = pair_matrix(3 * LANES // 8, LANES // 8, 0)
    for _, arrival in conduct_entries:
        wait_recv(arrival)
    conduct_one = assemble(0)
    conduct_two = restrict(conduct_one, matrix_two, 0.125)
    conduct_three = restrict(conduct_two, matrix_three, 0.125)

    for _, arrival in source_entries:
        wait_recv(arrival)
    solved, residual = smooth_planes(conduct_one, assemble(1), None, False)
    for p in range(len(solved)):
        block = solved[p][0 : 2 * rows // 2]
        solved_one[p] = jnp.where(first_z, block[0 : rows // 2], block[rows // 2 : rows])
    out_one[...] = solved_one[pl.ds(2 * x, 2), :, 0 : LANES // 2]
    solved, residual = smooth_planes(
        conduct_two, restrict(residual, matrix_two, 0.25), None, False)
    for p in range(len(solved)):
        half = rows // 4
        out_two[p] = jnp.where(first_z, solved[p][0:half], solved[p][half : 2 * half])[:, 0 : LANES // 4]
    solved, residual = smooth_planes(
        conduct_three, restrict(residual, matrix_three, 0.25), None, False)
    for p in range(len(solved)):
        half = rows // 8
        for result, out in ((solved, out_three), (residual, out_rest)):
            out[p] = jnp.where(first_z, result[p][0:half], result[p][half : 2 * half])[:, 0 : LANES // 8]

    for entry in fine:
        wait_send(entry)
    for entry, _ in conduct_entries + source_entries:
        wait_send(entry)
    store.wait()


def fits(mesh, shape):
    return (
        mesh.shape["gz"] == 2
        and mesh.shape["gx"] <= 4
        and shape[0] == WIDTH * mesh.shape["gx"]
        and shape[1] == 32 * mesh.shape["gz"]
        and shape[2] == LANES * mesh.shape["gy"]
    )


def fused(mesh, conductivity, initial_guess, right_side):
    sizes = (mesh.shape["gx"], mesh.shape["gy"], mesh.shape["gz"])
    count_x, _, count_z = sizes
    planes, rows, lanes = conductivity.shape
    f32 = jnp.float32
    shapes = [
        (planes, rows, lanes),
        (planes // 2, rows // 2, lanes // 2),
        (count_x * planes // 4, rows // 4, lanes // 4),
        (count_x * planes // 8, rows // 8, lanes // 8),
        (count_x * planes // 8, rows // 8, lanes // 8),
    ]
    others = 3 * count_x * count_z - 1
    dma = pltpu.SemaphoreType.DMA
    scratch = [pltpu.VMEM((3 * planes, rows + ROWS, 2 * LANES), f32)] * FIELDS + [
        pltpu.VMEM((rows, LANES), f32),
        pltpu.VMEM((ROWS, LANES), f32),
        pltpu.VMEM((FIELDS * planes, ROWS, LANES), f32),
        pltpu.VMEM((3, 2, rows, LANES), f32),
        pltpu.VMEM((3, 2, ROWS, LANES), f32),
        pltpu.VMEM((3, FIELDS * planes, ROWS, LANES), f32),
        pltpu.VMEM((2, rows // 2, LANES), f32),
        pltpu.VMEM((2, 2, ROWS, LANES), f32),
        pltpu.VMEM((2, count_x, count_z, rows // 2, LANES), f32),
        pltpu.VMEM((2, 2, count_x, count_z, ROWS, LANES), f32),
        pltpu.VMEM((rows, LANES), f32),
        pltpu.VMEM((2 * count_x, rows // 2, LANES), f32),
        pltpu.VMEM((planes, rows, LANES), f32),
        dma((3,)),
        dma((6,)), dma((6,)),
        dma((3,)), dma((3,)),
        dma((6,)), dma((6,)),
        dma((6,)), dma((6,)),
        dma((2, others)), dma((2, others)),
        dma,
    ]
    vmem = pl.BlockSpec(memory_space=pltpu.VMEM)
    anywhere = pl.BlockSpec(memory_space=pl.ANY)
    return pl.pallas_call(
        functools.partial(kernel, sizes),
        out_shape=[jax.ShapeDtypeStruct(shape, f32) for shape in shapes],
        in_specs=[anywhere] * 3,
        out_specs=[anywhere] + [vmem] * 4,
        scratch_shapes=scratch,
        compiler_params=pltpu.CompilerParams(
            collective_id=0, has_side_effects=True, vmem_limit_bytes=32 * 2**20),
    )(conductivity, initial_guess, right_side)


def solution(mesh):
    placed = (P("gx", "gz", "gy"), P("gx", "gz", "gy"), P("gx", "gz", "gy"))

    def whole(conductivity, initial_guess, right_side):
        local = shards
        if fits(mesh, conductivity.shape):
            local = functools.partial(fused, mesh)
        return jax.shard_map(
            local,
            mesh=mesh,
            in_specs=placed,
            out_specs=(
                P("gx", "gz", "gy"),
                P("gx", "gz", "gy"),
                P(None, "gz", "gy"),
                P(None, "gz", "gy"),
                P(None, "gz", "gy"),
            ),
            check_vma=False,
        )(conductivity, initial_guess, right_side)

    return whole
```

```python
import functools

import jax
import jax.numpy as jnp
from jax import lax
from jax.experimental import pallas as pl
from jax.experimental.pallas import tpu as pltpu
from jax.sharding import PartitionSpec as P

SWEEPS = 3


lower_bound = 0.25
upper_bound = 2.0


def with_halo(block, sides, width):
    for axis, dim in sides:
        count = lax.axis_size(axis)
        forward = [(i, i + 1) for i in range(count - 1)]
        backward = [(target, source) for source, target in forward]
        low = lax.ppermute(
            lax.slice_in_dim(block, block.shape[dim] - width, None, axis=dim), axis, forward
        )
        high = lax.ppermute(lax.slice_in_dim(block, 0, width, axis=dim), axis, backward)
        block = jnp.concatenate([low, block, high], axis=dim)
    return block


def extend(bundle):
    return with_halo(bundle, (("gx", 1), ("gy", 3), ("gz", 2)), 1)


def deep_extend(bundle, merged):
    if merged:
        grown = with_halo(bundle, (("gy", 3), ("gz", 2)), 4)
        return jnp.pad(grown, ((0, 0), (4, 4), (0, 0), (0, 0)))
    return with_halo(bundle, (("gx", 1), ("gy", 3), ("gz", 2)), 4)


def neighbours(padded):
    return [
        padded[:-2, 1:-1, 1:-1],
        padded[2:, 1:-1, 1:-1],
        padded[1:-1, :-2, 1:-1],
        padded[1:-1, 2:, 1:-1],
        padded[1:-1, 1:-1, :-2],
        padded[1:-1, 1:-1, 2:],
    ]


def face_terms(conduct):
    others = neighbours(extend(conduct[None])[0])
    weights = [0.5 * (conduct + other) for other in others]
    diagonal = weights[0] + weights[1] + weights[2] + weights[3] + weights[4] + weights[5]
    return (weights, diagonal)


def operate(field, weights, diagonal):
    others = neighbours(extend(field[None])[0])
    result = diagonal * field
    for face_index in range(6):
        result = result - weights[face_index] * others[face_index]
    return result


def smooth(source, conduct):
    theta = 0.5 * (upper_bound + lower_bound)
    delta = 0.5 * (upper_bound - lower_bound)
    sigma = theta / delta
    weights, diagonal = face_terms(conduct)
    solution = jnp.zeros_like(source)
    residual = source
    direction = residual / (theta * diagonal)
    ratio_now = 1.0 / sigma
    for sweep_index in range(SWEEPS):
        solution = solution + direction
        residual = residual - operate(direction, weights, diagonal)
        if sweep_index + 1 < SWEEPS:
            ratio_next = 1.0 / (2.0 * sigma - ratio_now)
            direction = (
                ratio_next * ratio_now * direction + 2.0 * ratio_next / delta * residual / diagonal
            )
            ratio_now = ratio_next
    return (solution, residual)


def local_operate(field, weights, diagonal):
    others = neighbours(jnp.pad(field, 1))
    result = diagonal * field
    for face_index in range(6):
        result = result - weights[face_index] * others[face_index]
    return result


def smooth_deep(source, start, conduct, merged):
    theta = 0.5 * (upper_bound + lower_bound)
    delta = 0.5 * (upper_bound - lower_bound)
    sigma = theta / delta
    members = [conduct, source, jnp.ones_like(source)]
    if start is not None:
        members.append(start)
    grown = deep_extend(jnp.stack(members), merged)
    padded_conduct = grown[0]
    padded_source = grown[1]
    inside = grown[2]
    others = neighbours(jnp.pad(padded_conduct, 1))
    weights = [0.5 * (padded_conduct + other) for other in others]
    diagonal = weights[0] + weights[1] + weights[2] + weights[3] + weights[4] + weights[5]
    safe_diagonal = jnp.where(inside > 0.5, diagonal, 1.0)
    if start is None:
        solution = jnp.zeros_like(padded_source)
        residual = padded_source
    else:
        solution = grown[3]
        residual = padded_source - local_operate(solution, weights, diagonal)
    direction = inside * (residual / (theta * safe_diagonal))
    ratio_now = 1.0 / sigma
    for sweep_index in range(SWEEPS):
        solution = solution + direction
        residual = residual - local_operate(direction, weights, diagonal)
        if sweep_index + 1 < SWEEPS:
            ratio_next = 1.0 / (2.0 * sigma - ratio_now)
            direction = inside * (
                ratio_next * ratio_now * direction
                + 2.0 * ratio_next / delta * residual / safe_diagonal
            )
            ratio_now = ratio_next
    return (solution[4:-4, 4:-4, 4:-4], residual[4:-4, 4:-4, 4:-4])


def level_smooth(source, start, conduct, merged):
    extents = source.shape[1:] if merged else source.shape
    if min(extents) >= 4:
        return smooth_deep(source, start, conduct, merged)
    return smooth(source, conduct)


def coarse_sum(field):
    first, second, third = field.shape
    blocks = field.reshape(first // 2, 2, second // 2, 2, third // 2, 2)
    return jnp.sum(blocks, axis=(1, 3, 5))


def shards(conductivity, initial_guess, right_side):
    fine_solution, residual_zero = level_smooth(right_side, initial_guess, conductivity, False)
    conduct_one = 0.125 * coarse_sum(conductivity)
    level_one_solution, residual_one = level_smooth(
        0.25 * coarse_sum(residual_zero), None, conduct_one, False
    )
    conduct_two = 0.125 * coarse_sum(conduct_one)
    source_two = 0.25 * coarse_sum(residual_one)
    bundle = jnp.stack([source_two, conduct_two])
    bundle = lax.all_gather(bundle, "gx", axis=1, tiled=True)
    level_two_solution, residual_two = level_smooth(bundle[0], None, bundle[1], True)
    conduct_three = 0.125 * coarse_sum(bundle[1])
    level_three_solution, level_three_residual = level_smooth(
        0.25 * coarse_sum(residual_two), None, conduct_three, True
    )
    return (
        fine_solution,
        level_one_solution,
        level_two_solution,
        level_three_solution,
        level_three_residual,
    )


FIELDS = 3
WIDTH = 4
ROWS = 8
LANES = 128


def in_range(index, count):
    return (index >= 0) & (index < count)


def shift(value, amount, axis):
    return pltpu.roll(value, amount % value.shape[axis], axis)


def face_planes(conduct, grown):
    count = len(conduct)
    edge = 1 if grown else 0
    weight_x = [None] * (count + 1)
    for i in range(1, count):
        weight_x[i] = 0.5 * (conduct[i - 1] + conduct[i])
    if not grown:
        weight_x[0] = 0.5 * conduct[0]
        weight_x[count] = 0.5 * conduct[count - 1]
    weight_z = [None] * count
    weight_y = [None] * count
    inverse = [None] * count
    for i in range(edge, count - edge):
        weight_z[i] = 0.5 * (conduct[i] + shift(conduct[i], -1, 0))
        weight_y[i] = 0.5 * (conduct[i] + shift(conduct[i], -1, 1))
        diagonal = weight_x[i] + weight_x[i + 1]
        diagonal = diagonal + (weight_z[i] + shift(weight_z[i], 1, 0))
        diagonal = diagonal + (weight_y[i] + shift(weight_y[i], 1, 1))
        inside = conduct[i] > 0.0
        inverse[i] = jnp.where(inside, 1.0 / jnp.where(inside, diagonal, 1.0), 0.0)
    return weight_x, weight_y, weight_z, inverse


def operate_planes(faces, field, low, high):
    weight_x, weight_y, weight_z, _ = faces
    count = len(field)
    flux_x = [None] * (count + 1)
    for i in range(low, high + 1):
        if i == 0:
            flux_x[i] = weight_x[i] * field[i]
        elif i == count:
            flux_x[i] = -(weight_x[i] * field[i - 1])
        else:
            flux_x[i] = weight_x[i] * (field[i] - field[i - 1])
    result = [None] * count
    for i in range(low, high):
        flux_z = weight_z[i] * (field[i] - shift(field[i], -1, 0))
        flux_y = weight_y[i] * (field[i] - shift(field[i], -1, 1))
        result[i] = (
            (flux_x[i] - flux_x[i + 1])
            + (flux_z - shift(flux_z, 1, 0))
            + (flux_y - shift(flux_y, 1, 1))
        )
    return result


def smooth_planes(faces, source, start, grown):
    theta = 0.5 * (upper_bound + lower_bound)
    delta = 0.5 * (upper_bound - lower_bound)
    sigma = theta / delta
    inverse = faces[3]
    count = len(source)
    edge = 1 if grown else 0
    low, high = edge, count - edge
    residual = list(source)
    if start is not None:
        applied = operate_planes(faces, start, low, high)
        for i in range(low, high):
            residual[i] = source[i] - applied[i]
    direction = [None] * count
    for i in range(low, high):
        direction[i] = residual[i] * (inverse[i] * (1.0 / theta))
    ratio_now = 1.0 / sigma
    solution = list(start) if start is not None else [None] * count
    for sweep_index in range(SWEEPS):
        for i in range(low, high):
            solution[i] = direction[i] if solution[i] is None else solution[i] + direction[i]
        low, high = low + edge, high - edge
        applied = operate_planes(faces, direction, low, high)
        for i in range(low, high):
            residual[i] = residual[i] - applied[i]
        if sweep_index + 1 < SWEEPS:
            ratio_next = 1.0 / (2.0 * sigma - ratio_now)
            turned = [None] * count
            for i in range(low, high):
                turned[i] = (ratio_next * ratio_now) * direction[i] + (
                    2.0 * ratio_next / delta
                ) * (residual[i] * inverse[i])
            direction = turned
            ratio_now = ratio_next
    return solution, residual


def split_dot(value, matrix):
    parts = []
    rest = value
    for _ in range(3):
        part = rest.astype(jnp.bfloat16)
        parts.append(part.astype(jnp.float32))
        rest = rest - parts[-1]
    rows = value.shape[0]
    stacked = jnp.concatenate(parts, axis=0).astype(jnp.bfloat16)
    product = jnp.dot(stacked, matrix, preferred_element_type=jnp.float32)
    return product[:rows] + product[rows : 2 * rows] + product[2 * rows :]


def pair_matrix(keep_low, keep_high, offset):
    source = lax.broadcasted_iota(jnp.int32, (LANES, LANES), 0)
    target = lax.broadcasted_iota(jnp.int32, (LANES, LANES), 1)
    low = (source < keep_low) & (target == offset + source // 2)
    high = (source >= LANES - keep_high) & (target == LANES // 2 + source // 2)
    return jnp.where(low | high, 1.0, 0.0).astype(jnp.bfloat16)


def pair_rows(value, hold):
    rows = value.shape[0]
    hold[0:rows, :] = value
    return hold[pl.ds(0, rows // 2, stride=2), :] + hold[pl.ds(1, rows // 2, stride=2), :]


def kernel(sizes, *refs):
    count_x, count_y, count_z = sizes
    inputs = refs[0:3]
    outs = refs[3:8]
    grown = refs[8:11]
    (pack_full, pack_edge, pack_rows, got_full, got_edge, got_rows, own_one, own_half, all_one,
     all_half, hold, solved_one, out_fine, out_one, out_two,
     out_three, out_rest, load_sem, face_send, face_recv, row_send, row_recv,
     full_send, full_recv, edge_send, edge_recv, one_send, one_recv, store_sem) = refs[11:]
    kept = (out_fine, out_one, out_two, out_three, out_rest)
    stores = [pltpu.make_async_copy(kept[i], outs[i], store_sem.at[i]) for i in range(5)]
    planes, rows = inputs[0].shape[0], inputs[0].shape[1]
    x = lax.axis_index("gx")
    y = lax.axis_index("gy")
    z = lax.axis_index("gz")
    first_z = z == 0

    loads = []
    for f in range(FIELDS):
        loads.append(pltpu.make_async_copy(
            inputs[f], grown[f].at[planes : 2 * planes, 0:rows, 0:LANES], load_sem.at[f]))
        loads[-1].start()

    def other(step, turn, dy):
        return {"gx": lax.rem(x + step, count_x), "gy": y + dy, "gz": lax.rem(z + turn, count_z)}

    partners = [
        (step, turn, dy)
        for step in range(count_x)
        for turn in range(count_z)
        for dy in (0, -1, 1)
        if (step, turn, dy) != (0, 0, 0)
    ]
    barrier = pltpu.get_barrier_semaphore()
    for dy in (0, -1, 1):
        @pl.when(in_range(y + dy, count_y))
        def _():
            chosen = [p for p in partners if p[2] == dy]
            for step, turn, _dy in chosen:
                pl.semaphore_signal(
                    barrier, inc=1, device_id=other(step, turn, dy),
                    device_id_type=pl.DeviceIdType.MESH)

    for f in range(FIELDS):
        @pl.when(x == 0)
        def _():
            grown[f][0:planes, 0:rows, 0:LANES] = jnp.zeros((planes, rows, LANES), jnp.float32)

        @pl.when(x == count_x - 1)
        def _():
            grown[f][2 * planes : 3 * planes, 0:rows, 0:LANES] = jnp.zeros(
                (planes, rows, LANES), jnp.float32)

    for slot in range(3):
        for side in range(2):
            there = in_range(x + (slot - 1), count_x) & in_range(y + (2 * side - 1), count_y)

            @pl.when(jnp.logical_not(there))
            def _():
                got_full[slot, side] = jnp.zeros((rows, LANES), jnp.float32)
                got_edge[slot, side] = jnp.zeros((ROWS, LANES), jnp.float32)

        if slot != 1:
            @pl.when(jnp.logical_not(in_range(x + (slot - 1), count_x)))
            def _():
                got_rows[slot] = jnp.zeros((FIELDS * planes, ROWS, LANES), jnp.float32)

    for side in range(2):
        @pl.when(jnp.logical_not(in_range(y + (2 * side - 1), count_y)))
        def _():
            for part in range(2):
                all_half[part, side] = jnp.zeros(all_half.shape[2:], jnp.float32)

    for load in loads:
        load.wait()

    lane = lax.broadcasted_iota(jnp.int32, (rows, LANES), 1)
    packed = jnp.zeros((rows, LANES), jnp.float32)
    for f in range(FIELDS):
        for q in range(planes):
            k = f * planes + q
            piece = grown[f][planes + q, 0:rows, 0:LANES]
            pack_rows[k] = jnp.where(first_z, piece[rows - ROWS :], piece[0:ROWS])
            moved = shift(piece, 2 * WIDTH * k, 1)
            window = lax.rem(lane - 2 * WIDTH * k + WIDTH + LANES, LANES) < 2 * WIDTH
            packed = jnp.where(window, moved, packed)
    pack_full[...] = packed
    pack_edge[...] = jnp.where(first_z, packed[rows - ROWS :], packed[0:ROWS])

    wanted = (count_x * count_z - 1) + count_x * count_z * (
        jnp.where(y > 0, 1, 0) + jnp.where(y < count_y - 1, 1, 0))
    pl.semaphore_wait(barrier, wanted)

    started = []

    def send(src, dst, send_sem, recv_sem, device, to, back):
        copy = pltpu.make_async_remote_copy(
            src_ref=src, dst_ref=dst, send_sem=send_sem, recv_sem=recv_sem,
            device_id=device, device_id_type=pl.DeviceIdType.MESH)
        if to is None:
            copy.start()
        else:
            pl.when(to)(copy.start)
        return copy, to, back

    def wait_recv(entry):
        copy, _, back = entry
        if back is None:
            copy.wait_recv()
        else:
            pl.when(back)(copy.wait_recv)

    def wait_send(entry):
        copy, to, _ = entry
        if to is None:
            copy.wait_send()
        else:
            pl.when(to)(copy.wait_send)

    fine = []
    for dx in (1, -1):
        to, back = in_range(x + dx, count_x), in_range(x - dx, count_x)
        for f in range(FIELDS):
            low, high = 0, planes
            if f == 2:
                low, high = (1, planes) if dx == 1 else (0, planes - 1)
            base = 0 if dx == 1 else 2 * planes
            fine.append(send(
                grown[f].at[planes + low : planes + high, 0:rows, 0:LANES],
                grown[f].at[base + low : base + high, 0:rows, 0:LANES],
                face_send.at[(dx + 1) // 2 * FIELDS + f], face_recv.at[(dx + 1) // 2 * FIELDS + f],
                {"gx": x + dx, "gy": y, "gz": z}, to, back))
    for dx in (0, 1, -1):
        slot = 1 - dx
        to, back = (in_range(x + dx, count_x), in_range(x - dx, count_x)) if dx else (None, None)
        fine.append(send(
            pack_rows, got_rows.at[slot], row_send.at[slot], row_recv.at[slot],
            {"gx": x + dx, "gy": y, "gz": 1 - z}, to, back))
    for dy in (1, -1):
        side = (1 - dy) // 2
        for dx in (0, 1, -1):
            slot = 1 - dx
            to = in_range(x + dx, count_x) & in_range(y + dy, count_y)
            back = in_range(x - dx, count_x) & in_range(y - dy, count_y)
            fine.append(send(
                pack_full, got_full.at[slot, side], full_send.at[slot * 2 + side],
                full_recv.at[slot * 2 + side], {"gx": x + dx, "gy": y + dy, "gz": z}, to, back))
            fine.append(send(
                pack_edge, got_edge.at[slot, side], edge_send.at[slot * 2 + side],
                edge_recv.at[slot * 2 + side], {"gx": x + dx, "gy": y + dy, "gz": 1 - z}, to, back))

    to_one = [pair_matrix(LANES, 0, 0), pair_matrix(LANES, 0, LANES // 2)]
    matrix_one = jnp.concatenate(to_one, axis=0)
    quarter = lax.broadcasted_iota(jnp.int32, (ROWS, LANES), 1) % (LANES // 2) < LANES // 4

    def restrict_fine(blocks, scale):
        pairs = [pair_rows(blocks[2 * q] + blocks[2 * q + 1], hold) for q in range(planes // 2)]
        return scale * split_dot(jnp.concatenate(pairs, axis=1), matrix_one)

    def spread(part, value):
        own_one[part] = value
        top, bottom = value[0:ROWS], value[ROWS : 2 * ROWS]
        own_half[part, 0] = jnp.where(quarter, top, shift(bottom, LANES // 4, 1))
        own_half[part, 1] = jnp.where(quarter, shift(bottom, -(LANES // 4), 1), top)
        all_one[part, x, z] = value
        entries = []
        for index, (step, turn, dy) in enumerate(partners):
            from_x, from_z = lax.rem(x + count_x - step, count_x), lax.rem(z + turn, count_z)
            here = (part, x, z)
            sems = (one_send.at[part, index], one_recv.at[part, index])
            device = other(step, turn, dy)
            if dy == 0:
                entry = send(own_one.at[part], all_one.at[part, x, z], *sems, device, None, None)
                landed = all_one.at[part, from_x, from_z]
                source = own_one.at[part]
                back = None
            else:
                side = (1 - dy) // 2
                source = own_half.at[part, 0 if dy < 0 else 1]
                entry = send(
                    source, all_half.at[part, side, x, z], *sems, device,
                    in_range(y + dy, count_y), None)
                landed = all_half.at[part, side, from_x, from_z]
                back = in_range(y - dy, count_y)
            arrival = pltpu.make_async_remote_copy(
                src_ref=source, dst_ref=landed, send_sem=sems[0], recv_sem=sems[1],
                device_id=device, device_id_type=pl.DeviceIdType.MESH)
            entries.append((entry, (arrival, None, back)))
        return entries

    conduct_entries = spread(
        0, restrict_fine([grown[0][planes + q, 0:rows, 0:LANES] for q in range(planes)], 0.125))

    for entry in fine:
        wait_recv(entry)

    row_index = lax.broadcasted_iota(jnp.int32, (ROWS, LANES), 0)
    row_keep = (row_index < WIDTH) == first_z
    lane_edge = lax.broadcasted_iota(jnp.int32, (rows + ROWS, LANES), 1)
    lane_keep = (lane_edge < WIDTH) | (lane_edge >= LANES - WIDTH)
    from_high = lax.rem(lane_edge, 2 * WIDTH) < WIDTH
    for slot in range(3):
        halves = []
        for side in range(2):
            halves.append(jnp.concatenate(
                [got_full[slot, side], jnp.where(row_keep, got_edge[slot, side], 0.0)], axis=0))
        joined = jnp.where(from_high, halves[1], halves[0])
        for f in range(FIELDS):
            for q in range(planes):
                k = f * planes + q
                p = slot * planes + q
                grown[f][p, rows : rows + ROWS, 0:LANES] = jnp.where(row_keep, got_rows[slot, k], 0.0)
                grown[f][p, :, LANES : 2 * LANES] = jnp.where(
                    lane_keep, shift(joined, -2 * WIDTH * k, 1), 0.0)

    faces = face_planes([grown[0][p] for p in range(3 * planes)], True)
    solved, residual = smooth_planes(
        faces,
        [None] + [grown[2][p] for p in range(1, 3 * planes - 1)] + [None],
        [grown[1][p] for p in range(3 * planes)],
        True,
    )
    source_entries = spread(
        1, restrict_fine([residual[planes + q][0:rows, 0:LANES] for q in range(planes)], 0.25))
    for q in range(planes):
        out_fine[q] = solved[planes + q][0:rows, 0:LANES]
    stores[0].start()

    lane_one = lax.broadcasted_iota(jnp.int32, (2 * ROWS, LANES), 1)
    lower = lane_one < LANES // 2
    empty = jnp.zeros((ROWS, LANES), jnp.float32)

    def assemble(part):
        level = []
        for from_x in range(count_x):
            blocks = [[], []]
            for from_z in range(count_z):
                own = all_one[part, from_x, from_z]
                low, high = all_half[part, 0, from_x, from_z], all_half[part, 1, from_x, from_z]
                beside = jnp.concatenate(
                    [jnp.where(quarter, high, low),
                     jnp.where(quarter, shift(high, -(LANES // 4), 1), shift(low, LANES // 4, 1))],
                    axis=0)
                blocks[0].append(jnp.where(lower, own, shift(beside, LANES // 2, 1)))
                blocks[1].append(jnp.where(lower, shift(own, LANES // 2, 1), beside))
            for q in range(2):
                level.append(jnp.concatenate(blocks[q] + [empty], axis=0))
        return level

    def restrict(level, matrix, scale):
        length = level[0].shape[0] - ROWS
        summed = []
        for q in range(len(level) // 2):
            both = level[2 * q] + level[2 * q + 1]
            summed.append(pair_rows(both[0:length], hold))
        joined = scale * split_dot(jnp.concatenate(summed, axis=0), matrix)
        half = length // 2
        return [
            jnp.concatenate([joined[q * half : (q + 1) * half], empty], axis=0)
            for q in range(len(summed))
        ]

    matrix_two = pair_matrix(3 * LANES // 4, LANES // 4, 0)
    matrix_three = pair_matrix(3 * LANES // 8, LANES // 8, 0)
    for _, arrival in conduct_entries:
        wait_recv(arrival)
    conduct_one = assemble(0)
    conduct_two = restrict(conduct_one, matrix_two, 0.125)
    conduct_three = restrict(conduct_two, matrix_three, 0.125)
    faces_one, faces_two, faces_three = (
        face_planes(conduct, False) for conduct in (conduct_one, conduct_two, conduct_three))

    for _, arrival in source_entries:
        wait_recv(arrival)
    solved, residual = smooth_planes(faces_one, assemble(1), None, False)
    for p in range(len(solved)):
        block = solved[p][0 : 2 * rows // 2]
        solved_one[p] = jnp.where(first_z, block[0 : rows // 2], block[rows // 2 : rows])
    out_one[...] = solved_one[pl.ds(2 * x, 2), :, 0 : LANES // 2]
    stores[1].start()
    solved, residual = smooth_planes(
        faces_two, restrict(residual, matrix_two, 0.25), None, False)
    for p in range(len(solved)):
        half = rows // 4
        out_two[p] = jnp.where(first_z, solved[p][0:half], solved[p][half : 2 * half])[:, 0 : LANES // 4]
    stores[2].start()
    solved, residual = smooth_planes(
        faces_three, restrict(residual, matrix_three, 0.25), None, False)
    for p in range(len(solved)):
        half = rows // 8
        for result, out in ((solved, out_three), (residual, out_rest)):
            out[p] = jnp.where(first_z, result[p][0:half], result[p][half : 2 * half])[:, 0 : LANES // 8]

    stores[3].start()
    stores[4].start()
    for entry in fine:
        wait_send(entry)
    for entry, _ in conduct_entries + source_entries:
        wait_send(entry)
    for store in stores:
        store.wait()


def hand_over(*refs):
    count = len(refs) // 2
    copies = []
    for i in range(count):
        copies.append(pltpu.make_async_copy(refs[i], refs[count + i], refs[-1].at[i]))
        copies[-1].start()
    for copy in copies:
        copy.wait()


def fits(mesh, shape):
    return (
        mesh.shape["gz"] == 2
        and mesh.shape["gx"] <= 4
        and shape[0] == WIDTH * mesh.shape["gx"]
        and shape[1] == 32 * mesh.shape["gz"]
        and shape[2] == LANES * mesh.shape["gy"]
    )


def fused(mesh, conductivity, initial_guess, right_side):
    sizes = (mesh.shape["gx"], mesh.shape["gy"], mesh.shape["gz"])
    count_x, _, count_z = sizes
    planes, rows, lanes = conductivity.shape
    f32 = jnp.float32
    shapes = [
        (planes, rows, lanes),
        (planes // 2, rows // 2, lanes // 2),
        (count_x * planes // 4, rows // 4, lanes // 4),
        (count_x * planes // 8, rows // 8, lanes // 8),
        (count_x * planes // 8, rows // 8, lanes // 8),
    ]
    others = 3 * count_x * count_z - 1
    dma = pltpu.SemaphoreType.DMA
    scratch = [pltpu.VMEM((3 * planes, rows + ROWS, 2 * LANES), f32)] * FIELDS + [
        pltpu.VMEM((rows, LANES), f32),
        pltpu.VMEM((ROWS, LANES), f32),
        pltpu.VMEM((FIELDS * planes, ROWS, LANES), f32),
        pltpu.VMEM((3, 2, rows, LANES), f32),
        pltpu.VMEM((3, 2, ROWS, LANES), f32),
        pltpu.VMEM((3, FIELDS * planes, ROWS, LANES), f32),
        pltpu.VMEM((2, rows // 2, LANES), f32),
        pltpu.VMEM((2, 2, ROWS, LANES), f32),
        pltpu.VMEM((2, count_x, count_z, rows // 2, LANES), f32),
        pltpu.VMEM((2, 2, count_x, count_z, ROWS, LANES), f32),
        pltpu.VMEM((rows, LANES), f32),
        pltpu.VMEM((2 * count_x, rows // 2, LANES), f32),
        *[pltpu.VMEM(shape, f32) for shape in shapes],
        dma((3,)),
        dma((6,)), dma((6,)),
        dma((3,)), dma((3,)),
        dma((6,)), dma((6,)),
        dma((6,)), dma((6,)),
        dma((2, others)), dma((2, others)),
        dma((5,)),
    ]
    outside = pl.BlockSpec(memory_space=pltpu.HBM)
    out_shape = [jax.ShapeDtypeStruct(shape, f32) for shape in shapes]
    results = pl.pallas_call(
        functools.partial(kernel, sizes),
        out_shape=out_shape,
        in_specs=[outside] * 3,
        out_specs=[outside] * 5,
        scratch_shapes=scratch,
        compiler_params=pltpu.CompilerParams(
            collective_id=0, has_side_effects=True, vmem_limit_bytes=56 * 2**20),
    )(conductivity, initial_guess, right_side)
    return pl.pallas_call(
        hand_over,
        out_shape=out_shape,
        in_specs=[outside] * 5,
        out_specs=[outside] * 5,
        scratch_shapes=[dma((5,))],
        compiler_params=pltpu.CompilerParams(vmem_limit_bytes=56 * 2**20),
    )(*results)


def solution(mesh):
    placed = (P("gx", "gz", "gy"), P("gx", "gz", "gy"), P("gx", "gz", "gy"))

    def whole(conductivity, initial_guess, right_side):
        local = shards
        if fits(mesh, conductivity.shape):
            local = functools.partial(fused, mesh)
        return jax.shard_map(
            local,
            mesh=mesh,
            in_specs=placed,
            out_specs=(
                P("gx", "gz", "gy"),
                P("gx", "gz", "gy"),
                P(None, "gz", "gy"),
                P(None, "gz", "gy"),
                P(None, "gz", "gy"),
            ),
            check_vma=False,
        )(conductivity, initial_guess, right_side)

    return whole
```

```python
import functools

import jax
import jax.numpy as jnp
from jax import lax
from jax.experimental import pallas as pl
from jax.experimental.pallas import tpu as pltpu
from jax.sharding import PartitionSpec as P

SWEEPS = 3


lower_bound = 0.25
upper_bound = 2.0


def with_halo(block, sides, width):
    for axis, dim in sides:
        count = lax.axis_size(axis)
        forward = [(i, i + 1) for i in range(count - 1)]
        backward = [(target, source) for source, target in forward]
        low = lax.ppermute(
            lax.slice_in_dim(block, block.shape[dim] - width, None, axis=dim), axis, forward
        )
        high = lax.ppermute(lax.slice_in_dim(block, 0, width, axis=dim), axis, backward)
        block = jnp.concatenate([low, block, high], axis=dim)
    return block


def extend(bundle):
    return with_halo(bundle, (("gx", 1), ("gy", 3), ("gz", 2)), 1)


def deep_extend(bundle, merged):
    if merged:
        grown = with_halo(bundle, (("gy", 3), ("gz", 2)), 4)
        return jnp.pad(grown, ((0, 0), (4, 4), (0, 0), (0, 0)))
    return with_halo(bundle, (("gx", 1), ("gy", 3), ("gz", 2)), 4)


def neighbours(padded):
    return [
        padded[:-2, 1:-1, 1:-1],
        padded[2:, 1:-1, 1:-1],
        padded[1:-1, :-2, 1:-1],
        padded[1:-1, 2:, 1:-1],
        padded[1:-1, 1:-1, :-2],
        padded[1:-1, 1:-1, 2:],
    ]


def face_terms(conduct):
    others = neighbours(extend(conduct[None])[0])
    weights = [0.5 * (conduct + other) for other in others]
    diagonal = weights[0] + weights[1] + weights[2] + weights[3] + weights[4] + weights[5]
    return (weights, diagonal)


def operate(field, weights, diagonal):
    others = neighbours(extend(field[None])[0])
    result = diagonal * field
    for face_index in range(6):
        result = result - weights[face_index] * others[face_index]
    return result


def smooth(source, conduct):
    theta = 0.5 * (upper_bound + lower_bound)
    delta = 0.5 * (upper_bound - lower_bound)
    sigma = theta / delta
    weights, diagonal = face_terms(conduct)
    solution = jnp.zeros_like(source)
    residual = source
    direction = residual / (theta * diagonal)
    ratio_now = 1.0 / sigma
    for sweep_index in range(SWEEPS):
        solution = solution + direction
        residual = residual - operate(direction, weights, diagonal)
        if sweep_index + 1 < SWEEPS:
            ratio_next = 1.0 / (2.0 * sigma - ratio_now)
            direction = (
                ratio_next * ratio_now * direction + 2.0 * ratio_next / delta * residual / diagonal
            )
            ratio_now = ratio_next
    return (solution, residual)


def local_operate(field, weights, diagonal):
    others = neighbours(jnp.pad(field, 1))
    result = diagonal * field
    for face_index in range(6):
        result = result - weights[face_index] * others[face_index]
    return result


def smooth_deep(source, start, conduct, merged):
    theta = 0.5 * (upper_bound + lower_bound)
    delta = 0.5 * (upper_bound - lower_bound)
    sigma = theta / delta
    members = [conduct, source, jnp.ones_like(source)]
    if start is not None:
        members.append(start)
    grown = deep_extend(jnp.stack(members), merged)
    padded_conduct = grown[0]
    padded_source = grown[1]
    inside = grown[2]
    others = neighbours(jnp.pad(padded_conduct, 1))
    weights = [0.5 * (padded_conduct + other) for other in others]
    diagonal = weights[0] + weights[1] + weights[2] + weights[3] + weights[4] + weights[5]
    safe_diagonal = jnp.where(inside > 0.5, diagonal, 1.0)
    if start is None:
        solution = jnp.zeros_like(padded_source)
        residual = padded_source
    else:
        solution = grown[3]
        residual = padded_source - local_operate(solution, weights, diagonal)
    direction = inside * (residual / (theta * safe_diagonal))
    ratio_now = 1.0 / sigma
    for sweep_index in range(SWEEPS):
        solution = solution + direction
        residual = residual - local_operate(direction, weights, diagonal)
        if sweep_index + 1 < SWEEPS:
            ratio_next = 1.0 / (2.0 * sigma - ratio_now)
            direction = inside * (
                ratio_next * ratio_now * direction
                + 2.0 * ratio_next / delta * residual / safe_diagonal
            )
            ratio_now = ratio_next
    return (solution[4:-4, 4:-4, 4:-4], residual[4:-4, 4:-4, 4:-4])


def level_smooth(source, start, conduct, merged):
    extents = source.shape[1:] if merged else source.shape
    if min(extents) >= 4:
        return smooth_deep(source, start, conduct, merged)
    return smooth(source, conduct)


def coarse_sum(field):
    first, second, third = field.shape
    blocks = field.reshape(first // 2, 2, second // 2, 2, third // 2, 2)
    return jnp.sum(blocks, axis=(1, 3, 5))


def shards(conductivity, initial_guess, right_side):
    fine_solution, residual_zero = level_smooth(right_side, initial_guess, conductivity, False)
    conduct_one = 0.125 * coarse_sum(conductivity)
    level_one_solution, residual_one = level_smooth(
        0.25 * coarse_sum(residual_zero), None, conduct_one, False
    )
    conduct_two = 0.125 * coarse_sum(conduct_one)
    source_two = 0.25 * coarse_sum(residual_one)
    bundle = jnp.stack([source_two, conduct_two])
    bundle = lax.all_gather(bundle, "gx", axis=1, tiled=True)
    level_two_solution, residual_two = level_smooth(bundle[0], None, bundle[1], True)
    conduct_three = 0.125 * coarse_sum(bundle[1])
    level_three_solution, level_three_residual = level_smooth(
        0.25 * coarse_sum(residual_two), None, conduct_three, True
    )
    return (
        fine_solution,
        level_one_solution,
        level_two_solution,
        level_three_solution,
        level_three_residual,
    )


FIELDS = 3
WIDTH = 4
ROWS = 8
LANES = 128


def in_range(index, count):
    return (index >= 0) & (index < count)


def shift(value, amount, axis):
    return pltpu.roll(value, amount % value.shape[axis], axis)


def face_planes(conduct, grown):
    count = len(conduct)
    edge = 1 if grown else 0
    weight_x = [None] * (count + 1)
    for i in range(1, count):
        weight_x[i] = 0.5 * (conduct[i - 1] + conduct[i])
    if not grown:
        weight_x[0] = 0.5 * conduct[0]
        weight_x[count] = 0.5 * conduct[count - 1]
    weight_z = [None] * count
    weight_y = [None] * count
    inverse = [None] * count
    for i in range(edge, count - edge):
        weight_z[i] = 0.5 * (conduct[i] + shift(conduct[i], -1, 0))
        weight_y[i] = 0.5 * (conduct[i] + shift(conduct[i], -1, 1))
        diagonal = weight_x[i] + weight_x[i + 1]
        diagonal = diagonal + (weight_z[i] + shift(weight_z[i], 1, 0))
        diagonal = diagonal + (weight_y[i] + shift(weight_y[i], 1, 1))
        inside = conduct[i] > 0.0
        inverse[i] = jnp.where(inside, 1.0 / jnp.where(inside, diagonal, 1.0), 0.0)
    return weight_x, weight_y, weight_z, inverse


def operate_planes(faces, field, low, high):
    weight_x, weight_y, weight_z, _ = faces
    count = len(field)
    flux_x = [None] * (count + 1)
    for i in range(low, high + 1):
        if i == 0:
            flux_x[i] = weight_x[i] * field[i]
        elif i == count:
            flux_x[i] = -(weight_x[i] * field[i - 1])
        else:
            flux_x[i] = weight_x[i] * (field[i] - field[i - 1])
    result = [None] * count
    for i in range(low, high):
        flux_z = weight_z[i] * (field[i] - shift(field[i], -1, 0))
        flux_y = weight_y[i] * (field[i] - shift(field[i], -1, 1))
        result[i] = (
            (flux_x[i] - flux_x[i + 1])
            + (flux_z - shift(flux_z, 1, 0))
            + (flux_y - shift(flux_y, 1, 1))
        )
    return result


def smooth_planes(faces, residual, start, grown):
    theta = 0.5 * (upper_bound + lower_bound)
    delta = 0.5 * (upper_bound - lower_bound)
    sigma = theta / delta
    inverse = faces[3]
    count = len(residual)
    edge = 1 if grown else 0
    low, high = edge, count - edge
    residual = list(residual)
    direction = [None] * count
    for i in range(low, high):
        direction[i] = residual[i] * (inverse[i] * (1.0 / theta))
    ratio_now = 1.0 / sigma
    solution = list(start) if start is not None else [None] * count
    for sweep_index in range(SWEEPS):
        for i in range(low, high):
            solution[i] = direction[i] if solution[i] is None else solution[i] + direction[i]
        low, high = low + edge, high - edge
        applied = operate_planes(faces, direction, low, high)
        for i in range(low, high):
            residual[i] = residual[i] - applied[i]
        if sweep_index + 1 < SWEEPS:
            ratio_next = 1.0 / (2.0 * sigma - ratio_now)
            turned = [None] * count
            for i in range(low, high):
                turned[i] = (ratio_next * ratio_now) * direction[i] + (
                    2.0 * ratio_next / delta
                ) * (residual[i] * inverse[i])
            direction = turned
            ratio_now = ratio_next
    return solution, residual


def split_dot(value, matrix):
    parts = []
    rest = value
    for _ in range(3):
        part = rest.astype(jnp.bfloat16)
        parts.append(part.astype(jnp.float32))
        rest = rest - parts[-1]
    rows = value.shape[0]
    stacked = jnp.concatenate(parts, axis=0).astype(jnp.bfloat16)
    product = jnp.dot(stacked, matrix, preferred_element_type=jnp.float32)
    return product[:rows] + product[rows : 2 * rows] + product[2 * rows :]


def pair_matrix(keep_low, keep_high, offset):
    source = lax.broadcasted_iota(jnp.int32, (LANES, LANES), 0)
    target = lax.broadcasted_iota(jnp.int32, (LANES, LANES), 1)
    low = (source < keep_low) & (target == offset + source // 2)
    high = (source >= LANES - keep_high) & (target == LANES // 2 + source // 2)
    return jnp.where(low | high, 1.0, 0.0).astype(jnp.bfloat16)


def pair_rows(value, hold):
    rows = value.shape[0]
    hold[0:rows, :] = value
    return hold[pl.ds(0, rows // 2, stride=2), :] + hold[pl.ds(1, rows // 2, stride=2), :]


def kernel(sizes, *refs):
    count_x, count_y, count_z = sizes
    inputs = refs[0:3]
    outs = refs[3:8]
    grown = refs[8:11]
    (pack_full, pack_edge, pack_rows, got_full, got_edge, got_rows, own_one, own_half, all_one,
     all_half, hold, solved_one, out_fine, out_one, out_two,
     out_three, out_rest, load_sem, face_send, face_recv, row_send, row_recv,
     full_send, full_recv, edge_send, edge_recv, one_send, one_recv, store_sem) = refs[11:]
    kept = (out_fine, out_one, out_two, out_three, out_rest)
    stores = [pltpu.make_async_copy(kept[i], outs[i], store_sem.at[i]) for i in range(5)]
    planes, rows = inputs[0].shape[0], inputs[0].shape[1]
    x = lax.axis_index("gx")
    y = lax.axis_index("gy")
    z = lax.axis_index("gz")
    first_z = z == 0

    loads = []
    for f in range(FIELDS):
        loads.append(pltpu.make_async_copy(
            inputs[f], grown[f].at[planes : 2 * planes, 0:rows, 0:LANES], load_sem.at[f]))
        loads[-1].start()

    def other(step, turn, dy):
        return {"gx": lax.rem(x + step, count_x), "gy": y + dy, "gz": lax.rem(z + turn, count_z)}

    near = planes - WIDTH
    strip_list = [
        [(f, q) for f in range(FIELDS) for q in range(planes)
         if q > near + (1 if f == 2 else 0)],
        [(f, q) for f in range(FIELDS) for q in range(planes)],
        [(f, q) for f in range(FIELDS) for q in range(planes)
         if q < WIDTH - 1 - (1 if f == 2 else 0)],
    ]
    partners = [
        (step, turn, dy)
        for step in range(count_x)
        for turn in range(count_z)
        for dy in (0, -1, 1)
        if (step, turn, dy) != (0, 0, 0)
    ]
    barrier = pltpu.get_barrier_semaphore()
    for dy in (0, -1, 1):
        @pl.when(in_range(y + dy, count_y))
        def _():
            chosen = [p for p in partners if p[2] == dy]
            for step, turn, _dy in chosen:
                pl.semaphore_signal(
                    barrier, inc=1, device_id=other(step, turn, dy),
                    device_id_type=pl.DeviceIdType.MESH)

    for f in range(FIELDS):
        @pl.when(x == 0)
        def _():
            grown[f][0:planes, 0:rows, 0:LANES] = jnp.zeros((planes, rows, LANES), jnp.float32)

        @pl.when(x == count_x - 1)
        def _():
            grown[f][2 * planes : 3 * planes, 0:rows, 0:LANES] = jnp.zeros(
                (planes, rows, LANES), jnp.float32)

    for slot in range(3):
        for side in range(2):
            there = in_range(x + (slot - 1), count_x) & in_range(y + (2 * side - 1), count_y)

            @pl.when(jnp.logical_not(there))
            def _():
                got_full[slot, side] = jnp.zeros((rows // 2, LANES), jnp.float32)
                got_edge[slot, side] = jnp.zeros((ROWS, LANES), jnp.float32)

        if slot != 1:
            @pl.when(jnp.logical_not(in_range(x + (slot - 1), count_x)))
            def _():
                got_rows[slot] = jnp.zeros(got_rows.shape[1:], jnp.float32)

    for side in range(2):
        @pl.when(jnp.logical_not(in_range(y + (2 * side - 1), count_y)))
        def _():
            for part in range(2):
                all_half[part, side] = jnp.zeros(all_half.shape[2:], jnp.float32)

    for load in loads:
        load.wait()

    lane = lax.broadcasted_iota(jnp.int32, (rows, LANES), 1)
    row_index = lax.broadcasted_iota(jnp.int32, (ROWS, LANES), 0)
    low_lane = lax.rem(lane[0 : rows // 2], 2 * WIDTH) < WIDTH
    leave = (row_index < WIDTH) == jnp.logical_not(first_z)
    strips = {}
    packed = jnp.zeros((rows, LANES), jnp.float32)
    for f in range(FIELDS):
        for q in range(planes):
            k = f * planes + q
            piece = grown[f][planes + q, 0:rows, 0:LANES]
            strips[f, q] = jnp.where(first_z, piece[rows - ROWS :], piece[0:ROWS])
            moved = shift(piece, 2 * WIDTH * k, 1)
            window = lax.rem(lane - 2 * WIDTH * k + WIDTH + LANES, LANES) < 2 * WIDTH
            packed = jnp.where(window, moved, packed)
    for slot in range(3):
        for t in range(len(strip_list[slot]) // 2):
            first, second = strip_list[slot][2 * t], strip_list[slot][2 * t + 1]
            pack_rows[slot, t] = jnp.where(
                leave, strips[first], shift(strips[second], WIDTH, 0))
    top, bottom = packed[0 : rows // 2], packed[rows // 2 : rows]
    pack_full[0] = jnp.where(low_lane, shift(bottom, -WIDTH, 1), top)
    pack_full[1] = jnp.where(low_lane, top, shift(bottom, WIDTH, 1))
    pack_edge[...] = jnp.where(first_z, packed[rows - ROWS :], packed[0:ROWS])

    wanted = (count_x * count_z - 1) + count_x * count_z * (
        jnp.where(y > 0, 1, 0) + jnp.where(y < count_y - 1, 1, 0))
    pl.semaphore_wait(barrier, wanted)

    def send(src, dst, send_sem, recv_sem, device, to, back):
        copy = pltpu.make_async_remote_copy(
            src_ref=src, dst_ref=dst, send_sem=send_sem, recv_sem=recv_sem,
            device_id=device, device_id_type=pl.DeviceIdType.MESH)
        if to is None:
            copy.start()
        else:
            pl.when(to)(copy.start)
        return copy, to, back

    def wait_recv(entry):
        copy, _, back = entry
        if back is None:
            copy.wait_recv()
        else:
            pl.when(back)(copy.wait_recv)

    def wait_send(entry):
        copy, to, _ = entry
        if to is None:
            copy.wait_send()
        else:
            pl.when(to)(copy.wait_send)

    faces = []
    strips_sent = []

    def send_face(f):
        for dx in (1, -1):
            to, back = in_range(x + dx, count_x), in_range(x - dx, count_x)
            low, high = 0, planes
            if f == 2:
                low, high = (1, planes) if dx == 1 else (0, planes - 1)
            base = 0 if dx == 1 else 2 * planes
            index = (dx + 1) // 2 * FIELDS + f
            faces.append((f, send(
                grown[f].at[planes + low : planes + high, 0:rows, 0:LANES],
                grown[f].at[base + low : base + high, 0:rows, 0:LANES],
                face_send.at[index], face_recv.at[index],
                {"gx": x + dx, "gy": y, "gz": z}, to, back)))

    send_face(0)
    for dx in (1, -1, 0):
        slot = 1 - dx
        to, back = (in_range(x + dx, count_x), in_range(x - dx, count_x)) if dx else (None, None)
        tiles = len(strip_list[slot]) // 2
        strips_sent.append(send(
            pack_rows.at[slot, 0:tiles], got_rows.at[slot, 0:tiles], row_send.at[slot],
            row_recv.at[slot], {"gx": x + dx, "gy": y, "gz": 1 - z}, to, back))
        for dy in (1, -1):
            side = (1 - dy) // 2
            to = in_range(x + dx, count_x) & in_range(y + dy, count_y)
            back = in_range(x - dx, count_x) & in_range(y - dy, count_y)
            strips_sent.append(send(
                pack_full.at[side], got_full.at[slot, side], full_send.at[slot * 2 + side],
                full_recv.at[slot * 2 + side], {"gx": x + dx, "gy": y + dy, "gz": z}, to, back))
            strips_sent.append(send(
                pack_edge, got_edge.at[slot, side], edge_send.at[slot * 2 + side],
                edge_recv.at[slot * 2 + side], {"gx": x + dx, "gy": y + dy, "gz": 1 - z}, to, back))
    send_face(1)
    send_face(2)

    to_one = [pair_matrix(LANES, 0, 0), pair_matrix(LANES, 0, LANES // 2)]
    matrix_one = jnp.concatenate(to_one, axis=0)
    quarter = lax.broadcasted_iota(jnp.int32, (ROWS, LANES), 1) % (LANES // 2) < LANES // 4

    def restrict_fine(blocks, scale):
        pairs = [pair_rows(blocks[2 * q] + blocks[2 * q + 1], hold) for q in range(planes // 2)]
        return scale * split_dot(jnp.concatenate(pairs, axis=1), matrix_one)

    here = x * count_z + z
    blocks_all = count_x * count_z

    def spread(part, value):
        own_one[part] = value
        top, bottom = value[0:ROWS], value[ROWS : 2 * ROWS]
        own_half[part, 0] = jnp.where(quarter, shift(bottom, -(LANES // 4), 1), top)
        own_half[part, 1] = jnp.where(quarter, top, shift(bottom, LANES // 4, 1))
        all_one[part, here] = value
        for dy in (0, 1, -1):
            side = (1 - dy) // 2

            def start():
                for step, turn, _dy in [p for p in partners if p[2] == dy]:
                    if dy == 0:
                        source, target = own_one.at[part], all_one.at[part, here]
                    else:
                        source, target = own_half.at[part, side], all_half.at[part, side, here]
                    pltpu.make_async_remote_copy(
                        src_ref=source, dst_ref=target, send_sem=one_send.at[part, dy + 1],
                        recv_sem=one_recv.at[part, dy + 1], device_id=other(step, turn, dy),
                        device_id_type=pl.DeviceIdType.MESH).start()

            if dy == 0:
                start()
            else:
                pl.when(in_range(y + dy, count_y))(start)

    def settle(part, received):
        for dy in (0, 1, -1):
            side = (1 - dy) // 2
            bytes_of = all_one.at[part, 0 : blocks_all - 1] if dy == 0 else all_half.at[part, side]
            copy = pltpu.make_async_remote_copy(
                src_ref=bytes_of, dst_ref=bytes_of, send_sem=one_send.at[part, dy + 1],
                recv_sem=one_recv.at[part, dy + 1], device_id=other(1, 0, 0),
                device_id_type=pl.DeviceIdType.MESH)
            finish = copy.wait_recv if received else copy.wait_send
            if dy == 0:
                finish()
            else:
                pl.when(in_range(y - dy if received else y + dy, count_y))(finish)

    coarse_conduct = restrict_fine(
        [grown[0][planes + q, 0:rows, 0:LANES] for q in range(planes)], 0.125)

    for entry in strips_sent:
        wait_recv(entry)
    row_keep = (row_index < WIDTH) == first_z
    lane_edge = lax.broadcasted_iota(jnp.int32, (rows + ROWS, LANES), 1)
    lane_keep = (lane_edge < WIDTH) | (lane_edge >= LANES - WIDTH)
    low_edge = low_lane[0:ROWS]
    joined = []
    for slot in range(3):
        low, high = got_full[slot, 1], got_full[slot, 0]
        joined.append(jnp.concatenate([
            jnp.where(low_lane, low, high),
            jnp.where(low_lane, shift(low, -WIDTH, 1), shift(high, WIDTH, 1)),
            jnp.where(row_keep, jnp.where(low_edge, got_edge[slot, 1], got_edge[slot, 0]), 0.0),
        ], axis=0))
    for f in range(FIELDS):
        for slot in range(3):
            for q in range(planes):
                p = slot * planes + q
                strip = jnp.zeros((ROWS, LANES), jnp.float32)
                if (f, q) in strip_list[slot]:
                    index = strip_list[slot].index((f, q))
                    strip = got_rows[slot, index // 2]
                    if index % 2 == 1:
                        strip = shift(strip, WIDTH, 0)
                    strip = jnp.where(row_keep, strip, 0.0)
                grown[f][p, rows : rows + ROWS, 0:LANES] = strip
                grown[f][p, :, LANES : 2 * LANES] = jnp.where(
                    lane_keep, shift(joined[slot], -2 * WIDTH * (f * planes + q), 1), 0.0)

    def wait_face(f):
        for index, entry in faces:
            if index == f:
                wait_recv(entry)

    wait_face(0)
    faces_fine = face_planes([grown[0][p] for p in range(3 * planes)], True)
    spread(0, coarse_conduct)
    wait_face(1)
    start = [grown[1][p] for p in range(3 * planes)]
    applied = operate_planes(faces_fine, start, 1, 3 * planes - 1)
    wait_face(2)
    residual = [None] * (3 * planes)
    for p in range(1, 3 * planes - 1):
        residual[p] = grown[2][p] - applied[p]
    solved, residual = smooth_planes(faces_fine, residual, start, True)
    spread(
        1, restrict_fine([residual[planes + q][0:rows, 0:LANES] for q in range(planes)], 0.25))
    for q in range(planes):
        out_fine[q] = solved[planes + q][0:rows, 0:LANES]
    stores[0].start()

    lane_one = lax.broadcasted_iota(jnp.int32, (2 * ROWS, LANES), 1)
    lower = lane_one < LANES // 2
    empty = jnp.zeros((ROWS, LANES), jnp.float32)

    def assemble(part):
        level = []
        for from_x in range(count_x):
            blocks = [[], []]
            for from_z in range(count_z):
                block = from_x * count_z + from_z
                own = all_one[part, block]
                low, high = all_half[part, 0, block], all_half[part, 1, block]
                beside = jnp.concatenate(
                    [jnp.where(quarter, high, low),
                     jnp.where(quarter, shift(high, -(LANES // 4), 1), shift(low, LANES // 4, 1))],
                    axis=0)
                blocks[0].append(jnp.where(lower, own, shift(beside, LANES // 2, 1)))
                blocks[1].append(jnp.where(lower, shift(own, LANES // 2, 1), beside))
            for q in range(2):
                level.append(jnp.concatenate(blocks[q] + [empty], axis=0))
        return level

    def restrict(level, matrix, scale):
        length = level[0].shape[0] - ROWS
        summed = []
        for q in range(len(level) // 2):
            both = level[2 * q] + level[2 * q + 1]
            summed.append(pair_rows(both[0:length], hold))
        joined = scale * split_dot(jnp.concatenate(summed, axis=0), matrix)
        half = length // 2
        return [
            jnp.concatenate([joined[q * half : (q + 1) * half], empty], axis=0)
            for q in range(len(summed))
        ]

    matrix_two = pair_matrix(3 * LANES // 4, LANES // 4, 0)
    matrix_three = pair_matrix(3 * LANES // 8, LANES // 8, 0)
    settle(0, True)
    conduct_one = assemble(0)
    conduct_two = restrict(conduct_one, matrix_two, 0.125)
    conduct_three = restrict(conduct_two, matrix_three, 0.125)
    faces_one, faces_two, faces_three = (
        face_planes(conduct, False) for conduct in (conduct_one, conduct_two, conduct_three))

    settle(1, True)
    solved, residual = smooth_planes(faces_one, assemble(1), None, False)
    for p in range(len(solved)):
        block = solved[p][0 : 2 * rows // 2]
        solved_one[p] = jnp.where(first_z, block[0 : rows // 2], block[rows // 2 : rows])
    out_one[...] = solved_one[pl.ds(2 * x, 2), :, 0 : LANES // 2]
    stores[1].start()
    solved, residual = smooth_planes(
        faces_two, restrict(residual, matrix_two, 0.25), None, False)
    for p in range(len(solved)):
        half = rows // 4
        out_two[p] = jnp.where(first_z, solved[p][0:half], solved[p][half : 2 * half])[:, 0 : LANES // 4]
    stores[2].start()
    solved, residual = smooth_planes(
        faces_three, restrict(residual, matrix_three, 0.25), None, False)
    for p in range(len(solved)):
        half = rows // 8
        for result, out in ((solved, out_three), (residual, out_rest)):
            out[p] = jnp.where(first_z, result[p][0:half], result[p][half : 2 * half])[:, 0 : LANES // 8]

    stores[3].start()
    stores[4].start()
    for entry in strips_sent + [entry for _, entry in faces]:
        wait_send(entry)
    settle(0, False)
    settle(1, False)
    for store in stores:
        store.wait()


def hand_over(*refs):
    count = len(refs) // 2
    copies = []
    for i in range(count):
        copies.append(pltpu.make_async_copy(refs[i], refs[count + i], refs[-1].at[i]))
        copies[-1].start()
    for copy in copies:
        copy.wait()


def fits(mesh, shape):
    return (
        mesh.shape["gz"] == 2
        and mesh.shape["gx"] <= 4
        and shape[0] == WIDTH * mesh.shape["gx"]
        and shape[1] == 32 * mesh.shape["gz"]
        and shape[2] == LANES * mesh.shape["gy"]
    )


def fused(mesh, conductivity, initial_guess, right_side):
    sizes = (mesh.shape["gx"], mesh.shape["gy"], mesh.shape["gz"])
    count_x, _, count_z = sizes
    planes, rows, lanes = conductivity.shape
    f32 = jnp.float32
    shapes = [
        (planes, rows, lanes),
        (planes // 2, rows // 2, lanes // 2),
        (count_x * planes // 4, rows // 4, lanes // 4),
        (count_x * planes // 8, rows // 8, lanes // 8),
        (count_x * planes // 8, rows // 8, lanes // 8),
    ]
    blocks_all = count_x * count_z
    dma = pltpu.SemaphoreType.DMA
    scratch = [pltpu.VMEM((3 * planes, rows + ROWS, 2 * LANES), f32)] * FIELDS + [
        pltpu.VMEM((2, rows // 2, LANES), f32),
        pltpu.VMEM((ROWS, LANES), f32),
        pltpu.VMEM((3, FIELDS * planes // 2, ROWS, LANES), f32),
        pltpu.VMEM((3, 2, rows // 2, LANES), f32),
        pltpu.VMEM((3, 2, ROWS, LANES), f32),
        pltpu.VMEM((3, FIELDS * planes // 2, ROWS, LANES), f32),
        pltpu.VMEM((2, rows // 2, LANES), f32),
        pltpu.VMEM((2, 2, ROWS, LANES), f32),
        pltpu.VMEM((2, blocks_all, rows // 2, LANES), f32),
        pltpu.VMEM((2, 2, blocks_all, ROWS, LANES), f32),
        pltpu.VMEM((rows, LANES), f32),
        pltpu.VMEM((2 * count_x, rows // 2, LANES), f32),
        *[pltpu.VMEM(shape, f32) for shape in shapes],
        dma((3,)),
        dma((6,)), dma((6,)),
        dma((3,)), dma((3,)),
        dma((6,)), dma((6,)),
        dma((6,)), dma((6,)),
        dma((2, 3)), dma((2, 3)),
        dma((5,)),
    ]
    outside = pl.BlockSpec(memory_space=pltpu.HBM)
    out_shape = [jax.ShapeDtypeStruct(shape, f32) for shape in shapes]
    results = pl.pallas_call(
        functools.partial(kernel, sizes),
        out_shape=out_shape,
        in_specs=[outside] * 3,
        out_specs=[outside] * 5,
        scratch_shapes=scratch,
        compiler_params=pltpu.CompilerParams(
            collective_id=0, has_side_effects=True, vmem_limit_bytes=56 * 2**20),
    )(conductivity, initial_guess, right_side)
    return pl.pallas_call(
        hand_over,
        out_shape=out_shape,
        in_specs=[pl.BlockSpec(memory_space=pltpu.VMEM)] * 5,
        out_specs=[outside] * 5,
        scratch_shapes=[dma((5,))],
        compiler_params=pltpu.CompilerParams(vmem_limit_bytes=56 * 2**20),
    )(*results)


def solution(mesh):
    placed = (P("gx", "gz", "gy"), P("gx", "gz", "gy"), P("gx", "gz", "gy"))

    def whole(conductivity, initial_guess, right_side):
        local = shards
        if fits(mesh, conductivity.shape):
            local = functools.partial(fused, mesh)
        return jax.shard_map(
            local,
            mesh=mesh,
            in_specs=placed,
            out_specs=(
                P("gx", "gz", "gy"),
                P("gx", "gz", "gy"),
                P(None, "gz", "gy"),
                P(None, "gz", "gy"),
                P(None, "gz", "gy"),
            ),
            check_vma=False,
        )(conductivity, initial_guess, right_side)

    return whole
```

```python
import functools

import jax
import jax.numpy as jnp
from jax import lax
from jax.experimental import pallas as pl
from jax.experimental.pallas import tpu as pltpu
from jax.sharding import PartitionSpec as P

SWEEPS = 3


lower_bound = 0.25
upper_bound = 2.0


def with_halo(block, sides, width):
    for axis, dim in sides:
        count = lax.axis_size(axis)
        forward = [(i, i + 1) for i in range(count - 1)]
        backward = [(target, source) for source, target in forward]
        low = lax.ppermute(
            lax.slice_in_dim(block, block.shape[dim] - width, None, axis=dim), axis, forward
        )
        high = lax.ppermute(lax.slice_in_dim(block, 0, width, axis=dim), axis, backward)
        block = jnp.concatenate([low, block, high], axis=dim)
    return block


def extend(bundle):
    return with_halo(bundle, (("gx", 1), ("gy", 3), ("gz", 2)), 1)


def deep_extend(bundle, merged):
    if merged:
        grown = with_halo(bundle, (("gy", 3), ("gz", 2)), 4)
        return jnp.pad(grown, ((0, 0), (4, 4), (0, 0), (0, 0)))
    return with_halo(bundle, (("gx", 1), ("gy", 3), ("gz", 2)), 4)


def neighbours(padded):
    return [
        padded[:-2, 1:-1, 1:-1],
        padded[2:, 1:-1, 1:-1],
        padded[1:-1, :-2, 1:-1],
        padded[1:-1, 2:, 1:-1],
        padded[1:-1, 1:-1, :-2],
        padded[1:-1, 1:-1, 2:],
    ]


def face_terms(conduct):
    others = neighbours(extend(conduct[None])[0])
    weights = [0.5 * (conduct + other) for other in others]
    diagonal = weights[0] + weights[1] + weights[2] + weights[3] + weights[4] + weights[5]
    return (weights, diagonal)


def operate(field, weights, diagonal):
    others = neighbours(extend(field[None])[0])
    result = diagonal * field
    for face_index in range(6):
        result = result - weights[face_index] * others[face_index]
    return result


def smooth(source, conduct):
    theta = 0.5 * (upper_bound + lower_bound)
    delta = 0.5 * (upper_bound - lower_bound)
    sigma = theta / delta
    weights, diagonal = face_terms(conduct)
    solution = jnp.zeros_like(source)
    residual = source
    direction = residual / (theta * diagonal)
    ratio_now = 1.0 / sigma
    for sweep_index in range(SWEEPS):
        solution = solution + direction
        residual = residual - operate(direction, weights, diagonal)
        if sweep_index + 1 < SWEEPS:
            ratio_next = 1.0 / (2.0 * sigma - ratio_now)
            direction = (
                ratio_next * ratio_now * direction + 2.0 * ratio_next / delta * residual / diagonal
            )
            ratio_now = ratio_next
    return (solution, residual)


def local_operate(field, weights, diagonal):
    others = neighbours(jnp.pad(field, 1))
    result = diagonal * field
    for face_index in range(6):
        result = result - weights[face_index] * others[face_index]
    return result


def smooth_deep(source, start, conduct, merged):
    theta = 0.5 * (upper_bound + lower_bound)
    delta = 0.5 * (upper_bound - lower_bound)
    sigma = theta / delta
    members = [conduct, source, jnp.ones_like(source)]
    if start is not None:
        members.append(start)
    grown = deep_extend(jnp.stack(members), merged)
    padded_conduct = grown[0]
    padded_source = grown[1]
    inside = grown[2]
    others = neighbours(jnp.pad(padded_conduct, 1))
    weights = [0.5 * (padded_conduct + other) for other in others]
    diagonal = weights[0] + weights[1] + weights[2] + weights[3] + weights[4] + weights[5]
    safe_diagonal = jnp.where(inside > 0.5, diagonal, 1.0)
    if start is None:
        solution = jnp.zeros_like(padded_source)
        residual = padded_source
    else:
        solution = grown[3]
        residual = padded_source - local_operate(solution, weights, diagonal)
    direction = inside * (residual / (theta * safe_diagonal))
    ratio_now = 1.0 / sigma
    for sweep_index in range(SWEEPS):
        solution = solution + direction
        residual = residual - local_operate(direction, weights, diagonal)
        if sweep_index + 1 < SWEEPS:
            ratio_next = 1.0 / (2.0 * sigma - ratio_now)
            direction = inside * (
                ratio_next * ratio_now * direction
                + 2.0 * ratio_next / delta * residual / safe_diagonal
            )
            ratio_now = ratio_next
    return (solution[4:-4, 4:-4, 4:-4], residual[4:-4, 4:-4, 4:-4])


def level_smooth(source, start, conduct, merged):
    extents = source.shape[1:] if merged else source.shape
    if min(extents) >= 4:
        return smooth_deep(source, start, conduct, merged)
    return smooth(source, conduct)


def coarse_sum(field):
    first, second, third = field.shape
    blocks = field.reshape(first // 2, 2, second // 2, 2, third // 2, 2)
    return jnp.sum(blocks, axis=(1, 3, 5))


def shards(conductivity, initial_guess, right_side):
    fine_solution, residual_zero = level_smooth(right_side, initial_guess, conductivity, False)
    conduct_one = 0.125 * coarse_sum(conductivity)
    level_one_solution, residual_one = level_smooth(
        0.25 * coarse_sum(residual_zero), None, conduct_one, False
    )
    conduct_two = 0.125 * coarse_sum(conduct_one)
    source_two = 0.25 * coarse_sum(residual_one)
    bundle = jnp.stack([source_two, conduct_two])
    bundle = lax.all_gather(bundle, "gx", axis=1, tiled=True)
    level_two_solution, residual_two = level_smooth(bundle[0], None, bundle[1], True)
    conduct_three = 0.125 * coarse_sum(bundle[1])
    level_three_solution, level_three_residual = level_smooth(
        0.25 * coarse_sum(residual_two), None, conduct_three, True
    )
    return (
        fine_solution,
        level_one_solution,
        level_two_solution,
        level_three_solution,
        level_three_residual,
    )


FIELDS = 3
WIDTH = 4
ROWS = 8
LANES = 128


def in_range(index, count):
    return (index >= 0) & (index < count)


def shift(value, amount, axis):
    return pltpu.roll(value, amount % value.shape[axis], axis)


def face_planes(conduct, grown):
    count = len(conduct)
    edge = 1 if grown else 0
    weight_x = [None] * (count + 1)
    for i in range(1, count):
        weight_x[i] = 0.5 * (conduct[i - 1] + conduct[i])
    if not grown:
        weight_x[0] = 0.5 * conduct[0]
        weight_x[count] = 0.5 * conduct[count - 1]
    weight_z = [None] * count
    weight_y = [None] * count
    inverse = [None] * count
    for i in range(edge, count - edge):
        weight_z[i] = 0.5 * (conduct[i] + shift(conduct[i], -1, 0))
        weight_y[i] = 0.5 * (conduct[i] + shift(conduct[i], -1, 1))
        diagonal = weight_x[i] + weight_x[i + 1]
        diagonal = diagonal + (weight_z[i] + shift(weight_z[i], 1, 0))
        diagonal = diagonal + (weight_y[i] + shift(weight_y[i], 1, 1))
        inside = conduct[i] > 0.0
        inverse[i] = jnp.where(inside, 1.0 / jnp.where(inside, diagonal, 1.0), 0.0)
    return weight_x, weight_y, weight_z, inverse


def operate_planes(faces, field, low, high):
    weight_x, weight_y, weight_z, _ = faces
    count = len(field)
    flux_x = [None] * (count + 1)
    for i in range(low, high + 1):
        if i == 0:
            flux_x[i] = weight_x[i] * field[i]
        elif i == count:
            flux_x[i] = -(weight_x[i] * field[i - 1])
        else:
            flux_x[i] = weight_x[i] * (field[i] - field[i - 1])
    result = [None] * count
    for i in range(low, high):
        flux_z = weight_z[i] * (field[i] - shift(field[i], -1, 0))
        flux_y = weight_y[i] * (field[i] - shift(field[i], -1, 1))
        result[i] = (
            (flux_x[i] - flux_x[i + 1])
            + (flux_z - shift(flux_z, 1, 0))
            + (flux_y - shift(flux_y, 1, 1))
        )
    return result


def smooth_planes(faces, residual, start, grown):
    theta = 0.5 * (upper_bound + lower_bound)
    delta = 0.5 * (upper_bound - lower_bound)
    sigma = theta / delta
    inverse = faces[3]
    count = len(residual)
    edge = 1 if grown else 0
    low, high = edge, count - edge
    residual = list(residual)
    direction = [None] * count
    for i in range(low, high):
        direction[i] = residual[i] * (inverse[i] * (1.0 / theta))
    ratio_now = 1.0 / sigma
    solution = list(start) if start is not None else [None] * count
    for sweep_index in range(SWEEPS):
        for i in range(low, high):
            solution[i] = direction[i] if solution[i] is None else solution[i] + direction[i]
        low, high = low + edge, high - edge
        applied = operate_planes(faces, direction, low, high)
        for i in range(low, high):
            residual[i] = residual[i] - applied[i]
        if sweep_index + 1 < SWEEPS:
            ratio_next = 1.0 / (2.0 * sigma - ratio_now)
            turned = [None] * count
            for i in range(low, high):
                turned[i] = (ratio_next * ratio_now) * direction[i] + (
                    2.0 * ratio_next / delta
                ) * (residual[i] * inverse[i])
            direction = turned
            ratio_now = ratio_next
    return solution, residual


def split_dot(value, matrix):
    parts = []
    rest = value
    for _ in range(3):
        part = rest.astype(jnp.bfloat16)
        parts.append(part.astype(jnp.float32))
        rest = rest - parts[-1]
    rows = value.shape[0]
    stacked = jnp.concatenate(parts, axis=0).astype(jnp.bfloat16)
    product = jnp.dot(stacked, matrix, preferred_element_type=jnp.float32)
    return product[:rows] + product[rows : 2 * rows] + product[2 * rows :]


def pair_matrix(keep_low, keep_high, offset):
    source = lax.broadcasted_iota(jnp.int32, (LANES, LANES), 0)
    target = lax.broadcasted_iota(jnp.int32, (LANES, LANES), 1)
    low = (source < keep_low) & (target == offset + source // 2)
    high = (source >= LANES - keep_high) & (target == LANES // 2 + source // 2)
    return jnp.where(low | high, 1.0, 0.0).astype(jnp.bfloat16)


def pair_rows(value, hold):
    rows = value.shape[0]
    hold[0:rows, :] = value
    return hold[pl.ds(0, rows // 2, stride=2), :] + hold[pl.ds(1, rows // 2, stride=2), :]


def kernel(sizes, *refs):
    count_x, count_y, count_z = sizes
    inputs = refs[0:3]
    outs = refs[3:8]
    grown = refs[8:11]
    (pack_full, pack_edge, pack_rows, got_full, got_edge, got_rows, own_one, own_half, line_half, all_one,
     all_half, hold, solved_one, out_fine, out_one, out_two,
     out_three, out_rest, load_sem, face_send, face_recv, row_send, row_recv,
     full_send, full_recv, edge_send, edge_recv, one_send, one_recv, hop_send, hop_recv, store_sem) = refs[11:]
    kept = (out_fine, out_one, out_two, out_three, out_rest)
    stores = [pltpu.make_async_copy(kept[i], outs[i], store_sem.at[i]) for i in range(5)]
    planes, rows = inputs[0].shape[0], inputs[0].shape[1]
    x = lax.axis_index("gx")
    y = lax.axis_index("gy")
    z = lax.axis_index("gz")
    first_z = z == 0

    loads = []
    for f in range(FIELDS):
        loads.append(pltpu.make_async_copy(
            inputs[f], grown[f].at[planes : 2 * planes, 0:rows, 0:LANES], load_sem.at[f]))
        loads[-1].start()

    def other(step, turn, dy):
        return {"gx": lax.rem(x + step, count_x), "gy": y + dy, "gz": lax.rem(z + turn, count_z)}

    near = planes - WIDTH
    strip_list = [
        [(f, q) for f in range(FIELDS) for q in range(planes)
         if q > near + (1 if f == 2 else 0)],
        [(f, q) for f in range(FIELDS) for q in range(planes)],
        [(f, q) for f in range(FIELDS) for q in range(planes)
         if q < WIDTH - 1 - (1 if f == 2 else 0)],
    ]
    partners = [
        (step, turn, dy)
        for step in range(count_x)
        for turn in range(count_z)
        for dy in (0, -1, 1)
        if (step, turn, dy) != (0, 0, 0)
    ]
    barrier = pltpu.get_barrier_semaphore()
    for dy in (0, -1, 1):
        @pl.when(in_range(y + dy, count_y))
        def _():
            chosen = [p for p in partners if p[2] == dy]
            for step, turn, _dy in chosen:
                pl.semaphore_signal(
                    barrier, inc=1, device_id=other(step, turn, dy),
                    device_id_type=pl.DeviceIdType.MESH)

    for f in range(FIELDS):
        @pl.when(x == 0)
        def _():
            grown[f][0:planes, 0:rows, 0:LANES] = jnp.zeros((planes, rows, LANES), jnp.float32)

        @pl.when(x == count_x - 1)
        def _():
            grown[f][2 * planes : 3 * planes, 0:rows, 0:LANES] = jnp.zeros(
                (planes, rows, LANES), jnp.float32)

    for slot in range(3):
        for side in range(2):
            there = in_range(x + (slot - 1), count_x) & in_range(y + (2 * side - 1), count_y)

            @pl.when(jnp.logical_not(there))
            def _():
                got_full[slot, side] = jnp.zeros((rows // 2, LANES), jnp.float32)
                got_edge[slot, side] = jnp.zeros((ROWS, LANES), jnp.float32)

        if slot != 1:
            @pl.when(jnp.logical_not(in_range(x + (slot - 1), count_x)))
            def _():
                got_rows[slot] = jnp.zeros(got_rows.shape[1:], jnp.float32)

    for side in range(2):
        @pl.when(jnp.logical_not(in_range(y + (2 * side - 1), count_y)))
        def _():
            for part in range(2):
                all_half[part, side] = jnp.zeros(all_half.shape[2:], jnp.float32)

    for load in loads:
        load.wait()

    lane = lax.broadcasted_iota(jnp.int32, (rows, LANES), 1)
    row_index = lax.broadcasted_iota(jnp.int32, (ROWS, LANES), 0)
    low_lane = lax.rem(lane[0 : rows // 2], 2 * WIDTH) < WIDTH
    leave = (row_index < WIDTH) == jnp.logical_not(first_z)
    strips = {}
    packed = jnp.zeros((rows, LANES), jnp.float32)
    for f in range(FIELDS):
        for q in range(planes):
            k = f * planes + q
            piece = grown[f][planes + q, 0:rows, 0:LANES]
            strips[f, q] = jnp.where(first_z, piece[rows - ROWS :], piece[0:ROWS])
            moved = shift(piece, 2 * WIDTH * k, 1)
            window = lax.rem(lane - 2 * WIDTH * k + WIDTH + LANES, LANES) < 2 * WIDTH
            packed = jnp.where(window, moved, packed)
    for slot in range(3):
        for t in range(len(strip_list[slot]) // 2):
            first, second = strip_list[slot][2 * t], strip_list[slot][2 * t + 1]
            pack_rows[slot, t] = jnp.where(
                leave, strips[first], shift(strips[second], WIDTH, 0))
    top, bottom = packed[0 : rows // 2], packed[rows // 2 : rows]
    pack_full[0] = jnp.where(low_lane, shift(bottom, -WIDTH, 1), top)
    pack_full[1] = jnp.where(low_lane, top, shift(bottom, WIDTH, 1))
    pack_edge[...] = jnp.where(first_z, packed[rows - ROWS :], packed[0:ROWS])

    wanted = (count_x * count_z - 1) + count_x * count_z * (
        jnp.where(y > 0, 1, 0) + jnp.where(y < count_y - 1, 1, 0))
    pl.semaphore_wait(barrier, wanted)

    def send(src, dst, send_sem, recv_sem, device, to, back):
        copy = pltpu.make_async_remote_copy(
            src_ref=src, dst_ref=dst, send_sem=send_sem, recv_sem=recv_sem,
            device_id=device, device_id_type=pl.DeviceIdType.MESH)
        if to is None:
            copy.start()
        else:
            pl.when(to)(copy.start)
        return copy, to, back

    def wait_recv(entry):
        copy, _, back = entry
        if back is None:
            copy.wait_recv()
        else:
            pl.when(back)(copy.wait_recv)

    def wait_send(entry):
        copy, to, _ = entry
        if to is None:
            copy.wait_send()
        else:
            pl.when(to)(copy.wait_send)

    faces = []
    strips_sent = []

    def send_face(f):
        for dx in (1, -1):
            to, back = in_range(x + dx, count_x), in_range(x - dx, count_x)
            low, high = 0, planes
            if f == 2:
                low, high = (1, planes) if dx == 1 else (0, planes - 1)
            base = 0 if dx == 1 else 2 * planes
            index = (dx + 1) // 2 * FIELDS + f
            faces.append((f, send(
                grown[f].at[planes + low : planes + high, 0:rows, 0:LANES],
                grown[f].at[base + low : base + high, 0:rows, 0:LANES],
                face_send.at[index], face_recv.at[index],
                {"gx": x + dx, "gy": y, "gz": z}, to, back)))

    send_face(0)
    for dx in (1, -1, 0):
        slot = 1 - dx
        to, back = (in_range(x + dx, count_x), in_range(x - dx, count_x)) if dx else (None, None)
        tiles = len(strip_list[slot]) // 2
        strips_sent.append(send(
            pack_rows.at[slot, 0:tiles], got_rows.at[slot, 0:tiles], row_send.at[slot],
            row_recv.at[slot], {"gx": x + dx, "gy": y, "gz": 1 - z}, to, back))
        for dy in (1, -1):
            side = (1 - dy) // 2
            to = in_range(x + dx, count_x) & in_range(y + dy, count_y)
            back = in_range(x - dx, count_x) & in_range(y - dy, count_y)
            strips_sent.append(send(
                pack_full.at[side], got_full.at[slot, side], full_send.at[slot * 2 + side],
                full_recv.at[slot * 2 + side], {"gx": x + dx, "gy": y + dy, "gz": z}, to, back))
            strips_sent.append(send(
                pack_edge, got_edge.at[slot, side], edge_send.at[slot * 2 + side],
                edge_recv.at[slot * 2 + side], {"gx": x + dx, "gy": y + dy, "gz": 1 - z}, to, back))
    send_face(1)
    send_face(2)

    to_one = [pair_matrix(LANES, 0, 0), pair_matrix(LANES, 0, LANES // 2)]
    matrix_one = jnp.concatenate(to_one, axis=0)
    quarter = lax.broadcasted_iota(jnp.int32, (ROWS, LANES), 1) % (LANES // 2) < LANES // 4

    def restrict_fine(blocks, scale):
        pairs = [pair_rows(blocks[2 * q] + blocks[2 * q + 1], hold) for q in range(planes // 2)]
        return scale * split_dot(jnp.concatenate(pairs, axis=1), matrix_one)

    hopped = (0,)
    here = z * count_x + x
    line = pl.ds(z * count_x, count_x)
    blocks_all = count_x * count_z

    def spread(part, value):
        own_one[part] = value
        top, bottom = value[0:ROWS], value[ROWS : 2 * ROWS]
        own_half[part, 0] = jnp.where(quarter, shift(bottom, -(LANES // 4), 1), top)
        own_half[part, 1] = jnp.where(quarter, top, shift(bottom, LANES // 4, 1))
        all_one[part, here] = value
        for dy in (0, 1, -1):
            side = (1 - dy) // 2

            def start():
                for step, turn, _dy in [p for p in partners if p[2] == dy]:
                    if dy == 0:
                        source, target = own_one.at[part], all_one.at[part, here]
                    else:
                        source, target = own_half.at[part, side], all_half.at[part, side, here]
                    pltpu.make_async_remote_copy(
                        src_ref=source, dst_ref=target, send_sem=one_send.at[part, dy + 1],
                        recv_sem=one_recv.at[part, dy + 1], device_id=other(step, turn, dy),
                        device_id_type=pl.DeviceIdType.MESH).start()

            if dy == 0:
                start()
            else:
                pl.when(in_range(y + dy, count_y))(start)

    def remote(source, target, send_sem, recv_sem, device):
        return pltpu.make_async_remote_copy(
            src_ref=source, dst_ref=target, send_sem=send_sem, recv_sem=recv_sem,
            device_id=device, device_id_type=pl.DeviceIdType.MESH)

    def first_hop(part, value):
        own_one[part] = value
        all_one[part, here] = value
        for step in range(1, count_x):
            remote(own_one.at[part], all_one.at[part, here], hop_send.at[part],
                   hop_recv.at[part], other(step, 0, 0)).start()

    def settle_hop(part, received):
        bytes_of = all_one.at[part, 0 : count_x - 1]
        copy = remote(bytes_of, bytes_of, hop_send.at[part], hop_recv.at[part], other(1, 0, 0))
        copy.wait_recv() if received else copy.wait_send()

    def line_copies(part, dy):
        side = (1 - dy) // 2
        sems = (one_send.at[part, dy + 1], one_recv.at[part, dy + 1])
        if dy == 0:
            return [remote(all_one.at[part, line], all_one.at[part, line], *sems, other(0, 1, 0))]
        return [
            remote(line_half.at[part, side], all_half.at[part, side, line], *sems,
                   other(0, turn, dy))
            for turn in range(count_z)
        ]

    def second_hop(part):
        for from_x in range(count_x):
            value = all_one[part, z * count_x + from_x]
            top, bottom = value[0:ROWS], value[ROWS : 2 * ROWS]
            line_half[part, 0, from_x] = jnp.where(quarter, shift(bottom, -(LANES // 4), 1), top)
            line_half[part, 1, from_x] = jnp.where(quarter, top, shift(bottom, LANES // 4, 1))
        for dy in (0, 1, -1):
            def start():
                for copy in line_copies(part, dy):
                    copy.start()

            if dy == 0:
                start()
            else:
                pl.when(in_range(y + dy, count_y))(start)

    def settle(part, received):
        for dy in (0, 1, -1):
            side = (1 - dy) // 2
            if dy == 0:
                extent = count_x if part in hopped else blocks_all - 1
                bytes_of = all_one.at[part, 0:extent]
            else:
                bytes_of = all_half.at[part, side]
            copy = remote(bytes_of, bytes_of, one_send.at[part, dy + 1],
                          one_recv.at[part, dy + 1], other(1, 0, 0))
            finish = copy.wait_recv if received else copy.wait_send
            if dy == 0:
                finish()
            else:
                pl.when(in_range(y - dy if received else y + dy, count_y))(finish)

    coarse_conduct = restrict_fine(
        [grown[0][planes + q, 0:rows, 0:LANES] for q in range(planes)], 0.125)
    first_hop(0, coarse_conduct)

    for entry in strips_sent:
        wait_recv(entry)
    row_keep = (row_index < WIDTH) == first_z
    lane_edge = lax.broadcasted_iota(jnp.int32, (rows + ROWS, LANES), 1)
    lane_keep = (lane_edge < WIDTH) | (lane_edge >= LANES - WIDTH)
    low_edge = low_lane[0:ROWS]
    joined = []
    for slot in range(3):
        low, high = got_full[slot, 1], got_full[slot, 0]
        joined.append(jnp.concatenate([
            jnp.where(low_lane, low, high),
            jnp.where(low_lane, shift(low, -WIDTH, 1), shift(high, WIDTH, 1)),
            jnp.where(row_keep, jnp.where(low_edge, got_edge[slot, 1], got_edge[slot, 0]), 0.0),
        ], axis=0))
    for f in range(FIELDS):
        for slot in range(3):
            for q in range(planes):
                p = slot * planes + q
                strip = jnp.zeros((ROWS, LANES), jnp.float32)
                if (f, q) in strip_list[slot]:
                    index = strip_list[slot].index((f, q))
                    strip = got_rows[slot, index // 2]
                    if index % 2 == 1:
                        strip = shift(strip, WIDTH, 0)
                    strip = jnp.where(row_keep, strip, 0.0)
                grown[f][p, rows : rows + ROWS, 0:LANES] = strip
                grown[f][p, :, LANES : 2 * LANES] = jnp.where(
                    lane_keep, shift(joined[slot], -2 * WIDTH * (f * planes + q), 1), 0.0)

    def wait_face(f):
        for index, entry in faces:
            if index == f:
                wait_recv(entry)

    wait_face(0)
    faces_fine = face_planes([grown[0][p] for p in range(3 * planes)], True)
    wait_face(1)
    start = [grown[1][p] for p in range(3 * planes)]
    applied = operate_planes(faces_fine, start, 1, 3 * planes - 1)
    wait_face(2)
    residual = [None] * (3 * planes)
    for p in range(1, 3 * planes - 1):
        residual[p] = grown[2][p] - applied[p]
    solved, residual = smooth_planes(faces_fine, residual, start, True)
    spread(
        1, restrict_fine([residual[planes + q][0:rows, 0:LANES] for q in range(planes)], 0.25))
    settle_hop(0, True)
    second_hop(0)
    for q in range(planes):
        out_fine[q] = solved[planes + q][0:rows, 0:LANES]
    stores[0].start()

    lane_one = lax.broadcasted_iota(jnp.int32, (2 * ROWS, LANES), 1)
    lower = lane_one < LANES // 2
    empty = jnp.zeros((ROWS, LANES), jnp.float32)

    def assemble(part):
        level = []
        for from_x in range(count_x):
            blocks = [[], []]
            for from_z in range(count_z):
                block = from_z * count_x + from_x
                own = all_one[part, block]
                low, high = all_half[part, 0, block], all_half[part, 1, block]
                beside = jnp.concatenate(
                    [jnp.where(quarter, high, low),
                     jnp.where(quarter, shift(high, -(LANES // 4), 1), shift(low, LANES // 4, 1))],
                    axis=0)
                blocks[0].append(jnp.where(lower, own, shift(beside, LANES // 2, 1)))
                blocks[1].append(jnp.where(lower, shift(own, LANES // 2, 1), beside))
            for q in range(2):
                level.append(jnp.concatenate(blocks[q] + [empty], axis=0))
        return level

    def restrict(level, matrix, scale):
        length = level[0].shape[0] - ROWS
        summed = []
        for q in range(len(level) // 2):
            both = level[2 * q] + level[2 * q + 1]
            summed.append(pair_rows(both[0:length], hold))
        joined = scale * split_dot(jnp.concatenate(summed, axis=0), matrix)
        half = length // 2
        return [
            jnp.concatenate([joined[q * half : (q + 1) * half], empty], axis=0)
            for q in range(len(summed))
        ]

    matrix_two = pair_matrix(3 * LANES // 4, LANES // 4, 0)
    matrix_three = pair_matrix(3 * LANES // 8, LANES // 8, 0)
    settle(0, True)
    conduct_one = assemble(0)
    conduct_two = restrict(conduct_one, matrix_two, 0.125)
    conduct_three = restrict(conduct_two, matrix_three, 0.125)
    faces_one, faces_two, faces_three = (
        face_planes(conduct, False) for conduct in (conduct_one, conduct_two, conduct_three))

    settle(1, True)
    solved, residual = smooth_planes(faces_one, assemble(1), None, False)
    for p in range(len(solved)):
        block = solved[p][0 : 2 * rows // 2]
        solved_one[p] = jnp.where(first_z, block[0 : rows // 2], block[rows // 2 : rows])
    out_one[...] = solved_one[pl.ds(2 * x, 2), :, 0 : LANES // 2]
    stores[1].start()
    solved, residual = smooth_planes(
        faces_two, restrict(residual, matrix_two, 0.25), None, False)
    for p in range(len(solved)):
        half = rows // 4
        out_two[p] = jnp.where(first_z, solved[p][0:half], solved[p][half : 2 * half])[:, 0 : LANES // 4]
    stores[2].start()
    solved, residual = smooth_planes(
        faces_three, restrict(residual, matrix_three, 0.25), None, False)
    for p in range(len(solved)):
        half = rows // 8
        for result, out in ((solved, out_three), (residual, out_rest)):
            out[p] = jnp.where(first_z, result[p][0:half], result[p][half : 2 * half])[:, 0 : LANES // 8]

    stores[3].start()
    stores[4].start()
    for entry in strips_sent + [entry for _, entry in faces]:
        wait_send(entry)
    settle_hop(0, False)
    settle(0, False)
    settle(1, False)
    for store in stores:
        store.wait()


def hand_over(*refs):
    count = len(refs) // 2
    copies = []
    for i in range(count):
        copies.append(pltpu.make_async_copy(refs[i], refs[count + i], refs[-1].at[i]))
        copies[-1].start()
    for copy in copies:
        copy.wait()


def fits(mesh, shape):
    return (
        mesh.shape["gz"] == 2
        and mesh.shape["gx"] <= 4
        and shape[0] == WIDTH * mesh.shape["gx"]
        and shape[1] == 32 * mesh.shape["gz"]
        and shape[2] == LANES * mesh.shape["gy"]
    )


def fused(mesh, conductivity, initial_guess, right_side):
    sizes = (mesh.shape["gx"], mesh.shape["gy"], mesh.shape["gz"])
    count_x, _, count_z = sizes
    planes, rows, lanes = conductivity.shape
    f32 = jnp.float32
    shapes = [
        (planes, rows, lanes),
        (planes // 2, rows // 2, lanes // 2),
        (count_x * planes // 4, rows // 4, lanes // 4),
        (count_x * planes // 8, rows // 8, lanes // 8),
        (count_x * planes // 8, rows // 8, lanes // 8),
    ]
    blocks_all = count_x * count_z
    dma = pltpu.SemaphoreType.DMA
    scratch = [pltpu.VMEM((3 * planes, rows + ROWS, 2 * LANES), f32)] * FIELDS + [
        pltpu.VMEM((2, rows // 2, LANES), f32),
        pltpu.VMEM((ROWS, LANES), f32),
        pltpu.VMEM((3, FIELDS * planes // 2, ROWS, LANES), f32),
        pltpu.VMEM((3, 2, rows // 2, LANES), f32),
        pltpu.VMEM((3, 2, ROWS, LANES), f32),
        pltpu.VMEM((3, FIELDS * planes // 2, ROWS, LANES), f32),
        pltpu.VMEM((2, rows // 2, LANES), f32),
        pltpu.VMEM((2, 2, ROWS, LANES), f32),
        pltpu.VMEM((2, 2, count_x, ROWS, LANES), f32),
        pltpu.VMEM((2, blocks_all, rows // 2, LANES), f32),
        pltpu.VMEM((2, 2, blocks_all, ROWS, LANES), f32),
        pltpu.VMEM((rows, LANES), f32),
        pltpu.VMEM((2 * count_x, rows // 2, LANES), f32),
        *[pltpu.VMEM(shape, f32) for shape in shapes],
        dma((3,)),
        dma((6,)), dma((6,)),
        dma((3,)), dma((3,)),
        dma((6,)), dma((6,)),
        dma((6,)), dma((6,)),
        dma((2, 3)), dma((2, 3)),
        dma((2,)), dma((2,)),
        dma((5,)),
    ]
    outside = pl.BlockSpec(memory_space=pltpu.HBM)
    out_shape = [jax.ShapeDtypeStruct(shape, f32) for shape in shapes]
    results = pl.pallas_call(
        functools.partial(kernel, sizes),
        out_shape=out_shape,
        in_specs=[outside] * 3,
        out_specs=[outside] * 5,
        scratch_shapes=scratch,
        compiler_params=pltpu.CompilerParams(
            collective_id=0, has_side_effects=True, vmem_limit_bytes=56 * 2**20),
    )(conductivity, initial_guess, right_side)
    return pl.pallas_call(
        hand_over,
        out_shape=out_shape,
        in_specs=[pl.BlockSpec(memory_space=pltpu.VMEM)] * 5,
        out_specs=[outside] * 5,
        scratch_shapes=[dma((5,))],
        compiler_params=pltpu.CompilerParams(vmem_limit_bytes=56 * 2**20),
    )(*results)


def solution(mesh):
    placed = (P("gx", "gz", "gy"), P("gx", "gz", "gy"), P("gx", "gz", "gy"))

    def whole(conductivity, initial_guess, right_side):
        local = shards
        if fits(mesh, conductivity.shape):
            local = functools.partial(fused, mesh)
        return jax.shard_map(
            local,
            mesh=mesh,
            in_specs=placed,
            out_specs=(
                P("gx", "gz", "gy"),
                P("gx", "gz", "gy"),
                P(None, "gz", "gy"),
                P(None, "gz", "gy"),
                P(None, "gz", "gy"),
            ),
            check_vma=False,
        )(conductivity, initial_guess, right_side)

    return whole
```

```python
import functools

import jax
import jax.numpy as jnp
from jax import lax
from jax.experimental import pallas as pl
from jax.experimental.pallas import tpu as pltpu
from jax.sharding import PartitionSpec as P

SWEEPS = 3


lower_bound = 0.25
upper_bound = 2.0


def with_halo(block, sides, width):
    for axis, dim in sides:
        count = lax.axis_size(axis)
        forward = [(i, i + 1) for i in range(count - 1)]
        backward = [(target, source) for source, target in forward]
        low = lax.ppermute(
            lax.slice_in_dim(block, block.shape[dim] - width, None, axis=dim), axis, forward
        )
        high = lax.ppermute(lax.slice_in_dim(block, 0, width, axis=dim), axis, backward)
        block = jnp.concatenate([low, block, high], axis=dim)
    return block


def extend(bundle):
    return with_halo(bundle, (("gx", 1), ("gy", 3), ("gz", 2)), 1)


def deep_extend(bundle, merged):
    if merged:
        grown = with_halo(bundle, (("gy", 3), ("gz", 2)), 4)
        return jnp.pad(grown, ((0, 0), (4, 4), (0, 0), (0, 0)))
    return with_halo(bundle, (("gx", 1), ("gy", 3), ("gz", 2)), 4)


def neighbours(padded):
    return [
        padded[:-2, 1:-1, 1:-1],
        padded[2:, 1:-1, 1:-1],
        padded[1:-1, :-2, 1:-1],
        padded[1:-1, 2:, 1:-1],
        padded[1:-1, 1:-1, :-2],
        padded[1:-1, 1:-1, 2:],
    ]


def face_terms(conduct):
    others = neighbours(extend(conduct[None])[0])
    weights = [0.5 * (conduct + other) for other in others]
    diagonal = weights[0] + weights[1] + weights[2] + weights[3] + weights[4] + weights[5]
    return (weights, diagonal)


def operate(field, weights, diagonal):
    others = neighbours(extend(field[None])[0])
    result = diagonal * field
    for face_index in range(6):
        result = result - weights[face_index] * others[face_index]
    return result


def smooth(source, conduct):
    theta = 0.5 * (upper_bound + lower_bound)
    delta = 0.5 * (upper_bound - lower_bound)
    sigma = theta / delta
    weights, diagonal = face_terms(conduct)
    solution = jnp.zeros_like(source)
    residual = source
    direction = residual / (theta * diagonal)
    ratio_now = 1.0 / sigma
    for sweep_index in range(SWEEPS):
        solution = solution + direction
        residual = residual - operate(direction, weights, diagonal)
        if sweep_index + 1 < SWEEPS:
            ratio_next = 1.0 / (2.0 * sigma - ratio_now)
            direction = (
                ratio_next * ratio_now * direction + 2.0 * ratio_next / delta * residual / diagonal
            )
            ratio_now = ratio_next
    return (solution, residual)


def local_operate(field, weights, diagonal):
    others = neighbours(jnp.pad(field, 1))
    result = diagonal * field
    for face_index in range(6):
        result = result - weights[face_index] * others[face_index]
    return result


def smooth_deep(source, start, conduct, merged):
    theta = 0.5 * (upper_bound + lower_bound)
    delta = 0.5 * (upper_bound - lower_bound)
    sigma = theta / delta
    members = [conduct, source, jnp.ones_like(source)]
    if start is not None:
        members.append(start)
    grown = deep_extend(jnp.stack(members), merged)
    padded_conduct = grown[0]
    padded_source = grown[1]
    inside = grown[2]
    others = neighbours(jnp.pad(padded_conduct, 1))
    weights = [0.5 * (padded_conduct + other) for other in others]
    diagonal = weights[0] + weights[1] + weights[2] + weights[3] + weights[4] + weights[5]
    safe_diagonal = jnp.where(inside > 0.5, diagonal, 1.0)
    if start is None:
        solution = jnp.zeros_like(padded_source)
        residual = padded_source
    else:
        solution = grown[3]
        residual = padded_source - local_operate(solution, weights, diagonal)
    direction = inside * (residual / (theta * safe_diagonal))
    ratio_now = 1.0 / sigma
    for sweep_index in range(SWEEPS):
        solution = solution + direction
        residual = residual - local_operate(direction, weights, diagonal)
        if sweep_index + 1 < SWEEPS:
            ratio_next = 1.0 / (2.0 * sigma - ratio_now)
            direction = inside * (
                ratio_next * ratio_now * direction
                + 2.0 * ratio_next / delta * residual / safe_diagonal
            )
            ratio_now = ratio_next
    return (solution[4:-4, 4:-4, 4:-4], residual[4:-4, 4:-4, 4:-4])


def level_smooth(source, start, conduct, merged):
    extents = source.shape[1:] if merged else source.shape
    if min(extents) >= 4:
        return smooth_deep(source, start, conduct, merged)
    return smooth(source, conduct)


def coarse_sum(field):
    first, second, third = field.shape
    blocks = field.reshape(first // 2, 2, second // 2, 2, third // 2, 2)
    return jnp.sum(blocks, axis=(1, 3, 5))


def shards(conductivity, initial_guess, right_side):
    fine_solution, residual_zero = level_smooth(right_side, initial_guess, conductivity, False)
    conduct_one = 0.125 * coarse_sum(conductivity)
    level_one_solution, residual_one = level_smooth(
        0.25 * coarse_sum(residual_zero), None, conduct_one, False
    )
    conduct_two = 0.125 * coarse_sum(conduct_one)
    source_two = 0.25 * coarse_sum(residual_one)
    bundle = jnp.stack([source_two, conduct_two])
    bundle = lax.all_gather(bundle, "gx", axis=1, tiled=True)
    level_two_solution, residual_two = level_smooth(bundle[0], None, bundle[1], True)
    conduct_three = 0.125 * coarse_sum(bundle[1])
    level_three_solution, level_three_residual = level_smooth(
        0.25 * coarse_sum(residual_two), None, conduct_three, True
    )
    return (
        fine_solution,
        level_one_solution,
        level_two_solution,
        level_three_solution,
        level_three_residual,
    )


FIELDS = 3
WIDTH = 4
ROWS = 8
LANES = 128


def in_range(index, count):
    return (index >= 0) & (index < count)


def shift(value, amount, axis):
    return pltpu.roll(value, amount % value.shape[axis], axis)


def face_planes(conduct, grown):
    count = len(conduct)
    edge = 1 if grown else 0
    weight_x = [None] * (count + 1)
    for i in range(1, count):
        weight_x[i] = 0.5 * (conduct[i - 1] + conduct[i])
    if not grown:
        weight_x[0] = 0.5 * conduct[0]
        weight_x[count] = 0.5 * conduct[count - 1]
    weight_z = [None] * count
    weight_y = [None] * count
    inverse = [None] * count
    for i in range(edge, count - edge):
        weight_z[i] = 0.5 * (conduct[i] + shift(conduct[i], -1, 0))
        weight_y[i] = 0.5 * (conduct[i] + shift(conduct[i], -1, 1))
        diagonal = weight_x[i] + weight_x[i + 1]
        diagonal = diagonal + (weight_z[i] + shift(weight_z[i], 1, 0))
        diagonal = diagonal + (weight_y[i] + shift(weight_y[i], 1, 1))
        inside = conduct[i] > 0.0
        inverse[i] = jnp.where(inside, 1.0 / jnp.where(inside, diagonal, 1.0), 0.0)
    return weight_x, weight_y, weight_z, inverse


def operate_planes(faces, field, low, high):
    weight_x, weight_y, weight_z, _ = faces
    count = len(field)
    flux_x = [None] * (count + 1)
    for i in range(low, high + 1):
        if i == 0:
            flux_x[i] = weight_x[i] * field[i]
        elif i == count:
            flux_x[i] = -(weight_x[i] * field[i - 1])
        else:
            flux_x[i] = weight_x[i] * (field[i] - field[i - 1])
    result = [None] * count
    for i in range(low, high):
        flux_z = weight_z[i] * (field[i] - shift(field[i], -1, 0))
        flux_y = weight_y[i] * (field[i] - shift(field[i], -1, 1))
        result[i] = (
            (flux_x[i] - flux_x[i + 1])
            + (flux_z - shift(flux_z, 1, 0))
            + (flux_y - shift(flux_y, 1, 1))
        )
    return result


def smooth_planes(faces, residual, start, grown):
    theta = 0.5 * (upper_bound + lower_bound)
    delta = 0.5 * (upper_bound - lower_bound)
    sigma = theta / delta
    inverse = faces[3]
    count = len(residual)
    edge = 1 if grown else 0
    low, high = edge, count - edge
    residual = list(residual)
    direction = [None] * count
    for i in range(low, high):
        direction[i] = residual[i] * (inverse[i] * (1.0 / theta))
    ratio_now = 1.0 / sigma
    solution = list(start) if start is not None else [None] * count
    for sweep_index in range(SWEEPS):
        for i in range(low, high):
            solution[i] = direction[i] if solution[i] is None else solution[i] + direction[i]
        low, high = low + edge, high - edge
        applied = operate_planes(faces, direction, low, high)
        for i in range(low, high):
            residual[i] = residual[i] - applied[i]
        if sweep_index + 1 < SWEEPS:
            ratio_next = 1.0 / (2.0 * sigma - ratio_now)
            turned = [None] * count
            for i in range(low, high):
                turned[i] = (ratio_next * ratio_now) * direction[i] + (
                    2.0 * ratio_next / delta
                ) * (residual[i] * inverse[i])
            direction = turned
            ratio_now = ratio_next
    return solution, residual


def split_dot(value, matrix):
    parts = []
    rest = value
    for _ in range(3):
        part = rest.astype(jnp.bfloat16)
        parts.append(part.astype(jnp.float32))
        rest = rest - parts[-1]
    rows = value.shape[0]
    stacked = jnp.concatenate(parts, axis=0).astype(jnp.bfloat16)
    product = jnp.dot(stacked, matrix, preferred_element_type=jnp.float32)
    return product[:rows] + product[rows : 2 * rows] + product[2 * rows :]


def pair_matrix(keep_low, keep_high, offset):
    source = lax.broadcasted_iota(jnp.int32, (LANES, LANES), 0)
    target = lax.broadcasted_iota(jnp.int32, (LANES, LANES), 1)
    low = (source < keep_low) & (target == offset + source // 2)
    high = (source >= LANES - keep_high) & (target == LANES // 2 + source // 2)
    return jnp.where(low | high, 1.0, 0.0).astype(jnp.bfloat16)


def pair_rows(value, hold):
    rows = value.shape[0]
    hold[0:rows, :] = value
    return hold[pl.ds(0, rows // 2, stride=2), :] + hold[pl.ds(1, rows // 2, stride=2), :]


def kernel(sizes, *refs):
    count_x, count_y, count_z = sizes
    inputs = refs[0:3]
    outs = refs[3:8]
    grown = refs[8:11]
    (pack_full, pack_edge, pack_rows, got_full, got_edge, got_rows, own_one, line_half, all_one,
     all_half, hold, solved_one, out_fine, out_one, out_two,
     out_three, out_rest, load_sem, face_send, face_recv, row_send, row_recv,
     full_send, full_recv, edge_send, edge_recv, one_send, one_recv, hop_send, hop_recv, store_sem) = refs[11:]
    kept = (out_fine, out_one, out_two, out_three, out_rest)
    stores = [pltpu.make_async_copy(kept[i], outs[i], store_sem.at[i]) for i in range(5)]
    planes, rows = inputs[0].shape[0], inputs[0].shape[1]
    x = lax.axis_index("gx")
    y = lax.axis_index("gy")
    z = lax.axis_index("gz")
    first_z = z == 0

    loads = []
    for f in range(FIELDS):
        loads.append(pltpu.make_async_copy(
            inputs[f], grown[f].at[planes : 2 * planes, 0:rows, 0:LANES], load_sem.at[f]))
        loads[-1].start()

    def other(step, turn, dy):
        return {"gx": lax.rem(x + step, count_x), "gy": y + dy, "gz": lax.rem(z + turn, count_z)}

    near = planes - WIDTH
    strip_list = [
        [(f, q) for f in range(FIELDS) for q in range(planes)
         if q > near + (1 if f == 2 else 0)],
        [(f, q) for f in range(FIELDS) for q in range(planes)],
        [(f, q) for f in range(FIELDS) for q in range(planes)
         if q < WIDTH - 1 - (1 if f == 2 else 0)],
    ]
    barrier = pltpu.get_barrier_semaphore()

    def greet(dx, dy, dz):
        pl.semaphore_signal(
            barrier, inc=1, device_id={"gx": x + dx, "gy": y + dy, "gz": lax.rem(z + dz, count_z)},
            device_id_type=pl.DeviceIdType.MESH)

    for dx in (0, 1, -1):
        for dy in (0, 1, -1):
            @pl.when(in_range(x + dx, count_x) & in_range(y + dy, count_y))
            def _():
                for dz in range(count_z):
                    if (dx, dy, dz) != (0, 0, 0):
                        greet(dx, dy, dz)
    for distance in range(2, count_x):
        for dx in (distance, -distance):
            pl.when(in_range(x + dx, count_x))(functools.partial(greet, dx, 0, 0))

    for f in range(FIELDS):
        @pl.when(x == 0)
        def _():
            grown[f][0:planes, 0:rows, 0:LANES] = jnp.zeros((planes, rows, LANES), jnp.float32)

        @pl.when(x == count_x - 1)
        def _():
            grown[f][2 * planes : 3 * planes, 0:rows, 0:LANES] = jnp.zeros(
                (planes, rows, LANES), jnp.float32)

    for slot in range(3):
        for side in range(2):
            there = in_range(x + (slot - 1), count_x) & in_range(y + (2 * side - 1), count_y)

            @pl.when(jnp.logical_not(there))
            def _():
                got_full[slot, side] = jnp.zeros((rows // 2, LANES), jnp.float32)
                got_edge[slot, side] = jnp.zeros((ROWS, LANES), jnp.float32)

        if slot != 1:
            @pl.when(jnp.logical_not(in_range(x + (slot - 1), count_x)))
            def _():
                got_rows[slot] = jnp.zeros(got_rows.shape[1:], jnp.float32)

    for side in range(2):
        @pl.when(jnp.logical_not(in_range(y + (2 * side - 1), count_y)))
        def _():
            for part in range(2):
                all_half[part, side] = jnp.zeros(all_half.shape[2:], jnp.float32)

    for load in loads:
        load.wait()

    lane = lax.broadcasted_iota(jnp.int32, (rows, LANES), 1)
    row_index = lax.broadcasted_iota(jnp.int32, (ROWS, LANES), 0)
    low_lane = lax.rem(lane[0 : rows // 2], 2 * WIDTH) < WIDTH
    leave = (row_index < WIDTH) == jnp.logical_not(first_z)
    strips = {}
    packed = jnp.zeros((rows, LANES), jnp.float32)
    for f in range(FIELDS):
        for q in range(planes):
            k = f * planes + q
            piece = grown[f][planes + q, 0:rows, 0:LANES]
            strips[f, q] = jnp.where(first_z, piece[rows - ROWS :], piece[0:ROWS])
            moved = shift(piece, 2 * WIDTH * k, 1)
            window = lax.rem(lane - 2 * WIDTH * k + WIDTH + LANES, LANES) < 2 * WIDTH
            packed = jnp.where(window, moved, packed)
    for slot in range(3):
        for t in range(len(strip_list[slot]) // 2):
            first, second = strip_list[slot][2 * t], strip_list[slot][2 * t + 1]
            pack_rows[slot, t] = jnp.where(
                leave, strips[first], shift(strips[second], WIDTH, 0))
    top, bottom = packed[0 : rows // 2], packed[rows // 2 : rows]
    pack_full[0] = jnp.where(low_lane, shift(bottom, -WIDTH, 1), top)
    pack_full[1] = jnp.where(low_lane, top, shift(bottom, WIDTH, 1))
    pack_edge[...] = jnp.where(first_z, packed[rows - ROWS :], packed[0:ROWS])

    beside_x = jnp.where(x > 0, 1, 0) + jnp.where(x < count_x - 1, 1, 0)
    beside_y = jnp.where(y > 0, 1, 0) + jnp.where(y < count_y - 1, 1, 0)
    wanted = (1 + beside_x) * (1 + beside_y) * count_z - 1 + (count_x - 1 - beside_x)
    pl.semaphore_wait(barrier, wanted)

    def send(src, dst, send_sem, recv_sem, device, to, back):
        copy = pltpu.make_async_remote_copy(
            src_ref=src, dst_ref=dst, send_sem=send_sem, recv_sem=recv_sem,
            device_id=device, device_id_type=pl.DeviceIdType.MESH)
        if to is None:
            copy.start()
        else:
            pl.when(to)(copy.start)
        return copy, to, back

    def wait_recv(entry):
        copy, _, back = entry
        if back is None:
            copy.wait_recv()
        else:
            pl.when(back)(copy.wait_recv)

    def wait_send(entry):
        copy, to, _ = entry
        if to is None:
            copy.wait_send()
        else:
            pl.when(to)(copy.wait_send)

    faces = []
    strips_sent = []

    def send_face(f):
        for dx in (1, -1):
            to, back = in_range(x + dx, count_x), in_range(x - dx, count_x)
            low, high = 0, planes
            if f == 2:
                low, high = (1, planes) if dx == 1 else (0, planes - 1)
            base = 0 if dx == 1 else 2 * planes
            index = (dx + 1) // 2 * FIELDS + f
            faces.append((f, send(
                grown[f].at[planes + low : planes + high, 0:rows, 0:LANES],
                grown[f].at[base + low : base + high, 0:rows, 0:LANES],
                face_send.at[index], face_recv.at[index],
                {"gx": x + dx, "gy": y, "gz": z}, to, back)))

    send_face(0)
    for dx in (1, -1, 0):
        slot = 1 - dx
        to, back = (in_range(x + dx, count_x), in_range(x - dx, count_x)) if dx else (None, None)
        tiles = len(strip_list[slot]) // 2
        strips_sent.append(send(
            pack_rows.at[slot, 0:tiles], got_rows.at[slot, 0:tiles], row_send.at[slot],
            row_recv.at[slot], {"gx": x + dx, "gy": y, "gz": 1 - z}, to, back))
        for dy in (1, -1):
            side = (1 - dy) // 2
            to = in_range(x + dx, count_x) & in_range(y + dy, count_y)
            back = in_range(x - dx, count_x) & in_range(y - dy, count_y)
            strips_sent.append(send(
                pack_full.at[side], got_full.at[slot, side], full_send.at[slot * 2 + side],
                full_recv.at[slot * 2 + side], {"gx": x + dx, "gy": y + dy, "gz": z}, to, back))
            strips_sent.append(send(
                pack_edge, got_edge.at[slot, side], edge_send.at[slot * 2 + side],
                edge_recv.at[slot * 2 + side], {"gx": x + dx, "gy": y + dy, "gz": 1 - z}, to, back))
    send_face(1)
    send_face(2)

    to_one = [pair_matrix(LANES, 0, 0), pair_matrix(LANES, 0, LANES // 2)]
    matrix_one = jnp.concatenate(to_one, axis=0)
    quarter = lax.broadcasted_iota(jnp.int32, (ROWS, LANES), 1) % (LANES // 2) < LANES // 4

    def restrict_fine(blocks, scale):
        pairs = [pair_rows(blocks[2 * q] + blocks[2 * q + 1], hold) for q in range(planes // 2)]
        return scale * split_dot(jnp.concatenate(pairs, axis=1), matrix_one)

    here = z * count_x + x
    line = pl.ds(z * count_x, count_x)

    def remote(source, target, send_sem, recv_sem, device):
        return pltpu.make_async_remote_copy(
            src_ref=source, dst_ref=target, send_sem=send_sem, recv_sem=recv_sem,
            device_id=device, device_id_type=pl.DeviceIdType.MESH)

    def first_hop(part, value):
        own_one[part] = value
        all_one[part, here] = value
        for step in range(1, count_x):
            remote(own_one.at[part], all_one.at[part, here], hop_send.at[part],
                   hop_recv.at[part], other(step, 0, 0)).start()

    def settle_hop(part, received):
        bytes_of = all_one.at[part, 0 : count_x - 1]
        copy = remote(bytes_of, bytes_of, hop_send.at[part], hop_recv.at[part], other(1, 0, 0))
        copy.wait_recv() if received else copy.wait_send()

    def line_copies(part, dy):
        side = (1 - dy) // 2
        sems = (one_send.at[part, dy + 1], one_recv.at[part, dy + 1])
        if dy == 0:
            return [remote(all_one.at[part, line], all_one.at[part, line], *sems, other(0, 1, 0))]
        return [
            remote(line_half.at[part, side], all_half.at[part, side, line], *sems,
                   other(0, turn, dy))
            for turn in range(count_z)
        ]

    def second_hop(part):
        for from_x in range(count_x):
            value = all_one[part, z * count_x + from_x]
            top, bottom = value[0:ROWS], value[ROWS : 2 * ROWS]
            line_half[part, 0, from_x] = jnp.where(quarter, shift(bottom, -(LANES // 4), 1), top)
            line_half[part, 1, from_x] = jnp.where(quarter, top, shift(bottom, LANES // 4, 1))
        for dy in (0, 1, -1):
            def start():
                for copy in line_copies(part, dy):
                    copy.start()

            if dy == 0:
                start()
            else:
                pl.when(in_range(y + dy, count_y))(start)

    def settle(part, received):
        for dy in (0, 1, -1):
            side = (1 - dy) // 2
            if dy == 0:
                bytes_of = all_one.at[part, line]
            else:
                bytes_of = all_half.at[part, side]
            copy = remote(bytes_of, bytes_of, one_send.at[part, dy + 1],
                          one_recv.at[part, dy + 1], other(1, 0, 0))
            finish = copy.wait_recv if received else copy.wait_send
            if dy == 0:
                finish()
            else:
                pl.when(in_range(y - dy if received else y + dy, count_y))(finish)

    coarse_conduct = restrict_fine(
        [grown[0][planes + q, 0:rows, 0:LANES] for q in range(planes)], 0.125)
    first_hop(0, coarse_conduct)

    for entry in strips_sent:
        wait_recv(entry)
    row_keep = (row_index < WIDTH) == first_z
    lane_edge = lax.broadcasted_iota(jnp.int32, (rows + ROWS, LANES), 1)
    lane_keep = (lane_edge < WIDTH) | (lane_edge >= LANES - WIDTH)
    low_edge = low_lane[0:ROWS]
    joined = []
    for slot in range(3):
        low, high = got_full[slot, 1], got_full[slot, 0]
        joined.append(jnp.concatenate([
            jnp.where(low_lane, low, high),
            jnp.where(low_lane, shift(low, -WIDTH, 1), shift(high, WIDTH, 1)),
            jnp.where(row_keep, jnp.where(low_edge, got_edge[slot, 1], got_edge[slot, 0]), 0.0),
        ], axis=0))
    for f in range(FIELDS):
        for slot in range(3):
            for q in range(planes):
                p = slot * planes + q
                strip = jnp.zeros((ROWS, LANES), jnp.float32)
                if (f, q) in strip_list[slot]:
                    index = strip_list[slot].index((f, q))
                    strip = got_rows[slot, index // 2]
                    if index % 2 == 1:
                        strip = shift(strip, WIDTH, 0)
                    strip = jnp.where(row_keep, strip, 0.0)
                grown[f][p, rows : rows + ROWS, 0:LANES] = strip
                grown[f][p, :, LANES : 2 * LANES] = jnp.where(
                    lane_keep, shift(joined[slot], -2 * WIDTH * (f * planes + q), 1), 0.0)

    def wait_face(f):
        for index, entry in faces:
            if index == f:
                wait_recv(entry)

    wait_face(0)
    faces_fine = face_planes([grown[0][p] for p in range(3 * planes)], True)
    wait_face(1)
    start = [grown[1][p] for p in range(3 * planes)]
    applied = operate_planes(faces_fine, start, 1, 3 * planes - 1)
    wait_face(2)
    residual = [None] * (3 * planes)
    for p in range(1, 3 * planes - 1):
        residual[p] = grown[2][p] - applied[p]
    solved, residual = smooth_planes(faces_fine, residual, start, True)
    first_hop(
        1, restrict_fine([residual[planes + q][0:rows, 0:LANES] for q in range(planes)], 0.25))
    settle_hop(0, True)
    second_hop(0)
    settle_hop(1, True)
    second_hop(1)
    for q in range(planes):
        out_fine[q] = solved[planes + q][0:rows, 0:LANES]
    stores[0].start()

    lane_one = lax.broadcasted_iota(jnp.int32, (2 * ROWS, LANES), 1)
    lower = lane_one < LANES // 2
    empty = jnp.zeros((ROWS, LANES), jnp.float32)

    def assemble(part):
        level = []
        for from_x in range(count_x):
            blocks = [[], []]
            for from_z in range(count_z):
                block = from_z * count_x + from_x
                own = all_one[part, block]
                low, high = all_half[part, 0, block], all_half[part, 1, block]
                beside = jnp.concatenate(
                    [jnp.where(quarter, high, low),
                     jnp.where(quarter, shift(high, -(LANES // 4), 1), shift(low, LANES // 4, 1))],
                    axis=0)
                blocks[0].append(jnp.where(lower, own, shift(beside, LANES // 2, 1)))
                blocks[1].append(jnp.where(lower, shift(own, LANES // 2, 1), beside))
            for q in range(2):
                level.append(jnp.concatenate(blocks[q] + [empty], axis=0))
        return level

    def restrict(level, matrix, scale):
        length = level[0].shape[0] - ROWS
        summed = []
        for q in range(len(level) // 2):
            both = level[2 * q] + level[2 * q + 1]
            summed.append(pair_rows(both[0:length], hold))
        joined = scale * split_dot(jnp.concatenate(summed, axis=0), matrix)
        half = length // 2
        return [
            jnp.concatenate([joined[q * half : (q + 1) * half], empty], axis=0)
            for q in range(len(summed))
        ]

    matrix_two = pair_matrix(3 * LANES // 4, LANES // 4, 0)
    matrix_three = pair_matrix(3 * LANES // 8, LANES // 8, 0)
    settle(0, True)
    conduct_one = assemble(0)
    conduct_two = restrict(conduct_one, matrix_two, 0.125)
    conduct_three = restrict(conduct_two, matrix_three, 0.125)
    faces_one, faces_two, faces_three = (
        face_planes(conduct, False) for conduct in (conduct_one, conduct_two, conduct_three))

    settle(1, True)
    solved, residual = smooth_planes(faces_one, assemble(1), None, False)
    for p in range(len(solved)):
        block = solved[p][0 : 2 * rows // 2]
        solved_one[p] = jnp.where(first_z, block[0 : rows // 2], block[rows // 2 : rows])
    out_one[...] = solved_one[pl.ds(2 * x, 2), :, 0 : LANES // 2]
    stores[1].start()
    solved, residual = smooth_planes(
        faces_two, restrict(residual, matrix_two, 0.25), None, False)
    for p in range(len(solved)):
        half = rows // 4
        out_two[p] = jnp.where(first_z, solved[p][0:half], solved[p][half : 2 * half])[:, 0 : LANES // 4]
    stores[2].start()
    solved, residual = smooth_planes(
        faces_three, restrict(residual, matrix_three, 0.25), None, False)
    for p in range(len(solved)):
        half = rows // 8
        for result, out in ((solved, out_three), (residual, out_rest)):
            out[p] = jnp.where(first_z, result[p][0:half], result[p][half : 2 * half])[:, 0 : LANES // 8]

    stores[3].start()
    stores[4].start()
    for entry in strips_sent + [entry for _, entry in faces]:
        wait_send(entry)
    settle_hop(0, False)
    settle_hop(1, False)
    settle(0, False)
    settle(1, False)
    for store in stores:
        store.wait()


def hand_over(*refs):
    count = len(refs) // 2
    copies = []
    for i in range(count):
        copies.append(pltpu.make_async_copy(refs[i], refs[count + i], refs[-1].at[i]))
        copies[-1].start()
    for copy in copies:
        copy.wait()


def fits(mesh, shape):
    return (
        mesh.shape["gz"] == 2
        and mesh.shape["gx"] <= 4
        and shape[0] == WIDTH * mesh.shape["gx"]
        and shape[1] == 32 * mesh.shape["gz"]
        and shape[2] == LANES * mesh.shape["gy"]
    )


def fused(mesh, conductivity, initial_guess, right_side):
    sizes = (mesh.shape["gx"], mesh.shape["gy"], mesh.shape["gz"])
    count_x, _, count_z = sizes
    planes, rows, lanes = conductivity.shape
    f32 = jnp.float32
    shapes = [
        (planes, rows, lanes),
        (planes // 2, rows // 2, lanes // 2),
        (count_x * planes // 4, rows // 4, lanes // 4),
        (count_x * planes // 8, rows // 8, lanes // 8),
        (count_x * planes // 8, rows // 8, lanes // 8),
    ]
    blocks_all = count_x * count_z
    dma = pltpu.SemaphoreType.DMA
    scratch = [pltpu.VMEM((3 * planes, rows + ROWS, 2 * LANES), f32)] * FIELDS + [
        pltpu.VMEM((2, rows // 2, LANES), f32),
        pltpu.VMEM((ROWS, LANES), f32),
        pltpu.VMEM((3, FIELDS * planes // 2, ROWS, LANES), f32),
        pltpu.VMEM((3, 2, rows // 2, LANES), f32),
        pltpu.VMEM((3, 2, ROWS, LANES), f32),
        pltpu.VMEM((3, FIELDS * planes // 2, ROWS, LANES), f32),
        pltpu.VMEM((2, rows // 2, LANES), f32),
        pltpu.VMEM((2, 2, count_x, ROWS, LANES), f32),
        pltpu.VMEM((2, blocks_all, rows // 2, LANES), f32),
        pltpu.VMEM((2, 2, blocks_all, ROWS, LANES), f32),
        pltpu.VMEM((rows, LANES), f32),
        pltpu.VMEM((2 * count_x, rows // 2, LANES), f32),
        *[pltpu.VMEM(shape, f32) for shape in shapes],
        dma((3,)),
        dma((6,)), dma((6,)),
        dma((3,)), dma((3,)),
        dma((6,)), dma((6,)),
        dma((6,)), dma((6,)),
        dma((2, 3)), dma((2, 3)),
        dma((2,)), dma((2,)),
        dma((5,)),
    ]
    outside = pl.BlockSpec(memory_space=pltpu.HBM)
    out_shape = [jax.ShapeDtypeStruct(shape, f32) for shape in shapes]
    results = pl.pallas_call(
        functools.partial(kernel, sizes),
        out_shape=out_shape,
        in_specs=[outside] * 3,
        out_specs=[outside] * 5,
        scratch_shapes=scratch,
        compiler_params=pltpu.CompilerParams(
            collective_id=0, has_side_effects=True, vmem_limit_bytes=56 * 2**20),
    )(conductivity, initial_guess, right_side)
    return pl.pallas_call(
        hand_over,
        out_shape=out_shape,
        in_specs=[pl.BlockSpec(memory_space=pltpu.VMEM)] * 5,
        out_specs=[outside] * 5,
        scratch_shapes=[dma((5,))],
        compiler_params=pltpu.CompilerParams(vmem_limit_bytes=56 * 2**20),
    )(*results)


def solution(mesh):
    placed = (P("gx", "gz", "gy"), P("gx", "gz", "gy"), P("gx", "gz", "gy"))

    def whole(conductivity, initial_guess, right_side):
        local = shards
        if fits(mesh, conductivity.shape):
            local = functools.partial(fused, mesh)
        return jax.shard_map(
            local,
            mesh=mesh,
            in_specs=placed,
            out_specs=(
                P("gx", "gz", "gy"),
                P("gx", "gz", "gy"),
                P(None, "gz", "gy"),
                P(None, "gz", "gy"),
                P(None, "gz", "gy"),
            ),
            check_vma=False,
        )(conductivity, initial_guess, right_side)

    return whole
```

```python
import functools

import jax
import jax.numpy as jnp
from jax import lax
from jax.experimental import pallas as pl
from jax.experimental.pallas import tpu as pltpu
from jax.sharding import PartitionSpec as P

SWEEPS = 3


lower_bound = 0.25
upper_bound = 2.0


def with_halo(block, sides, width):
    for axis, dim in sides:
        count = lax.axis_size(axis)
        forward = [(i, i + 1) for i in range(count - 1)]
        backward = [(target, source) for source, target in forward]
        low = lax.ppermute(
            lax.slice_in_dim(block, block.shape[dim] - width, None, axis=dim), axis, forward
        )
        high = lax.ppermute(lax.slice_in_dim(block, 0, width, axis=dim), axis, backward)
        block = jnp.concatenate([low, block, high], axis=dim)
    return block


def extend(bundle):
    return with_halo(bundle, (("gx", 1), ("gy", 3), ("gz", 2)), 1)


def deep_extend(bundle, merged):
    if merged:
        grown = with_halo(bundle, (("gy", 3), ("gz", 2)), 4)
        return jnp.pad(grown, ((0, 0), (4, 4), (0, 0), (0, 0)))
    return with_halo(bundle, (("gx", 1), ("gy", 3), ("gz", 2)), 4)


def neighbours(padded):
    return [
        padded[:-2, 1:-1, 1:-1],
        padded[2:, 1:-1, 1:-1],
        padded[1:-1, :-2, 1:-1],
        padded[1:-1, 2:, 1:-1],
        padded[1:-1, 1:-1, :-2],
        padded[1:-1, 1:-1, 2:],
    ]


def face_terms(conduct):
    others = neighbours(extend(conduct[None])[0])
    weights = [0.5 * (conduct + other) for other in others]
    diagonal = weights[0] + weights[1] + weights[2] + weights[3] + weights[4] + weights[5]
    return (weights, diagonal)


def operate(field, weights, diagonal):
    others = neighbours(extend(field[None])[0])
    result = diagonal * field
    for face_index in range(6):
        result = result - weights[face_index] * others[face_index]
    return result


def smooth(source, conduct):
    theta = 0.5 * (upper_bound + lower_bound)
    delta = 0.5 * (upper_bound - lower_bound)
    sigma = theta / delta
    weights, diagonal = face_terms(conduct)
    solution = jnp.zeros_like(source)
    residual = source
    direction = residual / (theta * diagonal)
    ratio_now = 1.0 / sigma
    for sweep_index in range(SWEEPS):
        solution = solution + direction
        residual = residual - operate(direction, weights, diagonal)
        if sweep_index + 1 < SWEEPS:
            ratio_next = 1.0 / (2.0 * sigma - ratio_now)
            direction = (
                ratio_next * ratio_now * direction + 2.0 * ratio_next / delta * residual / diagonal
            )
            ratio_now = ratio_next
    return (solution, residual)


def local_operate(field, weights, diagonal):
    others = neighbours(jnp.pad(field, 1))
    result = diagonal * field
    for face_index in range(6):
        result = result - weights[face_index] * others[face_index]
    return result


def smooth_deep(source, start, conduct, merged):
    theta = 0.5 * (upper_bound + lower_bound)
    delta = 0.5 * (upper_bound - lower_bound)
    sigma = theta / delta
    members = [conduct, source, jnp.ones_like(source)]
    if start is not None:
        members.append(start)
    grown = deep_extend(jnp.stack(members), merged)
    padded_conduct = grown[0]
    padded_source = grown[1]
    inside = grown[2]
    others = neighbours(jnp.pad(padded_conduct, 1))
    weights = [0.5 * (padded_conduct + other) for other in others]
    diagonal = weights[0] + weights[1] + weights[2] + weights[3] + weights[4] + weights[5]
    safe_diagonal = jnp.where(inside > 0.5, diagonal, 1.0)
    if start is None:
        solution = jnp.zeros_like(padded_source)
        residual = padded_source
    else:
        solution = grown[3]
        residual = padded_source - local_operate(solution, weights, diagonal)
    direction = inside * (residual / (theta * safe_diagonal))
    ratio_now = 1.0 / sigma
    for sweep_index in range(SWEEPS):
        solution = solution + direction
        residual = residual - local_operate(direction, weights, diagonal)
        if sweep_index + 1 < SWEEPS:
            ratio_next = 1.0 / (2.0 * sigma - ratio_now)
            direction = inside * (
                ratio_next * ratio_now * direction
                + 2.0 * ratio_next / delta * residual / safe_diagonal
            )
            ratio_now = ratio_next
    return (solution[4:-4, 4:-4, 4:-4], residual[4:-4, 4:-4, 4:-4])


def level_smooth(source, start, conduct, merged):
    extents = source.shape[1:] if merged else source.shape
    if min(extents) >= 4:
        return smooth_deep(source, start, conduct, merged)
    return smooth(source, conduct)


def coarse_sum(field):
    first, second, third = field.shape
    blocks = field.reshape(first // 2, 2, second // 2, 2, third // 2, 2)
    return jnp.sum(blocks, axis=(1, 3, 5))


def shards(conductivity, initial_guess, right_side):
    fine_solution, residual_zero = level_smooth(right_side, initial_guess, conductivity, False)
    conduct_one = 0.125 * coarse_sum(conductivity)
    level_one_solution, residual_one = level_smooth(
        0.25 * coarse_sum(residual_zero), None, conduct_one, False
    )
    conduct_two = 0.125 * coarse_sum(conduct_one)
    source_two = 0.25 * coarse_sum(residual_one)
    bundle = jnp.stack([source_two, conduct_two])
    bundle = lax.all_gather(bundle, "gx", axis=1, tiled=True)
    level_two_solution, residual_two = level_smooth(bundle[0], None, bundle[1], True)
    conduct_three = 0.125 * coarse_sum(bundle[1])
    level_three_solution, level_three_residual = level_smooth(
        0.25 * coarse_sum(residual_two), None, conduct_three, True
    )
    return (
        fine_solution,
        level_one_solution,
        level_two_solution,
        level_three_solution,
        level_three_residual,
    )


FIELDS = 3
WIDTH = 4
ROWS = 8
LANES = 128


def in_range(index, count):
    return (index >= 0) & (index < count)


def shift(value, amount, axis):
    return pltpu.roll(value, amount % value.shape[axis], axis)


def face_planes(conduct, grown):
    count = len(conduct)
    edge = 1 if grown else 0
    weight_x = [None] * (count + 1)
    for i in range(1, count):
        weight_x[i] = 0.5 * (conduct[i - 1] + conduct[i])
    if not grown:
        weight_x[0] = 0.5 * conduct[0]
        weight_x[count] = 0.5 * conduct[count - 1]
    weight_z = [None] * count
    weight_y = [None] * count
    inverse = [None] * count
    for i in range(edge, count - edge):
        weight_z[i] = 0.5 * (conduct[i] + shift(conduct[i], -1, 0))
        weight_y[i] = 0.5 * (conduct[i] + shift(conduct[i], -1, 1))
        diagonal = weight_x[i] + weight_x[i + 1]
        diagonal = diagonal + (weight_z[i] + shift(weight_z[i], 1, 0))
        diagonal = diagonal + (weight_y[i] + shift(weight_y[i], 1, 1))
        inside = conduct[i] > 0.0
        inverse[i] = jnp.where(inside, 1.0 / jnp.where(inside, diagonal, 1.0), 0.0)
    return weight_x, weight_y, weight_z, inverse


def operate_planes(faces, field, low, high):
    weight_x, weight_y, weight_z, _ = faces
    count = len(field)
    flux_x = [None] * (count + 1)
    for i in range(low, high + 1):
        if i == 0:
            flux_x[i] = weight_x[i] * field[i]
        elif i == count:
            flux_x[i] = -(weight_x[i] * field[i - 1])
        else:
            flux_x[i] = weight_x[i] * (field[i] - field[i - 1])
    result = [None] * count
    for i in range(low, high):
        flux_z = weight_z[i] * (field[i] - shift(field[i], -1, 0))
        flux_y = weight_y[i] * (field[i] - shift(field[i], -1, 1))
        result[i] = (
            (flux_x[i] - flux_x[i + 1])
            + (flux_z - shift(flux_z, 1, 0))
            + (flux_y - shift(flux_y, 1, 1))
        )
    return result


def smooth_planes(faces, residual, start, grown):
    theta = 0.5 * (upper_bound + lower_bound)
    delta = 0.5 * (upper_bound - lower_bound)
    sigma = theta / delta
    inverse = faces[3]
    count = len(residual)
    edge = 1 if grown else 0
    low, high = edge, count - edge
    residual = list(residual)
    direction = [None] * count
    for i in range(low, high):
        direction[i] = residual[i] * (inverse[i] * (1.0 / theta))
    ratio_now = 1.0 / sigma
    solution = list(start) if start is not None else [None] * count
    for sweep_index in range(SWEEPS):
        for i in range(low, high):
            solution[i] = direction[i] if solution[i] is None else solution[i] + direction[i]
        low, high = low + edge, high - edge
        applied = operate_planes(faces, direction, low, high)
        for i in range(low, high):
            residual[i] = residual[i] - applied[i]
        if sweep_index + 1 < SWEEPS:
            ratio_next = 1.0 / (2.0 * sigma - ratio_now)
            turned = [None] * count
            for i in range(low, high):
                turned[i] = (ratio_next * ratio_now) * direction[i] + (
                    2.0 * ratio_next / delta
                ) * (residual[i] * inverse[i])
            direction = turned
            ratio_now = ratio_next
    return solution, residual


def split_dot(value, matrix):
    parts = []
    rest = value
    for _ in range(3):
        part = rest.astype(jnp.bfloat16)
        parts.append(part.astype(jnp.float32))
        rest = rest - parts[-1]
    rows = value.shape[0]
    stacked = jnp.concatenate(parts, axis=0).astype(jnp.bfloat16)
    product = jnp.dot(stacked, matrix, preferred_element_type=jnp.float32)
    return product[:rows] + product[rows : 2 * rows] + product[2 * rows :]


def pair_matrix(keep_low, keep_high, offset):
    source = lax.broadcasted_iota(jnp.int32, (LANES, LANES), 0)
    target = lax.broadcasted_iota(jnp.int32, (LANES, LANES), 1)
    low = (source < keep_low) & (target == offset + source // 2)
    high = (source >= LANES - keep_high) & (target == LANES // 2 + source // 2)
    return jnp.where(low | high, 1.0, 0.0).astype(jnp.bfloat16)


def pair_rows(value, hold):
    rows = value.shape[0]
    hold[0:rows, :] = value
    return hold[pl.ds(0, rows // 2, stride=2), :] + hold[pl.ds(1, rows // 2, stride=2), :]


def kernel(sizes, *refs):
    count_x, count_y, count_z = sizes
    inputs = refs[0:3]
    outs = refs[3:8]
    grown = refs[8:11]
    (pack_full, pack_edge, pack_rows, got_full, got_edge, got_rows, own_one, own_half, line_half, all_one,
     all_half, hold, solved_one, out_fine, out_one, out_two,
     out_three, out_rest, load_sem, face_send, face_recv, row_send, row_recv,
     full_send, full_recv, edge_send, edge_recv, one_send, one_recv, hop_send, hop_recv, store_sem) = refs[11:]
    kept = (out_fine, out_one, out_two, out_three, out_rest)
    stores = [pltpu.make_async_copy(kept[i], outs[i], store_sem.at[i]) for i in range(5)]
    planes, rows = inputs[0].shape[0], inputs[0].shape[1]
    x = lax.axis_index("gx")
    y = lax.axis_index("gy")
    z = lax.axis_index("gz")
    first_z = z == 0

    loads = []
    for f in range(FIELDS):
        loads.append(pltpu.make_async_copy(
            inputs[f], grown[f].at[planes : 2 * planes, 0:rows, 0:LANES], load_sem.at[f]))
        loads[-1].start()

    def other(step, turn, dy):
        return {"gx": lax.rem(x + step, count_x), "gy": y + dy, "gz": lax.rem(z + turn, count_z)}

    near = planes - WIDTH
    strip_list = [
        [(f, q) for f in range(FIELDS) for q in range(planes)
         if q > near + (1 if f == 2 else 0)],
        [(f, q) for f in range(FIELDS) for q in range(planes)],
        [(f, q) for f in range(FIELDS) for q in range(planes)
         if q < WIDTH - 1 - (1 if f == 2 else 0)],
    ]
    partners = [
        (step, turn, dy)
        for step in range(count_x)
        for turn in range(count_z)
        for dy in (0, -1, 1)
        if (step, turn, dy) != (0, 0, 0)
    ]
    barrier = pltpu.get_barrier_semaphore()
    for dy in (0, -1, 1):
        @pl.when(in_range(y + dy, count_y))
        def _():
            chosen = [p for p in partners if p[2] == dy]
            for step, turn, _dy in chosen:
                pl.semaphore_signal(
                    barrier, inc=1, device_id=other(step, turn, dy),
                    device_id_type=pl.DeviceIdType.MESH)

    for f in range(FIELDS):
        @pl.when(x == 0)
        def _():
            grown[f][0:planes, 0:rows, 0:LANES] = jnp.zeros((planes, rows, LANES), jnp.float32)

        @pl.when(x == count_x - 1)
        def _():
            grown[f][2 * planes : 3 * planes, 0:rows, 0:LANES] = jnp.zeros(
                (planes, rows, LANES), jnp.float32)

    for slot in range(3):
        for side in range(2):
            there = in_range(x + (slot - 1), count_x) & in_range(y + (2 * side - 1), count_y)

            @pl.when(jnp.logical_not(there))
            def _():
                got_full[slot, side] = jnp.zeros((rows // 2, LANES), jnp.float32)
                got_edge[slot, side] = jnp.zeros((ROWS, LANES), jnp.float32)

        if slot != 1:
            @pl.when(jnp.logical_not(in_range(x + (slot - 1), count_x)))
            def _():
                got_rows[slot] = jnp.zeros(got_rows.shape[1:], jnp.float32)

    for side in range(2):
        @pl.when(jnp.logical_not(in_range(y + (2 * side - 1), count_y)))
        def _():
            for part in range(2):
                all_half[part, side] = jnp.zeros(all_half.shape[2:], jnp.float32)

    wanted = (count_x * count_z - 1) + count_x * count_z * (
        jnp.where(y > 0, 1, 0) + jnp.where(y < count_y - 1, 1, 0))
    pl.semaphore_wait(barrier, wanted)

    def send(src, dst, send_sem, recv_sem, device, to, back):
        copy = pltpu.make_async_remote_copy(
            src_ref=src, dst_ref=dst, send_sem=send_sem, recv_sem=recv_sem,
            device_id=device, device_id_type=pl.DeviceIdType.MESH)
        if to is None:
            copy.start()
        else:
            pl.when(to)(copy.start)
        return copy, to, back

    def wait_recv(entry):
        copy, _, back = entry
        if back is None:
            copy.wait_recv()
        else:
            pl.when(back)(copy.wait_recv)

    def wait_send(entry):
        copy, to, _ = entry
        if to is None:
            copy.wait_send()
        else:
            pl.when(to)(copy.wait_send)

    faces = []
    strips_sent = []

    def send_face(f):
        for dx in (1, -1):
            to, back = in_range(x + dx, count_x), in_range(x - dx, count_x)
            low, high = 0, planes
            if f == 2:
                low, high = (1, planes) if dx == 1 else (0, planes - 1)
            base = 0 if dx == 1 else 2 * planes
            index = (dx + 1) // 2 * FIELDS + f
            faces.append((f, send(
                inputs[f].at[low:high],
                grown[f].at[base + low : base + high, 0:rows, 0:LANES],
                face_send.at[index], face_recv.at[index],
                {"gx": x + dx, "gy": y, "gz": z}, to, back)))

    send_face(0)
    for load in loads:
        load.wait()

    lane = lax.broadcasted_iota(jnp.int32, (rows, LANES), 1)
    row_index = lax.broadcasted_iota(jnp.int32, (ROWS, LANES), 0)
    low_lane = lax.rem(lane[0 : rows // 2], 2 * WIDTH) < WIDTH
    leave = (row_index < WIDTH) == jnp.logical_not(first_z)
    strips = {}
    packed = jnp.zeros((rows, LANES), jnp.float32)
    for f in range(FIELDS):
        for q in range(planes):
            k = f * planes + q
            piece = grown[f][planes + q, 0:rows, 0:LANES]
            strips[f, q] = jnp.where(first_z, piece[rows - ROWS :], piece[0:ROWS])
            moved = shift(piece, 2 * WIDTH * k, 1)
            window = lax.rem(lane - 2 * WIDTH * k + WIDTH + LANES, LANES) < 2 * WIDTH
            packed = jnp.where(window, moved, packed)
    for slot in range(3):
        for t in range(len(strip_list[slot]) // 2):
            first, second = strip_list[slot][2 * t], strip_list[slot][2 * t + 1]
            pack_rows[slot, t] = jnp.where(
                leave, strips[first], shift(strips[second], WIDTH, 0))
    top, bottom = packed[0 : rows // 2], packed[rows // 2 : rows]
    pack_full[0] = jnp.where(low_lane, shift(bottom, -WIDTH, 1), top)
    pack_full[1] = jnp.where(low_lane, top, shift(bottom, WIDTH, 1))
    pack_edge[...] = jnp.where(first_z, packed[rows - ROWS :], packed[0:ROWS])

    for dx in (1, -1, 0):
        slot = 1 - dx
        to, back = (in_range(x + dx, count_x), in_range(x - dx, count_x)) if dx else (None, None)
        tiles = len(strip_list[slot]) // 2
        strips_sent.append(send(
            pack_rows.at[slot, 0:tiles], got_rows.at[slot, 0:tiles], row_send.at[slot],
            row_recv.at[slot], {"gx": x + dx, "gy": y, "gz": 1 - z}, to, back))
        for dy in (1, -1):
            side = (1 - dy) // 2
            to = in_range(x + dx, count_x) & in_range(y + dy, count_y)
            back = in_range(x - dx, count_x) & in_range(y - dy, count_y)
            strips_sent.append(send(
                pack_full.at[side], got_full.at[slot, side], full_send.at[slot * 2 + side],
                full_recv.at[slot * 2 + side], {"gx": x + dx, "gy": y + dy, "gz": z}, to, back))
            strips_sent.append(send(
                pack_edge, got_edge.at[slot, side], edge_send.at[slot * 2 + side],
                edge_recv.at[slot * 2 + side], {"gx": x + dx, "gy": y + dy, "gz": 1 - z}, to, back))
    send_face(1)
    send_face(2)

    to_one = [pair_matrix(LANES, 0, 0), pair_matrix(LANES, 0, LANES // 2)]
    matrix_one = jnp.concatenate(to_one, axis=0)
    quarter = lax.broadcasted_iota(jnp.int32, (ROWS, LANES), 1) % (LANES // 2) < LANES // 4

    def restrict_fine(blocks, scale):
        pairs = [pair_rows(blocks[2 * q] + blocks[2 * q + 1], hold) for q in range(planes // 2)]
        return scale * split_dot(jnp.concatenate(pairs, axis=1), matrix_one)

    hopped = (0,)
    here = z * count_x + x
    line = pl.ds(z * count_x, count_x)
    blocks_all = count_x * count_z

    def spread(part, value):
        own_one[part] = value
        top, bottom = value[0:ROWS], value[ROWS : 2 * ROWS]
        own_half[part, 0] = jnp.where(quarter, shift(bottom, -(LANES // 4), 1), top)
        own_half[part, 1] = jnp.where(quarter, top, shift(bottom, LANES // 4, 1))
        all_one[part, here] = value
        for dy in (0, 1, -1):
            side = (1 - dy) // 2

            def start():
                for step, turn, _dy in [p for p in partners if p[2] == dy]:
                    if dy == 0:
                        source, target = own_one.at[part], all_one.at[part, here]
                    else:
                        source, target = own_half.at[part, side], all_half.at[part, side, here]
                    pltpu.make_async_remote_copy(
                        src_ref=source, dst_ref=target, send_sem=one_send.at[part, dy + 1],
                        recv_sem=one_recv.at[part, dy + 1], device_id=other(step, turn, dy),
                        device_id_type=pl.DeviceIdType.MESH).start()

            if dy == 0:
                start()
            else:
                pl.when(in_range(y + dy, count_y))(start)

    def remote(source, target, send_sem, recv_sem, device):
        return pltpu.make_async_remote_copy(
            src_ref=source, dst_ref=target, send_sem=send_sem, recv_sem=recv_sem,
            device_id=device, device_id_type=pl.DeviceIdType.MESH)

    def first_hop(part, value):
        own_one[part] = value
        all_one[part, here] = value
        for step in range(1, count_x):
            remote(own_one.at[part], all_one.at[part, here], hop_send.at[part],
                   hop_recv.at[part], other(step, 0, 0)).start()

    def settle_hop(part, received):
        bytes_of = all_one.at[part, 0 : count_x - 1]
        copy = remote(bytes_of, bytes_of, hop_send.at[part], hop_recv.at[part], other(1, 0, 0))
        copy.wait_recv() if received else copy.wait_send()

    def line_copies(part, dy):
        side = (1 - dy) // 2
        sems = (one_send.at[part, dy + 1], one_recv.at[part, dy + 1])
        if dy == 0:
            return [remote(all_one.at[part, line], all_one.at[part, line], *sems, other(0, 1, 0))]
        return [
            remote(line_half.at[part, side], all_half.at[part, side, line], *sems,
                   other(0, turn, dy))
            for turn in range(count_z)
        ]

    def second_hop(part):
        for from_x in range(count_x):
            value = all_one[part, z * count_x + from_x]
            top, bottom = value[0:ROWS], value[ROWS : 2 * ROWS]
            line_half[part, 0, from_x] = jnp.where(quarter, shift(bottom, -(LANES // 4), 1), top)
            line_half[part, 1, from_x] = jnp.where(quarter, top, shift(bottom, LANES // 4, 1))
        for dy in (0, 1, -1):
            def start():
                for copy in line_copies(part, dy):
                    copy.start()

            if dy == 0:
                start()
            else:
                pl.when(in_range(y + dy, count_y))(start)

    def settle(part, received):
        for dy in (0, 1, -1):
            side = (1 - dy) // 2
            if dy == 0:
                extent = count_x if part in hopped else blocks_all - 1
                bytes_of = all_one.at[part, 0:extent]
            else:
                bytes_of = all_half.at[part, side]
            copy = remote(bytes_of, bytes_of, one_send.at[part, dy + 1],
                          one_recv.at[part, dy + 1], other(1, 0, 0))
            finish = copy.wait_recv if received else copy.wait_send
            if dy == 0:
                finish()
            else:
                pl.when(in_range(y - dy if received else y + dy, count_y))(finish)

    coarse_conduct = restrict_fine(
        [grown[0][planes + q, 0:rows, 0:LANES] for q in range(planes)], 0.125)
    first_hop(0, coarse_conduct)

    for entry in strips_sent:
        wait_recv(entry)
    row_keep = (row_index < WIDTH) == first_z
    lane_edge = lax.broadcasted_iota(jnp.int32, (rows + ROWS, LANES), 1)
    lane_keep = (lane_edge < WIDTH) | (lane_edge >= LANES - WIDTH)
    low_edge = low_lane[0:ROWS]
    joined = []
    for slot in range(3):
        low, high = got_full[slot, 1], got_full[slot, 0]
        joined.append(jnp.concatenate([
            jnp.where(low_lane, low, high),
            jnp.where(low_lane, shift(low, -WIDTH, 1), shift(high, WIDTH, 1)),
            jnp.where(row_keep, jnp.where(low_edge, got_edge[slot, 1], got_edge[slot, 0]), 0.0),
        ], axis=0))
    for f in range(FIELDS):
        for slot in range(3):
            for q in range(planes):
                p = slot * planes + q
                strip = jnp.zeros((ROWS, LANES), jnp.float32)
                if (f, q) in strip_list[slot]:
                    index = strip_list[slot].index((f, q))
                    strip = got_rows[slot, index // 2]
                    if index % 2 == 1:
                        strip = shift(strip, WIDTH, 0)
                    strip = jnp.where(row_keep, strip, 0.0)
                grown[f][p, rows : rows + ROWS, 0:LANES] = strip
                grown[f][p, :, LANES : 2 * LANES] = jnp.where(
                    lane_keep, shift(joined[slot], -2 * WIDTH * (f * planes + q), 1), 0.0)

    def wait_face(f):
        for index, entry in faces:
            if index == f:
                wait_recv(entry)

    wait_face(0)
    faces_fine = face_planes([grown[0][p] for p in range(3 * planes)], True)
    wait_face(1)
    start = [grown[1][p] for p in range(3 * planes)]
    applied = operate_planes(faces_fine, start, 1, 3 * planes - 1)
    wait_face(2)
    residual = [None] * (3 * planes)
    for p in range(1, 3 * planes - 1):
        residual[p] = grown[2][p] - applied[p]
    solved, residual = smooth_planes(faces_fine, residual, start, True)
    spread(
        1, restrict_fine([residual[planes + q][0:rows, 0:LANES] for q in range(planes)], 0.25))
    settle_hop(0, True)
    second_hop(0)
    for q in range(planes):
        out_fine[q] = solved[planes + q][0:rows, 0:LANES]
    stores[0].start()

    lane_one = lax.broadcasted_iota(jnp.int32, (2 * ROWS, LANES), 1)
    lower = lane_one < LANES // 2
    empty = jnp.zeros((ROWS, LANES), jnp.float32)

    def assemble(part):
        level = []
        for from_x in range(count_x):
            blocks = [[], []]
            for from_z in range(count_z):
                block = from_z * count_x + from_x
                own = all_one[part, block]
                low, high = all_half[part, 0, block], all_half[part, 1, block]
                beside = jnp.concatenate(
                    [jnp.where(quarter, high, low),
                     jnp.where(quarter, shift(high, -(LANES // 4), 1), shift(low, LANES // 4, 1))],
                    axis=0)
                blocks[0].append(jnp.where(lower, own, shift(beside, LANES // 2, 1)))
                blocks[1].append(jnp.where(lower, shift(own, LANES // 2, 1), beside))
            for q in range(2):
                level.append(jnp.concatenate(blocks[q] + [empty], axis=0))
        return level

    def restrict(level, matrix, scale):
        length = level[0].shape[0] - ROWS
        summed = []
        for q in range(len(level) // 2):
            both = level[2 * q] + level[2 * q + 1]
            summed.append(pair_rows(both[0:length], hold))
        joined = scale * split_dot(jnp.concatenate(summed, axis=0), matrix)
        half = length // 2
        return [
            jnp.concatenate([joined[q * half : (q + 1) * half], empty], axis=0)
            for q in range(len(summed))
        ]

    matrix_two = pair_matrix(3 * LANES // 4, LANES // 4, 0)
    matrix_three = pair_matrix(3 * LANES // 8, LANES // 8, 0)
    settle(0, True)
    conduct_one = assemble(0)
    conduct_two = restrict(conduct_one, matrix_two, 0.125)
    conduct_three = restrict(conduct_two, matrix_three, 0.125)
    faces_one, faces_two, faces_three = (
        face_planes(conduct, False) for conduct in (conduct_one, conduct_two, conduct_three))

    settle(1, True)
    solved, residual = smooth_planes(faces_one, assemble(1), None, False)
    for p in range(len(solved)):
        block = solved[p][0 : 2 * rows // 2]
        solved_one[p] = jnp.where(first_z, block[0 : rows // 2], block[rows // 2 : rows])
    out_one[...] = solved_one[pl.ds(2 * x, 2), :, 0 : LANES // 2]
    stores[1].start()
    solved, residual = smooth_planes(
        faces_two, restrict(residual, matrix_two, 0.25), None, False)
    for p in range(len(solved)):
        half = rows // 4
        out_two[p] = jnp.where(first_z, solved[p][0:half], solved[p][half : 2 * half])[:, 0 : LANES // 4]
    stores[2].start()
    solved, residual = smooth_planes(
        faces_three, restrict(residual, matrix_three, 0.25), None, False)
    for p in range(len(solved)):
        half = rows // 8
        for result, out in ((solved, out_three), (residual, out_rest)):
            out[p] = jnp.where(first_z, result[p][0:half], result[p][half : 2 * half])[:, 0 : LANES // 8]

    stores[3].start()
    stores[4].start()
    for entry in strips_sent + [entry for _, entry in faces]:
        wait_send(entry)
    settle_hop(0, False)
    settle(0, False)
    settle(1, False)
    for store in stores:
        store.wait()


def hand_over(*refs):
    count = len(refs) // 2
    copies = []
    for i in range(count):
        copies.append(pltpu.make_async_copy(refs[i], refs[count + i], refs[-1].at[i]))
        copies[-1].start()
    for copy in copies:
        copy.wait()


def fits(mesh, shape):
    return (
        mesh.shape["gz"] == 2
        and mesh.shape["gx"] <= 4
        and shape[0] == WIDTH * mesh.shape["gx"]
        and shape[1] == 32 * mesh.shape["gz"]
        and shape[2] == LANES * mesh.shape["gy"]
    )


def fused(mesh, conductivity, initial_guess, right_side):
    sizes = (mesh.shape["gx"], mesh.shape["gy"], mesh.shape["gz"])
    count_x, _, count_z = sizes
    planes, rows, lanes = conductivity.shape
    f32 = jnp.float32
    shapes = [
        (planes, rows, lanes),
        (planes // 2, rows // 2, lanes // 2),
        (count_x * planes // 4, rows // 4, lanes // 4),
        (count_x * planes // 8, rows // 8, lanes // 8),
        (count_x * planes // 8, rows // 8, lanes // 8),
    ]
    blocks_all = count_x * count_z
    dma = pltpu.SemaphoreType.DMA
    scratch = [pltpu.VMEM((3 * planes, rows + ROWS, 2 * LANES), f32)] * FIELDS + [
        pltpu.VMEM((2, rows // 2, LANES), f32),
        pltpu.VMEM((ROWS, LANES), f32),
        pltpu.VMEM((3, FIELDS * planes // 2, ROWS, LANES), f32),
        pltpu.VMEM((3, 2, rows // 2, LANES), f32),
        pltpu.VMEM((3, 2, ROWS, LANES), f32),
        pltpu.VMEM((3, FIELDS * planes // 2, ROWS, LANES), f32),
        pltpu.VMEM((2, rows // 2, LANES), f32),
        pltpu.VMEM((2, 2, ROWS, LANES), f32),
        pltpu.VMEM((2, 2, count_x, ROWS, LANES), f32),
        pltpu.VMEM((2, blocks_all, rows // 2, LANES), f32),
        pltpu.VMEM((2, 2, blocks_all, ROWS, LANES), f32),
        pltpu.VMEM((rows, LANES), f32),
        pltpu.VMEM((2 * count_x, rows // 2, LANES), f32),
        *[pltpu.VMEM(shape, f32) for shape in shapes],
        dma((3,)),
        dma((6,)), dma((6,)),
        dma((3,)), dma((3,)),
        dma((6,)), dma((6,)),
        dma((6,)), dma((6,)),
        dma((2, 3)), dma((2, 3)),
        dma((2,)), dma((2,)),
        dma((5,)),
    ]
    outside = pl.BlockSpec(memory_space=pltpu.HBM)
    out_shape = [jax.ShapeDtypeStruct(shape, f32) for shape in shapes]
    results = pl.pallas_call(
        functools.partial(kernel, sizes),
        out_shape=out_shape,
        in_specs=[outside] * 3,
        out_specs=[outside] * 5,
        scratch_shapes=scratch,
        compiler_params=pltpu.CompilerParams(
            collective_id=0, has_side_effects=True, vmem_limit_bytes=56 * 2**20),
    )(conductivity, initial_guess, right_side)
    return pl.pallas_call(
        hand_over,
        out_shape=out_shape,
        in_specs=[pl.BlockSpec(memory_space=pltpu.VMEM)] * 5,
        out_specs=[outside] * 5,
        scratch_shapes=[dma((5,))],
        compiler_params=pltpu.CompilerParams(vmem_limit_bytes=56 * 2**20),
    )(*results)


def solution(mesh):
    placed = (P("gx", "gz", "gy"), P("gx", "gz", "gy"), P("gx", "gz", "gy"))

    def whole(conductivity, initial_guess, right_side):
        local = shards
        if fits(mesh, conductivity.shape):
            local = functools.partial(fused, mesh)
        return jax.shard_map(
            local,
            mesh=mesh,
            in_specs=placed,
            out_specs=(
                P("gx", "gz", "gy"),
                P("gx", "gz", "gy"),
                P(None, "gz", "gy"),
                P(None, "gz", "gy"),
                P(None, "gz", "gy"),
            ),
            check_vma=False,
        )(conductivity, initial_guess, right_side)

    return whole
```

```python
import functools

import jax
import jax.numpy as jnp
from jax import lax
from jax.experimental import pallas as pl
from jax.experimental.pallas import tpu as pltpu
from jax.sharding import PartitionSpec as P

SWEEPS = 3


lower_bound = 0.25
upper_bound = 2.0


def with_halo(block, sides, width):
    for axis, dim in sides:
        count = lax.axis_size(axis)
        forward = [(i, i + 1) for i in range(count - 1)]
        backward = [(target, source) for source, target in forward]
        low = lax.ppermute(
            lax.slice_in_dim(block, block.shape[dim] - width, None, axis=dim), axis, forward
        )
        high = lax.ppermute(lax.slice_in_dim(block, 0, width, axis=dim), axis, backward)
        block = jnp.concatenate([low, block, high], axis=dim)
    return block


def extend(bundle):
    return with_halo(bundle, (("gx", 1), ("gy", 3), ("gz", 2)), 1)


def deep_extend(bundle, merged):
    if merged:
        grown = with_halo(bundle, (("gy", 3), ("gz", 2)), 4)
        return jnp.pad(grown, ((0, 0), (4, 4), (0, 0), (0, 0)))
    return with_halo(bundle, (("gx", 1), ("gy", 3), ("gz", 2)), 4)


def neighbours(padded):
    return [
        padded[:-2, 1:-1, 1:-1],
        padded[2:, 1:-1, 1:-1],
        padded[1:-1, :-2, 1:-1],
        padded[1:-1, 2:, 1:-1],
        padded[1:-1, 1:-1, :-2],
        padded[1:-1, 1:-1, 2:],
    ]


def face_terms(conduct):
    others = neighbours(extend(conduct[None])[0])
    weights = [0.5 * (conduct + other) for other in others]
    diagonal = weights[0] + weights[1] + weights[2] + weights[3] + weights[4] + weights[5]
    return (weights, diagonal)


def operate(field, weights, diagonal):
    others = neighbours(extend(field[None])[0])
    result = diagonal * field
    for face_index in range(6):
        result = result - weights[face_index] * others[face_index]
    return result


def smooth(source, conduct):
    theta = 0.5 * (upper_bound + lower_bound)
    delta = 0.5 * (upper_bound - lower_bound)
    sigma = theta / delta
    weights, diagonal = face_terms(conduct)
    solution = jnp.zeros_like(source)
    residual = source
    direction = residual / (theta * diagonal)
    ratio_now = 1.0 / sigma
    for sweep_index in range(SWEEPS):
        solution = solution + direction
        residual = residual - operate(direction, weights, diagonal)
        if sweep_index + 1 < SWEEPS:
            ratio_next = 1.0 / (2.0 * sigma - ratio_now)
            direction = (
                ratio_next * ratio_now * direction + 2.0 * ratio_next / delta * residual / diagonal
            )
            ratio_now = ratio_next
    return (solution, residual)


def local_operate(field, weights, diagonal):
    others = neighbours(jnp.pad(field, 1))
    result = diagonal * field
    for face_index in range(6):
        result = result - weights[face_index] * others[face_index]
    return result


def smooth_deep(source, start, conduct, merged):
    theta = 0.5 * (upper_bound + lower_bound)
    delta = 0.5 * (upper_bound - lower_bound)
    sigma = theta / delta
    members = [conduct, source, jnp.ones_like(source)]
    if start is not None:
        members.append(start)
    grown = deep_extend(jnp.stack(members), merged)
    padded_conduct = grown[0]
    padded_source = grown[1]
    inside = grown[2]
    others = neighbours(jnp.pad(padded_conduct, 1))
    weights = [0.5 * (padded_conduct + other) for other in others]
    diagonal = weights[0] + weights[1] + weights[2] + weights[3] + weights[4] + weights[5]
    safe_diagonal = jnp.where(inside > 0.5, diagonal, 1.0)
    if start is None:
        solution = jnp.zeros_like(padded_source)
        residual = padded_source
    else:
        solution = grown[3]
        residual = padded_source - local_operate(solution, weights, diagonal)
    direction = inside * (residual / (theta * safe_diagonal))
    ratio_now = 1.0 / sigma
    for sweep_index in range(SWEEPS):
        solution = solution + direction
        residual = residual - local_operate(direction, weights, diagonal)
        if sweep_index + 1 < SWEEPS:
            ratio_next = 1.0 / (2.0 * sigma - ratio_now)
            direction = inside * (
                ratio_next * ratio_now * direction
                + 2.0 * ratio_next / delta * residual / safe_diagonal
            )
            ratio_now = ratio_next
    return (solution[4:-4, 4:-4, 4:-4], residual[4:-4, 4:-4, 4:-4])


def level_smooth(source, start, conduct, merged):
    extents = source.shape[1:] if merged else source.shape
    if min(extents) >= 4:
        return smooth_deep(source, start, conduct, merged)
    return smooth(source, conduct)


def coarse_sum(field):
    first, second, third = field.shape
    blocks = field.reshape(first // 2, 2, second // 2, 2, third // 2, 2)
    return jnp.sum(blocks, axis=(1, 3, 5))


def shards(conductivity, initial_guess, right_side):
    fine_solution, residual_zero = level_smooth(right_side, initial_guess, conductivity, False)
    conduct_one = 0.125 * coarse_sum(conductivity)
    level_one_solution, residual_one = level_smooth(
        0.25 * coarse_sum(residual_zero), None, conduct_one, False
    )
    conduct_two = 0.125 * coarse_sum(conduct_one)
    source_two = 0.25 * coarse_sum(residual_one)
    bundle = jnp.stack([source_two, conduct_two])
    bundle = lax.all_gather(bundle, "gx", axis=1, tiled=True)
    level_two_solution, residual_two = level_smooth(bundle[0], None, bundle[1], True)
    conduct_three = 0.125 * coarse_sum(bundle[1])
    level_three_solution, level_three_residual = level_smooth(
        0.25 * coarse_sum(residual_two), None, conduct_three, True
    )
    return (
        fine_solution,
        level_one_solution,
        level_two_solution,
        level_three_solution,
        level_three_residual,
    )


FIELDS = 3
WIDTH = 4
ROWS = 8
LANES = 128


def in_range(index, count):
    return (index >= 0) & (index < count)


def shift(value, amount, axis):
    return pltpu.roll(value, amount % value.shape[axis], axis)


def face_planes(conduct, grown):
    count = len(conduct)
    edge = 1 if grown else 0
    weight_x = [None] * (count + 1)
    for i in range(1, count):
        weight_x[i] = 0.5 * (conduct[i - 1] + conduct[i])
    if not grown:
        weight_x[0] = 0.5 * conduct[0]
        weight_x[count] = 0.5 * conduct[count - 1]
    weight_z = [None] * count
    weight_y = [None] * count
    inverse = [None] * count
    for i in range(edge, count - edge):
        weight_z[i] = 0.5 * (conduct[i] + shift(conduct[i], -1, 0))
        weight_y[i] = 0.5 * (conduct[i] + shift(conduct[i], -1, 1))
        diagonal = weight_x[i] + weight_x[i + 1]
        diagonal = diagonal + (weight_z[i] + shift(weight_z[i], 1, 0))
        diagonal = diagonal + (weight_y[i] + shift(weight_y[i], 1, 1))
        inside = conduct[i] > 0.0
        inverse[i] = jnp.where(inside, 1.0 / jnp.where(inside, diagonal, 1.0), 0.0)
    return weight_x, weight_y, weight_z, inverse


def operate_planes(faces, field, low, high):
    weight_x, weight_y, weight_z, _ = faces
    count = len(field)
    flux_x = [None] * (count + 1)
    for i in range(low, high + 1):
        if i == 0:
            flux_x[i] = weight_x[i] * field[i]
        elif i == count:
            flux_x[i] = -(weight_x[i] * field[i - 1])
        else:
            flux_x[i] = weight_x[i] * (field[i] - field[i - 1])
    result = [None] * count
    for i in range(low, high):
        flux_z = weight_z[i] * (field[i] - shift(field[i], -1, 0))
        flux_y = weight_y[i] * (field[i] - shift(field[i], -1, 1))
        result[i] = (
            (flux_x[i] - flux_x[i + 1])
            + (flux_z - shift(flux_z, 1, 0))
            + (flux_y - shift(flux_y, 1, 1))
        )
    return result


def coarse_faces(conduct):
    count, length = len(conduct), conduct[0].shape[0]
    row = lax.broadcasted_iota(jnp.int32, conduct[0].shape, 0)
    first, last = row == 0, row == length - 1
    weights, diagonals, inverses = [], [], []
    for i in range(count):
        own = conduct[i]
        half = 0.5 * own
        below = 0.5 * (own + conduct[i - 1]) if i > 0 else half
        above = 0.5 * (own + conduct[i + 1]) if i + 1 < count else half
        before = jnp.where(first, half, 0.5 * (own + shift(own, 1, 0)))
        after = jnp.where(last, half, 0.5 * (own + shift(own, -1, 0)))
        left = 0.5 * (own + shift(own, 1, 1))
        right = 0.5 * (own + shift(own, -1, 1))
        diagonal = (below + above) + (before + after) + (left + right)
        inside = own > 0.0
        diagonals.append(diagonal)
        inverses.append(jnp.where(inside, 1.0 / jnp.where(inside, diagonal, 1.0), 0.0))
        before = jnp.where(first, 0.0, before)
        after = jnp.where(last, 0.0, after)
        weights.append((below, above, before, after, left, right))
    return weights, diagonals, None, inverses


def operate_coarse(faces, field):
    weights, diagonals = faces[0], faces[1]
    count = len(field)
    result = []
    for i in range(count):
        below, above, before, after, left, right = weights[i]
        own = field[i]
        value = diagonals[i] * own
        if i > 0:
            value = value - below * field[i - 1]
        if i + 1 < count:
            value = value - above * field[i + 1]
        rolled = before * shift(own, 1, 0) + after * shift(own, -1, 0)
        rolled = rolled + (left * shift(own, 1, 1) + right * shift(own, -1, 1))
        result.append(value - rolled)
    return result


def smooth_planes(faces, residual, start, grown):
    theta = 0.5 * (upper_bound + lower_bound)
    delta = 0.5 * (upper_bound - lower_bound)
    sigma = theta / delta
    inverse = faces[3]
    count = len(residual)
    edge = 1 if grown else 0
    low, high = edge, count - edge
    residual = list(residual)
    direction = [None] * count
    for i in range(low, high):
        direction[i] = residual[i] * (inverse[i] * (1.0 / theta))
    ratio_now = 1.0 / sigma
    solution = list(start) if start is not None else [None] * count
    for sweep_index in range(SWEEPS):
        for i in range(low, high):
            solution[i] = direction[i] if solution[i] is None else solution[i] + direction[i]
        low, high = low + edge, high - edge
        if grown:
            applied = operate_planes(faces, direction, low, high)
        else:
            applied = operate_coarse(faces, direction)
        for i in range(low, high):
            residual[i] = residual[i] - applied[i]
        if sweep_index + 1 < SWEEPS:
            ratio_next = 1.0 / (2.0 * sigma - ratio_now)
            turned = [None] * count
            for i in range(low, high):
                turned[i] = (ratio_next * ratio_now) * direction[i] + (
                    2.0 * ratio_next / delta
                ) * (residual[i] * inverse[i])
            direction = turned
            ratio_now = ratio_next
    return solution, residual


def split_dot(value, matrix):
    parts = []
    rest = value
    for _ in range(3):
        part = rest.astype(jnp.bfloat16)
        parts.append(part.astype(jnp.float32))
        rest = rest - parts[-1]
    rows = value.shape[0]
    stacked = jnp.concatenate(parts, axis=0).astype(jnp.bfloat16)
    product = jnp.dot(stacked, matrix, preferred_element_type=jnp.float32)
    return product[:rows] + product[rows : 2 * rows] + product[2 * rows :]


def pair_matrix(keep_low, keep_high, offset):
    source = lax.broadcasted_iota(jnp.int32, (LANES, LANES), 0)
    target = lax.broadcasted_iota(jnp.int32, (LANES, LANES), 1)
    low = (source < keep_low) & (target == offset + (source >> 1))
    high = (source >= LANES - keep_high) & (target == LANES // 2 + (source >> 1))
    return jnp.where(low | high, 1.0, 0.0).astype(jnp.bfloat16)


def pair_rows(value, hold, q):
    rows = value.shape[0]
    hold[q, 0:rows, :] = value
    even = hold[q, pl.ds(0, rows // 2, stride=2), :]
    return even + hold[q, pl.ds(1, rows // 2, stride=2), :]


def kernel(sizes, *refs):
    count_x, count_y, count_z = sizes
    inputs = refs[0:3]
    outs = refs[3:8]
    grown = refs[8:11]
    (pack_full, pack_edge, pack_rows, got_full, got_edge, got_rows, own_one, own_half, line_half, all_one,
     all_half, hold, solved_one, out_fine, out_one, out_two,
     out_three, out_rest, load_sem, face_send, face_recv, row_send, row_recv,
     full_send, full_recv, edge_send, edge_recv, one_send, one_recv, hop_send, hop_recv, store_sem) = refs[11:]
    kept = (out_fine, out_one, out_two, out_three, out_rest)
    stores = [pltpu.make_async_copy(kept[i], outs[i], store_sem.at[i]) for i in range(5)]
    planes, rows = inputs[0].shape[0], inputs[0].shape[1]
    x = lax.axis_index("gx")
    y = lax.axis_index("gy")
    z = lax.axis_index("gz")
    first_z = z == 0

    loads = []
    for f in range(FIELDS):
        loads.append(pltpu.make_async_copy(
            inputs[f], grown[f].at[planes : 2 * planes, 0:rows, 0:LANES], load_sem.at[f]))
        loads[-1].start()

    def other(step, turn, dy):
        return {"gx": lax.rem(x + step, count_x), "gy": y + dy, "gz": lax.rem(z + turn, count_z)}

    near = planes - WIDTH
    strip_list = [
        [(f, q) for f in range(FIELDS) for q in range(planes)
         if q > near + (1 if f == 2 else 0)],
        [(f, q) for f in range(FIELDS) for q in range(planes)],
        [(f, q) for f in range(FIELDS) for q in range(planes)
         if q < WIDTH - 1 - (1 if f == 2 else 0)],
    ]
    partners = [
        (step, turn, dy)
        for step in range(count_x)
        for turn in range(count_z)
        for dy in (0, -1, 1)
        if (step, turn, dy) != (0, 0, 0)
    ]
    barrier = pltpu.get_barrier_semaphore()
    for dy in (0, -1, 1):
        @pl.when(in_range(y + dy, count_y))
        def _():
            chosen = [p for p in partners if p[2] == dy]
            for step, turn, _dy in chosen:
                pl.semaphore_signal(
                    barrier, inc=1, device_id=other(step, turn, dy),
                    device_id_type=pl.DeviceIdType.MESH)

    for f in range(FIELDS):
        @pl.when(x == 0)
        def _():
            grown[f][0:planes, 0:rows, 0:LANES] = jnp.zeros((planes, rows, LANES), jnp.float32)

        @pl.when(x == count_x - 1)
        def _():
            grown[f][2 * planes : 3 * planes, 0:rows, 0:LANES] = jnp.zeros(
                (planes, rows, LANES), jnp.float32)

    for slot in range(3):
        for side in range(2):
            there = in_range(x + (slot - 1), count_x) & in_range(y + (2 * side - 1), count_y)

            @pl.when(jnp.logical_not(there))
            def _():
                got_full[slot, side] = jnp.zeros((rows // 2, LANES), jnp.float32)
                got_edge[slot, side] = jnp.zeros((ROWS, LANES), jnp.float32)

        if slot != 1:
            @pl.when(jnp.logical_not(in_range(x + (slot - 1), count_x)))
            def _():
                got_rows[slot] = jnp.zeros(got_rows.shape[1:], jnp.float32)

    for side in range(2):
        @pl.when(jnp.logical_not(in_range(y + (2 * side - 1), count_y)))
        def _():
            for part in range(2):
                all_half[part, side] = jnp.zeros(all_half.shape[2:], jnp.float32)

    for load in loads:
        load.wait()

    lane = lax.broadcasted_iota(jnp.int32, (rows, LANES), 1)
    row_index = lax.broadcasted_iota(jnp.int32, (ROWS, LANES), 0)
    low_lane = (lane[0 : rows // 2] & WIDTH) == 0
    leave = (row_index < WIDTH) == jnp.logical_not(first_z)
    strips = {}
    packed = jnp.zeros((rows, LANES), jnp.float32)
    for f in range(FIELDS):
        for q in range(planes):
            k = f * planes + q
            piece = grown[f][planes + q, 0:rows, 0:LANES]
            strips[f, q] = jnp.where(first_z, piece[rows - ROWS :], piece[0:ROWS])
            moved = shift(piece, 2 * WIDTH * k, 1)
            window = ((lane + (LANES + WIDTH - 2 * WIDTH * k)) & (LANES - 1)) < 2 * WIDTH
            packed = jnp.where(window, moved, packed)
    for slot in range(3):
        for t in range(len(strip_list[slot]) // 2):
            first, second = strip_list[slot][2 * t], strip_list[slot][2 * t + 1]
            pack_rows[slot, t] = jnp.where(
                leave, strips[first], shift(strips[second], WIDTH, 0))
    top, bottom = packed[0 : rows // 2], packed[rows // 2 : rows]
    pack_full[0] = jnp.where(low_lane, shift(bottom, -WIDTH, 1), top)
    pack_full[1] = jnp.where(low_lane, top, shift(bottom, WIDTH, 1))
    pack_edge[...] = jnp.where(first_z, packed[rows - ROWS :], packed[0:ROWS])

    wanted = (count_x * count_z - 1) + count_x * count_z * (
        jnp.where(y > 0, 1, 0) + jnp.where(y < count_y - 1, 1, 0))
    pl.semaphore_wait(barrier, wanted)

    def send(src, dst, send_sem, recv_sem, device, to, back):
        copy = pltpu.make_async_remote_copy(
            src_ref=src, dst_ref=dst, send_sem=send_sem, recv_sem=recv_sem,
            device_id=device, device_id_type=pl.DeviceIdType.MESH)
        if to is None:
            copy.start()
        else:
            pl.when(to)(copy.start)
        return copy, to, back

    def wait_recv(entry):
        copy, _, back = entry
        if back is None:
            copy.wait_recv()
        else:
            pl.when(back)(copy.wait_recv)

    def wait_send(entry):
        copy, to, _ = entry
        if to is None:
            copy.wait_send()
        else:
            pl.when(to)(copy.wait_send)

    faces = []
    strips_sent = []

    def send_face(f):
        for dx in (1, -1):
            to, back = in_range(x + dx, count_x), in_range(x - dx, count_x)
            low, high = 0, planes
            if f == 2:
                low, high = (1, planes) if dx == 1 else (0, planes - 1)
            base = 0 if dx == 1 else 2 * planes
            index = (dx + 1) // 2 * FIELDS + f
            faces.append((f, send(
                grown[f].at[planes + low : planes + high, 0:rows, 0:LANES],
                grown[f].at[base + low : base + high, 0:rows, 0:LANES],
                face_send.at[index], face_recv.at[index],
                {"gx": x + dx, "gy": y, "gz": z}, to, back)))

    send_face(0)
    for dx in (1, -1, 0):
        slot = 1 - dx
        to, back = (in_range(x + dx, count_x), in_range(x - dx, count_x)) if dx else (None, None)
        tiles = len(strip_list[slot]) // 2
        strips_sent.append(send(
            pack_rows.at[slot, 0:tiles], got_rows.at[slot, 0:tiles], row_send.at[slot],
            row_recv.at[slot], {"gx": x + dx, "gy": y, "gz": 1 - z}, to, back))
        for dy in (1, -1):
            side = (1 - dy) // 2
            to = in_range(x + dx, count_x) & in_range(y + dy, count_y)
            back = in_range(x - dx, count_x) & in_range(y - dy, count_y)
            strips_sent.append(send(
                pack_full.at[side], got_full.at[slot, side], full_send.at[slot * 2 + side],
                full_recv.at[slot * 2 + side], {"gx": x + dx, "gy": y + dy, "gz": z}, to, back))
            strips_sent.append(send(
                pack_edge, got_edge.at[slot, side], edge_send.at[slot * 2 + side],
                edge_recv.at[slot * 2 + side], {"gx": x + dx, "gy": y + dy, "gz": 1 - z}, to, back))
    send_face(1)
    send_face(2)

    to_one = [pair_matrix(LANES, 0, 0), pair_matrix(LANES, 0, LANES // 2)]
    matrix_one = jnp.concatenate(to_one, axis=0)
    quarter = (lax.broadcasted_iota(jnp.int32, (ROWS, LANES), 1) & (LANES // 4)) == 0

    def restrict_fine(blocks, scale):
        pairs = [pair_rows(blocks[2 * q] + blocks[2 * q + 1], hold, q) for q in range(planes // 2)]
        return scale * split_dot(jnp.concatenate(pairs, axis=1), matrix_one)

    hopped = (0,)
    here = z * count_x + x
    line = pl.ds(z * count_x, count_x)
    blocks_all = count_x * count_z

    def spread(part, value):
        own_one[part] = value
        top, bottom = value[0:ROWS], value[ROWS : 2 * ROWS]
        own_half[part, 0] = jnp.where(quarter, shift(bottom, -(LANES // 4), 1), top)
        own_half[part, 1] = jnp.where(quarter, top, shift(bottom, LANES // 4, 1))
        all_one[part, here] = value
        for dy in (0, 1, -1):
            side = (1 - dy) // 2

            def start():
                for step, turn, _dy in [p for p in partners if p[2] == dy]:
                    if dy == 0:
                        source, target = own_one.at[part], all_one.at[part, here]
                    else:
                        source, target = own_half.at[part, side], all_half.at[part, side, here]
                    pltpu.make_async_remote_copy(
                        src_ref=source, dst_ref=target, send_sem=one_send.at[part, dy + 1],
                        recv_sem=one_recv.at[part, dy + 1], device_id=other(step, turn, dy),
                        device_id_type=pl.DeviceIdType.MESH).start()

            if dy == 0:
                start()
            else:
                pl.when(in_range(y + dy, count_y))(start)

    def remote(source, target, send_sem, recv_sem, device):
        return pltpu.make_async_remote_copy(
            src_ref=source, dst_ref=target, send_sem=send_sem, recv_sem=recv_sem,
            device_id=device, device_id_type=pl.DeviceIdType.MESH)

    def first_hop(part, value):
        own_one[part] = value
        all_one[part, here] = value
        for step in range(1, count_x):
            remote(own_one.at[part], all_one.at[part, here], hop_send.at[part],
                   hop_recv.at[part], other(step, 0, 0)).start()

    def settle_hop(part, received):
        bytes_of = all_one.at[part, 0 : count_x - 1]
        copy = remote(bytes_of, bytes_of, hop_send.at[part], hop_recv.at[part], other(1, 0, 0))
        copy.wait_recv() if received else copy.wait_send()

    def line_copies(part, dy):
        side = (1 - dy) // 2
        sems = (one_send.at[part, dy + 1], one_recv.at[part, dy + 1])
        if dy == 0:
            return [remote(all_one.at[part, line], all_one.at[part, line], *sems, other(0, 1, 0))]
        return [
            remote(line_half.at[part, side], all_half.at[part, side, line], *sems,
                   other(0, turn, dy))
            for turn in range(count_z)
        ]

    def second_hop(part):
        for from_x in range(count_x):
            value = all_one[part, z * count_x + from_x]
            top, bottom = value[0:ROWS], value[ROWS : 2 * ROWS]
            line_half[part, 0, from_x] = jnp.where(quarter, shift(bottom, -(LANES // 4), 1), top)
            line_half[part, 1, from_x] = jnp.where(quarter, top, shift(bottom, LANES // 4, 1))
        for dy in (0, 1, -1):
            def start():
                for copy in line_copies(part, dy):
                    copy.start()

            if dy == 0:
                start()
            else:
                pl.when(in_range(y + dy, count_y))(start)

    def settle(part, received):
        for dy in (0, 1, -1):
            side = (1 - dy) // 2
            if dy == 0:
                extent = count_x if part in hopped else blocks_all - 1
                bytes_of = all_one.at[part, 0:extent]
            else:
                bytes_of = all_half.at[part, side]
            copy = remote(bytes_of, bytes_of, one_send.at[part, dy + 1],
                          one_recv.at[part, dy + 1], other(1, 0, 0))
            finish = copy.wait_recv if received else copy.wait_send
            if dy == 0:
                finish()
            else:
                pl.when(in_range(y - dy if received else y + dy, count_y))(finish)

    coarse_conduct = restrict_fine(
        [grown[0][planes + q, 0:rows, 0:LANES] for q in range(planes)], 0.125)
    first_hop(0, coarse_conduct)

    for entry in strips_sent:
        wait_recv(entry)
    row_keep = (row_index < WIDTH) == first_z
    lane_edge = lax.broadcasted_iota(jnp.int32, (rows + ROWS, LANES), 1)
    lane_keep = (lane_edge < WIDTH) | (lane_edge >= LANES - WIDTH)
    low_edge = low_lane[0:ROWS]
    joined = []
    for slot in range(3):
        low, high = got_full[slot, 1], got_full[slot, 0]
        joined.append(jnp.concatenate([
            jnp.where(low_lane, low, high),
            jnp.where(low_lane, shift(low, -WIDTH, 1), shift(high, WIDTH, 1)),
            jnp.where(row_keep, jnp.where(low_edge, got_edge[slot, 1], got_edge[slot, 0]), 0.0),
        ], axis=0))
    for f in range(FIELDS):
        for slot in range(3):
            for q in range(planes):
                p = slot * planes + q
                strip = jnp.zeros((ROWS, LANES), jnp.float32)
                if (f, q) in strip_list[slot]:
                    index = strip_list[slot].index((f, q))
                    strip = got_rows[slot, index // 2]
                    if index % 2 == 1:
                        strip = shift(strip, WIDTH, 0)
                    strip = jnp.where(row_keep, strip, 0.0)
                grown[f][p, rows : rows + ROWS, 0:LANES] = strip
                grown[f][p, :, LANES : 2 * LANES] = jnp.where(
                    lane_keep, shift(joined[slot], -2 * WIDTH * (f * planes + q), 1), 0.0)

    def wait_face(f):
        for index, entry in faces:
            if index == f:
                wait_recv(entry)

    wait_face(0)
    faces_fine = face_planes([grown[0][p] for p in range(3 * planes)], True)
    wait_face(1)
    start = [grown[1][p] for p in range(3 * planes)]
    applied = operate_planes(faces_fine, start, 1, 3 * planes - 1)
    wait_face(2)
    residual = [None] * (3 * planes)
    for p in range(1, 3 * planes - 1):
        residual[p] = grown[2][p] - applied[p]
    solved, residual = smooth_planes(faces_fine, residual, start, True)
    spread(
        1, restrict_fine([residual[planes + q][0:rows, 0:LANES] for q in range(planes)], 0.25))
    settle_hop(0, True)
    second_hop(0)
    for q in range(planes):
        out_fine[q] = solved[planes + q][0:rows, 0:LANES]
    stores[0].start()

    lane_one = lax.broadcasted_iota(jnp.int32, (2 * ROWS, LANES), 1)
    lower = lane_one < LANES // 2

    def assemble(part):
        level = []
        for from_x in range(count_x):
            blocks = [[], []]
            for from_z in range(count_z):
                block = from_z * count_x + from_x
                own = all_one[part, block]
                low, high = all_half[part, 0, block], all_half[part, 1, block]
                beside = jnp.concatenate(
                    [jnp.where(quarter, high, low),
                     jnp.where(quarter, shift(high, -(LANES // 4), 1), shift(low, LANES // 4, 1))],
                    axis=0)
                blocks[0].append(jnp.where(lower, own, shift(beside, LANES // 2, 1)))
                blocks[1].append(jnp.where(lower, shift(own, LANES // 2, 1), beside))
            for q in range(2):
                level.append(jnp.concatenate(blocks[q], axis=0))
        return level

    def restrict(level, matrix, scale):
        length = level[0].shape[0]
        summed = []
        for q in range(len(level) // 2):
            both = level[2 * q] + level[2 * q + 1]
            summed.append(pair_rows(both, hold, q))
        joined = scale * split_dot(jnp.concatenate(summed, axis=0), matrix)
        half = length // 2
        return [joined[q * half : (q + 1) * half] for q in range(len(summed))]

    matrix_two = pair_matrix(3 * LANES // 4, LANES // 4, 0)
    matrix_three = pair_matrix(3 * LANES // 8, LANES // 8, 0)
    settle(0, True)
    conduct_one = assemble(0)
    conduct_two = restrict(conduct_one, matrix_two, 0.125)
    conduct_three = restrict(conduct_two, matrix_three, 0.125)
    faces_one, faces_two, faces_three = (
        coarse_faces(conduct) for conduct in (conduct_one, conduct_two, conduct_three))

    settle(1, True)
    solved, residual = smooth_planes(faces_one, assemble(1), None, False)
    for p in range(len(solved)):
        block = solved[p][0 : 2 * rows // 2]
        solved_one[p] = jnp.where(first_z, block[0 : rows // 2], block[rows // 2 : rows])
    out_one[...] = solved_one[pl.ds(2 * x, 2), :, 0 : LANES // 2]
    stores[1].start()
    solved, residual = smooth_planes(
        faces_two, restrict(residual, matrix_two, 0.25), None, False)
    for p in range(len(solved)):
        half = rows // 4
        out_two[p] = jnp.where(first_z, solved[p][0:half], solved[p][half : 2 * half])[:, 0 : LANES // 4]
    stores[2].start()
    solved, residual = smooth_planes(
        faces_three, restrict(residual, matrix_three, 0.25), None, False)
    for p in range(len(solved)):
        half = rows // 8
        for result, out in ((solved, out_three), (residual, out_rest)):
            out[p] = jnp.where(first_z, result[p][0:half], result[p][half : 2 * half])[:, 0 : LANES // 8]

    stores[3].start()
    stores[4].start()
    for entry in strips_sent + [entry for _, entry in faces]:
        wait_send(entry)
    settle_hop(0, False)
    settle(0, False)
    settle(1, False)
    for store in stores:
        store.wait()


def hand_over(*refs):
    count = len(refs) // 2
    copies = []
    for i in range(count):
        copies.append(pltpu.make_async_copy(refs[i], refs[count + i], refs[-1].at[i]))
        copies[-1].start()
    for copy in copies:
        copy.wait()


def fits(mesh, shape):
    return (
        mesh.shape["gz"] == 2
        and mesh.shape["gx"] <= 4
        and shape[0] == WIDTH * mesh.shape["gx"]
        and shape[1] == 32 * mesh.shape["gz"]
        and shape[2] == LANES * mesh.shape["gy"]
    )


def fused(mesh, conductivity, initial_guess, right_side):
    sizes = (mesh.shape["gx"], mesh.shape["gy"], mesh.shape["gz"])
    count_x, _, count_z = sizes
    planes, rows, lanes = conductivity.shape
    f32 = jnp.float32
    shapes = [
        (planes, rows, lanes),
        (planes // 2, rows // 2, lanes // 2),
        (count_x * planes // 4, rows // 4, lanes // 4),
        (count_x * planes // 8, rows // 8, lanes // 8),
        (count_x * planes // 8, rows // 8, lanes // 8),
    ]
    blocks_all = count_x * count_z
    dma = pltpu.SemaphoreType.DMA
    scratch = [pltpu.VMEM((3 * planes, rows + ROWS, 2 * LANES), f32)] * FIELDS + [
        pltpu.VMEM((2, rows // 2, LANES), f32),
        pltpu.VMEM((ROWS, LANES), f32),
        pltpu.VMEM((3, FIELDS * planes // 2, ROWS, LANES), f32),
        pltpu.VMEM((3, 2, rows // 2, LANES), f32),
        pltpu.VMEM((3, 2, ROWS, LANES), f32),
        pltpu.VMEM((3, FIELDS * planes // 2, ROWS, LANES), f32),
        pltpu.VMEM((2, rows // 2, LANES), f32),
        pltpu.VMEM((2, 2, ROWS, LANES), f32),
        pltpu.VMEM((2, 2, count_x, ROWS, LANES), f32),
        pltpu.VMEM((2, blocks_all, rows // 2, LANES), f32),
        pltpu.VMEM((2, 2, blocks_all, ROWS, LANES), f32),
        pltpu.VMEM((count_x, rows, LANES), f32),
        pltpu.VMEM((2 * count_x, rows // 2, LANES), f32),
        *[pltpu.VMEM(shape, f32) for shape in shapes],
        dma((3,)),
        dma((6,)), dma((6,)),
        dma((3,)), dma((3,)),
        dma((6,)), dma((6,)),
        dma((6,)), dma((6,)),
        dma((2, 3)), dma((2, 3)),
        dma((2,)), dma((2,)),
        dma((5,)),
    ]
    outside = pl.BlockSpec(memory_space=pltpu.HBM)
    out_shape = [jax.ShapeDtypeStruct(shape, f32) for shape in shapes]
    results = pl.pallas_call(
        functools.partial(kernel, sizes),
        out_shape=out_shape,
        in_specs=[outside] * 3,
        out_specs=[outside] * 5,
        scratch_shapes=scratch,
        compiler_params=pltpu.CompilerParams(
            collective_id=0, has_side_effects=True, vmem_limit_bytes=56 * 2**20),
    )(conductivity, initial_guess, right_side)
    return pl.pallas_call(
        hand_over,
        out_shape=out_shape,
        in_specs=[pl.BlockSpec(memory_space=pltpu.VMEM)] * 5,
        out_specs=[outside] * 5,
        scratch_shapes=[dma((5,))],
        compiler_params=pltpu.CompilerParams(vmem_limit_bytes=56 * 2**20),
    )(*results)


def solution(mesh):
    placed = (P("gx", "gz", "gy"), P("gx", "gz", "gy"), P("gx", "gz", "gy"))

    def whole(conductivity, initial_guess, right_side):
        local = shards
        if fits(mesh, conductivity.shape):
            local = functools.partial(fused, mesh)
        return jax.shard_map(
            local,
            mesh=mesh,
            in_specs=placed,
            out_specs=(
                P("gx", "gz", "gy"),
                P("gx", "gz", "gy"),
                P(None, "gz", "gy"),
                P(None, "gz", "gy"),
                P(None, "gz", "gy"),
            ),
            check_vma=False,
        )(conductivity, initial_guess, right_side)

    return whole
```

```python
import functools

import jax
import jax.numpy as jnp
from jax import lax
from jax.experimental import pallas as pl
from jax.experimental.pallas import tpu as pltpu
from jax.sharding import PartitionSpec as P

SWEEPS = 3


lower_bound = 0.25
upper_bound = 2.0


def with_halo(block, sides, width):
    for axis, dim in sides:
        count = lax.axis_size(axis)
        forward = [(i, i + 1) for i in range(count - 1)]
        backward = [(target, source) for source, target in forward]
        low = lax.ppermute(
            lax.slice_in_dim(block, block.shape[dim] - width, None, axis=dim), axis, forward
        )
        high = lax.ppermute(lax.slice_in_dim(block, 0, width, axis=dim), axis, backward)
        block = jnp.concatenate([low, block, high], axis=dim)
    return block


def extend(bundle):
    return with_halo(bundle, (("gx", 1), ("gy", 3), ("gz", 2)), 1)


def deep_extend(bundle, merged):
    if merged:
        grown = with_halo(bundle, (("gy", 3), ("gz", 2)), 4)
        return jnp.pad(grown, ((0, 0), (4, 4), (0, 0), (0, 0)))
    return with_halo(bundle, (("gx", 1), ("gy", 3), ("gz", 2)), 4)


def neighbours(padded):
    return [
        padded[:-2, 1:-1, 1:-1],
        padded[2:, 1:-1, 1:-1],
        padded[1:-1, :-2, 1:-1],
        padded[1:-1, 2:, 1:-1],
        padded[1:-1, 1:-1, :-2],
        padded[1:-1, 1:-1, 2:],
    ]


def face_terms(conduct):
    others = neighbours(extend(conduct[None])[0])
    weights = [0.5 * (conduct + other) for other in others]
    diagonal = weights[0] + weights[1] + weights[2] + weights[3] + weights[4] + weights[5]
    return (weights, diagonal)


def operate(field, weights, diagonal):
    others = neighbours(extend(field[None])[0])
    result = diagonal * field
    for face_index in range(6):
        result = result - weights[face_index] * others[face_index]
    return result


def smooth(source, conduct):
    theta = 0.5 * (upper_bound + lower_bound)
    delta = 0.5 * (upper_bound - lower_bound)
    sigma = theta / delta
    weights, diagonal = face_terms(conduct)
    solution = jnp.zeros_like(source)
    residual = source
    direction = residual / (theta * diagonal)
    ratio_now = 1.0 / sigma
    for sweep_index in range(SWEEPS):
        solution = solution + direction
        residual = residual - operate(direction, weights, diagonal)
        if sweep_index + 1 < SWEEPS:
            ratio_next = 1.0 / (2.0 * sigma - ratio_now)
            direction = (
                ratio_next * ratio_now * direction + 2.0 * ratio_next / delta * residual / diagonal
            )
            ratio_now = ratio_next
    return (solution, residual)


def local_operate(field, weights, diagonal):
    others = neighbours(jnp.pad(field, 1))
    result = diagonal * field
    for face_index in range(6):
        result = result - weights[face_index] * others[face_index]
    return result


def smooth_deep(source, start, conduct, merged):
    theta = 0.5 * (upper_bound + lower_bound)
    delta = 0.5 * (upper_bound - lower_bound)
    sigma = theta / delta
    members = [conduct, source, jnp.ones_like(source)]
    if start is not None:
        members.append(start)
    grown = deep_extend(jnp.stack(members), merged)
    padded_conduct = grown[0]
    padded_source = grown[1]
    inside = grown[2]
    others = neighbours(jnp.pad(padded_conduct, 1))
    weights = [0.5 * (padded_conduct + other) for other in others]
    diagonal = weights[0] + weights[1] + weights[2] + weights[3] + weights[4] + weights[5]
    safe_diagonal = jnp.where(inside > 0.5, diagonal, 1.0)
    if start is None:
        solution = jnp.zeros_like(padded_source)
        residual = padded_source
    else:
        solution = grown[3]
        residual = padded_source - local_operate(solution, weights, diagonal)
    direction = inside * (residual / (theta * safe_diagonal))
    ratio_now = 1.0 / sigma
    for sweep_index in range(SWEEPS):
        solution = solution + direction
        residual = residual - local_operate(direction, weights, diagonal)
        if sweep_index + 1 < SWEEPS:
            ratio_next = 1.0 / (2.0 * sigma - ratio_now)
            direction = inside * (
                ratio_next * ratio_now * direction
                + 2.0 * ratio_next / delta * residual / safe_diagonal
            )
            ratio_now = ratio_next
    return (solution[4:-4, 4:-4, 4:-4], residual[4:-4, 4:-4, 4:-4])


def level_smooth(source, start, conduct, merged):
    extents = source.shape[1:] if merged else source.shape
    if min(extents) >= 4:
        return smooth_deep(source, start, conduct, merged)
    return smooth(source, conduct)


def coarse_sum(field):
    first, second, third = field.shape
    blocks = field.reshape(first // 2, 2, second // 2, 2, third // 2, 2)
    return jnp.sum(blocks, axis=(1, 3, 5))


def shards(conductivity, initial_guess, right_side):
    fine_solution, residual_zero = level_smooth(right_side, initial_guess, conductivity, False)
    conduct_one = 0.125 * coarse_sum(conductivity)
    level_one_solution, residual_one = level_smooth(
        0.25 * coarse_sum(residual_zero), None, conduct_one, False
    )
    conduct_two = 0.125 * coarse_sum(conduct_one)
    source_two = 0.25 * coarse_sum(residual_one)
    bundle = jnp.stack([source_two, conduct_two])
    bundle = lax.all_gather(bundle, "gx", axis=1, tiled=True)
    level_two_solution, residual_two = level_smooth(bundle[0], None, bundle[1], True)
    conduct_three = 0.125 * coarse_sum(bundle[1])
    level_three_solution, level_three_residual = level_smooth(
        0.25 * coarse_sum(residual_two), None, conduct_three, True
    )
    return (
        fine_solution,
        level_one_solution,
        level_two_solution,
        level_three_solution,
        level_three_residual,
    )


FIELDS = 3
WIDTH = 4
ROWS = 8
LANES = 128


def in_range(index, count):
    return (index >= 0) & (index < count)


def shift(value, amount, axis):
    return pltpu.roll(value, amount % value.shape[axis], axis)


def face_planes(conduct, grown):
    count = len(conduct)
    edge = 1 if grown else 0
    weight_x = [None] * (count + 1)
    for i in range(1, count):
        weight_x[i] = 0.5 * (conduct[i - 1] + conduct[i])
    if not grown:
        weight_x[0] = 0.5 * conduct[0]
        weight_x[count] = 0.5 * conduct[count - 1]
    weight_z = [None] * count
    weight_y = [None] * count
    inverse = [None] * count
    for i in range(edge, count - edge):
        weight_z[i] = 0.5 * (conduct[i] + shift(conduct[i], -1, 0))
        weight_y[i] = 0.5 * (conduct[i] + shift(conduct[i], -1, 1))
        diagonal = weight_x[i] + weight_x[i + 1]
        diagonal = diagonal + (weight_z[i] + shift(weight_z[i], 1, 0))
        diagonal = diagonal + (weight_y[i] + shift(weight_y[i], 1, 1))
        inside = conduct[i] > 0.0
        inverse[i] = jnp.where(inside, 1.0 / jnp.where(inside, diagonal, 1.0), 0.0)
    return weight_x, weight_y, weight_z, inverse


def operate_planes(faces, field, low, high):
    weight_x, weight_y, weight_z, _ = faces
    count = len(field)
    flux_x = [None] * (count + 1)
    for i in range(low, high + 1):
        if i == 0:
            flux_x[i] = weight_x[i] * field[i]
        elif i == count:
            flux_x[i] = -(weight_x[i] * field[i - 1])
        else:
            flux_x[i] = weight_x[i] * (field[i] - field[i - 1])
    result = [None] * count
    for i in range(low, high):
        flux_z = weight_z[i] * (field[i] - shift(field[i], -1, 0))
        flux_y = weight_y[i] * (field[i] - shift(field[i], -1, 1))
        result[i] = (
            (flux_x[i] - flux_x[i + 1])
            + (flux_z - shift(flux_z, 1, 0))
            + (flux_y - shift(flux_y, 1, 1))
        )
    return result


def coarse_faces(conduct):
    count, length = len(conduct), conduct[0].shape[0]
    row = lax.broadcasted_iota(jnp.int32, conduct[0].shape, 0)
    first, last = row == 0, row == length - 1
    weights, diagonals, inverses = [], [], []
    for i in range(count):
        own = conduct[i]
        half = 0.5 * own
        below = 0.5 * (own + conduct[i - 1]) if i > 0 else half
        above = 0.5 * (own + conduct[i + 1]) if i + 1 < count else half
        before = jnp.where(first, half, 0.5 * (own + shift(own, 1, 0)))
        after = jnp.where(last, half, 0.5 * (own + shift(own, -1, 0)))
        left = 0.5 * (own + shift(own, 1, 1))
        right = 0.5 * (own + shift(own, -1, 1))
        diagonal = (below + above) + (before + after) + (left + right)
        inside = own > 0.0
        diagonals.append(diagonal)
        inverses.append(jnp.where(inside, 1.0 / jnp.where(inside, diagonal, 1.0), 0.0))
        before = jnp.where(first, 0.0, before)
        after = jnp.where(last, 0.0, after)
        weights.append((below, above, before, after, left, right))
    return weights, diagonals, None, inverses


def operate_coarse(faces, field):
    weights, diagonals = faces[0], faces[1]
    count = len(field)
    result = []
    for i in range(count):
        below, above, before, after, left, right = weights[i]
        own = field[i]
        value = diagonals[i] * own
        if i > 0:
            value = value - below * field[i - 1]
        if i + 1 < count:
            value = value - above * field[i + 1]
        rolled = before * shift(own, 1, 0) + after * shift(own, -1, 0)
        rolled = rolled + (left * shift(own, 1, 1) + right * shift(own, -1, 1))
        result.append(value - rolled)
    return result


def smooth_planes(faces, residual, start, grown, between=None):
    theta = 0.5 * (upper_bound + lower_bound)
    delta = 0.5 * (upper_bound - lower_bound)
    sigma = theta / delta
    inverse = faces[3]
    count = len(residual)
    edge = 1 if grown else 0
    low, high = edge, count - edge
    residual = list(residual)
    direction = [None] * count
    for i in range(low, high):
        direction[i] = residual[i] * (inverse[i] * (1.0 / theta))
    ratio_now = 1.0 / sigma
    solution = list(start) if start is not None else [None] * count
    for sweep_index in range(SWEEPS):
        for i in range(low, high):
            solution[i] = direction[i] if solution[i] is None else solution[i] + direction[i]
        low, high = low + edge, high - edge
        if grown:
            applied = operate_planes(faces, direction, low, high)
        else:
            applied = operate_coarse(faces, direction)
        for i in range(low, high):
            residual[i] = residual[i] - applied[i]
        if between is not None and sweep_index == 0:
            between()
        if sweep_index + 1 < SWEEPS:
            ratio_next = 1.0 / (2.0 * sigma - ratio_now)
            turned = [None] * count
            for i in range(low, high):
                turned[i] = (ratio_next * ratio_now) * direction[i] + (
                    2.0 * ratio_next / delta
                ) * (residual[i] * inverse[i])
            direction = turned
            ratio_now = ratio_next
    return solution, residual


def split_dot(value, matrix):
    parts = []
    rest = value
    for _ in range(3):
        part = rest.astype(jnp.bfloat16)
        parts.append(part.astype(jnp.float32))
        rest = rest - parts[-1]
    rows = value.shape[0]
    stacked = jnp.concatenate(parts, axis=0).astype(jnp.bfloat16)
    product = jnp.dot(stacked, matrix, preferred_element_type=jnp.float32)
    return product[:rows] + product[rows : 2 * rows] + product[2 * rows :]


def pair_matrix(keep_low, keep_high, offset):
    source = lax.broadcasted_iota(jnp.int32, (LANES, LANES), 0)
    target = lax.broadcasted_iota(jnp.int32, (LANES, LANES), 1)
    low = (source < keep_low) & (target == offset + (source >> 1))
    high = (source >= LANES - keep_high) & (target == LANES // 2 + (source >> 1))
    return jnp.where(low | high, 1.0, 0.0).astype(jnp.bfloat16)


def pair_rows(value, hold, q):
    rows = value.shape[0]
    hold[q, 0:rows, :] = value
    even = hold[q, pl.ds(0, rows // 2, stride=2), :]
    return even + hold[q, pl.ds(1, rows // 2, stride=2), :]


def kernel(sizes, *refs):
    count_x, count_y, count_z = sizes
    inputs = refs[0:3]
    outs = refs[3:8]
    grown = refs[8:11]
    (pack_full, pack_edge, pack_rows, got_full, got_edge, got_rows, own_one, own_half, line_half, all_one,
     all_half, hold, solved_one, out_fine, out_one, out_two,
     out_three, out_rest, load_sem, face_send, face_recv, row_send, row_recv,
     full_send, full_recv, edge_send, edge_recv, one_send, one_recv, hop_send, hop_recv, store_sem) = refs[11:]
    kept = (out_fine, out_one, out_two, out_three, out_rest)
    stores = [pltpu.make_async_copy(kept[i], outs[i], store_sem.at[i]) for i in range(5)]
    planes, rows = inputs[0].shape[0], inputs[0].shape[1]
    x = lax.axis_index("gx")
    y = lax.axis_index("gy")
    z = lax.axis_index("gz")
    first_z = z == 0

    loads = []
    for f in range(FIELDS):
        loads.append(pltpu.make_async_copy(
            inputs[f], grown[f].at[planes : 2 * planes, 0:rows, 0:LANES], load_sem.at[f]))
        loads[-1].start()

    def other(step, turn, dy):
        return {"gx": lax.rem(x + step, count_x), "gy": y + dy, "gz": lax.rem(z + turn, count_z)}

    near = planes - WIDTH
    strip_list = [
        [(f, q) for f in range(FIELDS) for q in range(planes)
         if q > near + (1 if f == 2 else 0)],
        [(f, q) for f in range(FIELDS) for q in range(planes)],
        [(f, q) for f in range(FIELDS) for q in range(planes)
         if q < WIDTH - 1 - (1 if f == 2 else 0)],
    ]
    partners = [
        (step, turn, dy)
        for step in sorted(range(count_x), key=lambda step: -min(step, count_x - step))
        for turn in range(count_z)
        for dy in (0, -1, 1)
        if (step, turn, dy) != (0, 0, 0)
    ]
    barrier = pltpu.get_barrier_semaphore()
    for dy in (0, -1, 1):
        @pl.when(in_range(y + dy, count_y))
        def _():
            chosen = [p for p in partners if p[2] == dy]
            for step, turn, _dy in chosen:
                pl.semaphore_signal(
                    barrier, inc=1, device_id=other(step, turn, dy),
                    device_id_type=pl.DeviceIdType.MESH)

    for f in range(FIELDS):
        @pl.when(x == 0)
        def _():
            grown[f][0:planes, 0:rows, 0:LANES] = jnp.zeros((planes, rows, LANES), jnp.float32)

        @pl.when(x == count_x - 1)
        def _():
            grown[f][2 * planes : 3 * planes, 0:rows, 0:LANES] = jnp.zeros(
                (planes, rows, LANES), jnp.float32)

    for slot in range(3):
        for side in range(2):
            there = in_range(x + (slot - 1), count_x) & in_range(y + (2 * side - 1), count_y)

            @pl.when(jnp.logical_not(there))
            def _():
                got_full[slot, side] = jnp.zeros((rows // 2, LANES), jnp.float32)
                got_edge[slot, side] = jnp.zeros((ROWS, LANES), jnp.float32)

        if slot != 1:
            @pl.when(jnp.logical_not(in_range(x + (slot - 1), count_x)))
            def _():
                got_rows[slot] = jnp.zeros(got_rows.shape[1:], jnp.float32)

    for side in range(2):
        @pl.when(jnp.logical_not(in_range(y + (2 * side - 1), count_y)))
        def _():
            for part in range(2):
                all_half[part, side] = jnp.zeros(all_half.shape[2:], jnp.float32)

    for load in loads:
        load.wait()

    lane = lax.broadcasted_iota(jnp.int32, (rows, LANES), 1)
    row_index = lax.broadcasted_iota(jnp.int32, (ROWS, LANES), 0)
    low_lane = (lane[0 : rows // 2] & WIDTH) == 0
    leave = (row_index < WIDTH) == jnp.logical_not(first_z)
    strips = {}
    packed = jnp.zeros((rows, LANES), jnp.float32)
    for f in range(FIELDS):
        for q in range(planes):
            k = f * planes + q
            piece = grown[f][planes + q, 0:rows, 0:LANES]
            strips[f, q] = jnp.where(first_z, piece[rows - ROWS :], piece[0:ROWS])
            moved = shift(piece, 2 * WIDTH * k, 1)
            window = ((lane + (LANES + WIDTH - 2 * WIDTH * k)) & (LANES - 1)) < 2 * WIDTH
            packed = jnp.where(window, moved, packed)
    for slot in range(3):
        for t in range(len(strip_list[slot]) // 2):
            first, second = strip_list[slot][2 * t], strip_list[slot][2 * t + 1]
            pack_rows[slot, t] = jnp.where(
                leave, strips[first], shift(strips[second], WIDTH, 0))
    top, bottom = packed[0 : rows // 2], packed[rows // 2 : rows]
    pack_full[0] = jnp.where(low_lane, shift(bottom, -WIDTH, 1), top)
    pack_full[1] = jnp.where(low_lane, top, shift(bottom, WIDTH, 1))
    pack_edge[...] = jnp.where(first_z, packed[rows - ROWS :], packed[0:ROWS])

    wanted = (count_x * count_z - 1) + count_x * count_z * (
        jnp.where(y > 0, 1, 0) + jnp.where(y < count_y - 1, 1, 0))
    pl.semaphore_wait(barrier, wanted)

    def send(src, dst, send_sem, recv_sem, device, to, back):
        copy = pltpu.make_async_remote_copy(
            src_ref=src, dst_ref=dst, send_sem=send_sem, recv_sem=recv_sem,
            device_id=device, device_id_type=pl.DeviceIdType.MESH)
        if to is None:
            copy.start()
        else:
            pl.when(to)(copy.start)
        return copy, to, back

    def wait_recv(entry):
        copy, _, back = entry
        if back is None:
            copy.wait_recv()
        else:
            pl.when(back)(copy.wait_recv)

    def wait_send(entry):
        copy, to, _ = entry
        if to is None:
            copy.wait_send()
        else:
            pl.when(to)(copy.wait_send)

    faces = []
    strips_sent = []

    def send_face(f):
        for dx in (1, -1):
            to, back = in_range(x + dx, count_x), in_range(x - dx, count_x)
            low, high = 0, planes
            if f == 2:
                low, high = (1, planes) if dx == 1 else (0, planes - 1)
            base = 0 if dx == 1 else 2 * planes
            index = (dx + 1) // 2 * FIELDS + f
            faces.append((f, send(
                grown[f].at[planes + low : planes + high, 0:rows, 0:LANES],
                grown[f].at[base + low : base + high, 0:rows, 0:LANES],
                face_send.at[index], face_recv.at[index],
                {"gx": x + dx, "gy": y, "gz": z}, to, back)))

    send_face(0)
    for dx in (1, -1, 0):
        slot = 1 - dx
        to, back = (in_range(x + dx, count_x), in_range(x - dx, count_x)) if dx else (None, None)
        tiles = len(strip_list[slot]) // 2
        strips_sent.append(send(
            pack_rows.at[slot, 0:tiles], got_rows.at[slot, 0:tiles], row_send.at[slot],
            row_recv.at[slot], {"gx": x + dx, "gy": y, "gz": 1 - z}, to, back))
        for dy in (1, -1):
            side = (1 - dy) // 2
            to = in_range(x + dx, count_x) & in_range(y + dy, count_y)
            back = in_range(x - dx, count_x) & in_range(y - dy, count_y)
            strips_sent.append(send(
                pack_full.at[side], got_full.at[slot, side], full_send.at[slot * 2 + side],
                full_recv.at[slot * 2 + side], {"gx": x + dx, "gy": y + dy, "gz": z}, to, back))
            strips_sent.append(send(
                pack_edge, got_edge.at[slot, side], edge_send.at[slot * 2 + side],
                edge_recv.at[slot * 2 + side], {"gx": x + dx, "gy": y + dy, "gz": 1 - z}, to, back))
    send_face(1)
    send_face(2)

    to_one = [pair_matrix(LANES, 0, 0), pair_matrix(LANES, 0, LANES // 2)]
    matrix_one = jnp.concatenate(to_one, axis=0)
    quarter = (lax.broadcasted_iota(jnp.int32, (ROWS, LANES), 1) & (LANES // 4)) == 0

    def restrict_fine(blocks, scale):
        pairs = [pair_rows(blocks[2 * q] + blocks[2 * q + 1], hold, q) for q in range(planes // 2)]
        return scale * split_dot(jnp.concatenate(pairs, axis=1), matrix_one)

    hopped = (0,)
    here = z * count_x + x
    line = pl.ds(z * count_x, count_x)
    blocks_all = count_x * count_z

    def spread(part, value):
        own_one[part] = value
        top, bottom = value[0:ROWS], value[ROWS : 2 * ROWS]
        own_half[part, 0] = jnp.where(quarter, shift(bottom, -(LANES // 4), 1), top)
        own_half[part, 1] = jnp.where(quarter, top, shift(bottom, LANES // 4, 1))
        all_one[part, here] = value
        for dy in (0, 1, -1):
            side = (1 - dy) // 2

            def start():
                for step, turn, _dy in [p for p in partners if p[2] == dy]:
                    if dy == 0:
                        source, target = own_one.at[part], all_one.at[part, here]
                    else:
                        source, target = own_half.at[part, side], all_half.at[part, side, here]
                    pltpu.make_async_remote_copy(
                        src_ref=source, dst_ref=target, send_sem=one_send.at[part, dy + 1],
                        recv_sem=one_recv.at[part, dy + 1], device_id=other(step, turn, dy),
                        device_id_type=pl.DeviceIdType.MESH).start()

            if dy == 0:
                start()
            else:
                pl.when(in_range(y + dy, count_y))(start)

    def remote(source, target, send_sem, recv_sem, device):
        return pltpu.make_async_remote_copy(
            src_ref=source, dst_ref=target, send_sem=send_sem, recv_sem=recv_sem,
            device_id=device, device_id_type=pl.DeviceIdType.MESH)

    def first_hop(part, value):
        own_one[part] = value
        all_one[part, here] = value
        for step in range(1, count_x):
            remote(own_one.at[part], all_one.at[part, here], hop_send.at[part],
                   hop_recv.at[part], other(step, 0, 0)).start()

    def settle_hop(part, received):
        bytes_of = all_one.at[part, 0 : count_x - 1]
        copy = remote(bytes_of, bytes_of, hop_send.at[part], hop_recv.at[part], other(1, 0, 0))
        copy.wait_recv() if received else copy.wait_send()

    def line_copies(part, dy):
        side = (1 - dy) // 2
        sems = (one_send.at[part, dy + 1], one_recv.at[part, dy + 1])
        if dy == 0:
            return [remote(all_one.at[part, line], all_one.at[part, line], *sems, other(0, 1, 0))]
        return [
            remote(line_half.at[part, side], all_half.at[part, side, line], *sems,
                   other(0, turn, dy))
            for turn in range(count_z)
        ]

    def second_hop(part):
        for from_x in range(count_x):
            value = all_one[part, z * count_x + from_x]
            top, bottom = value[0:ROWS], value[ROWS : 2 * ROWS]
            line_half[part, 0, from_x] = jnp.where(quarter, shift(bottom, -(LANES // 4), 1), top)
            line_half[part, 1, from_x] = jnp.where(quarter, top, shift(bottom, LANES // 4, 1))
        for dy in (0, 1, -1):
            def start():
                for copy in line_copies(part, dy):
                    copy.start()

            if dy == 0:
                start()
            else:
                pl.when(in_range(y + dy, count_y))(start)

    def settle(part, received):
        for dy in (0, 1, -1):
            side = (1 - dy) // 2
            if dy == 0:
                extent = count_x if part in hopped else blocks_all - 1
                bytes_of = all_one.at[part, 0:extent]
            else:
                bytes_of = all_half.at[part, side]
            copy = remote(bytes_of, bytes_of, one_send.at[part, dy + 1],
                          one_recv.at[part, dy + 1], other(1, 0, 0))
            finish = copy.wait_recv if received else copy.wait_send
            if dy == 0:
                finish()
            else:
                pl.when(in_range(y - dy if received else y + dy, count_y))(finish)

    coarse_conduct = restrict_fine(
        [grown[0][planes + q, 0:rows, 0:LANES] for q in range(planes)], 0.125)
    first_hop(0, coarse_conduct)

    for entry in strips_sent:
        wait_recv(entry)
    row_keep = (row_index < WIDTH) == first_z
    lane_edge = lax.broadcasted_iota(jnp.int32, (rows + ROWS, LANES), 1)
    lane_keep = (lane_edge < WIDTH) | (lane_edge >= LANES - WIDTH)
    low_edge = low_lane[0:ROWS]
    joined = []
    for slot in range(3):
        low, high = got_full[slot, 1], got_full[slot, 0]
        joined.append(jnp.concatenate([
            jnp.where(low_lane, low, high),
            jnp.where(low_lane, shift(low, -WIDTH, 1), shift(high, WIDTH, 1)),
            jnp.where(row_keep, jnp.where(low_edge, got_edge[slot, 1], got_edge[slot, 0]), 0.0),
        ], axis=0))
    for f in range(FIELDS):
        for slot in range(3):
            for q in range(planes):
                p = slot * planes + q
                strip = jnp.zeros((ROWS, LANES), jnp.float32)
                if (f, q) in strip_list[slot]:
                    index = strip_list[slot].index((f, q))
                    strip = got_rows[slot, index // 2]
                    if index % 2 == 1:
                        strip = shift(strip, WIDTH, 0)
                    strip = jnp.where(row_keep, strip, 0.0)
                grown[f][p, rows : rows + ROWS, 0:LANES] = strip
                grown[f][p, :, LANES : 2 * LANES] = jnp.where(
                    lane_keep, shift(joined[slot], -2 * WIDTH * (f * planes + q), 1), 0.0)

    def wait_face(f):
        for index, entry in faces:
            if index == f:
                wait_recv(entry)

    wait_face(0)
    faces_fine = face_planes([grown[0][p] for p in range(3 * planes)], True)
    wait_face(1)
    start = [grown[1][p] for p in range(3 * planes)]
    applied = operate_planes(faces_fine, start, 1, 3 * planes - 1)
    wait_face(2)
    residual = [None] * (3 * planes)
    for p in range(1, 3 * planes - 1):
        residual[p] = grown[2][p] - applied[p]

    def pass_on():
        settle_hop(0, True)
        second_hop(0)

    solved, residual = smooth_planes(faces_fine, residual, start, True, pass_on)
    spread(
        1, restrict_fine([residual[planes + q][0:rows, 0:LANES] for q in range(planes)], 0.25))
    for q in range(planes):
        out_fine[q] = solved[planes + q][0:rows, 0:LANES]
    stores[0].start()

    lane_one = lax.broadcasted_iota(jnp.int32, (2 * ROWS, LANES), 1)
    lower = lane_one < LANES // 2

    def assemble(part):
        level = []
        for from_x in range(count_x):
            blocks = [[], []]
            for from_z in range(count_z):
                block = from_z * count_x + from_x
                own = all_one[part, block]
                low, high = all_half[part, 0, block], all_half[part, 1, block]
                beside = jnp.concatenate(
                    [jnp.where(quarter, high, low),
                     jnp.where(quarter, shift(high, -(LANES // 4), 1), shift(low, LANES // 4, 1))],
                    axis=0)
                blocks[0].append(jnp.where(lower, own, shift(beside, LANES // 2, 1)))
                blocks[1].append(jnp.where(lower, shift(own, LANES // 2, 1), beside))
            for q in range(2):
                level.append(jnp.concatenate(blocks[q], axis=0))
        return level

    def restrict(level, matrix, scale):
        length = level[0].shape[0]
        summed = []
        for q in range(len(level) // 2):
            both = level[2 * q] + level[2 * q + 1]
            summed.append(pair_rows(both, hold, q))
        joined = scale * split_dot(jnp.concatenate(summed, axis=0), matrix)
        half = length // 2
        return [joined[q * half : (q + 1) * half] for q in range(len(summed))]

    matrix_two = pair_matrix(3 * LANES // 4, LANES // 4, 0)
    matrix_three = pair_matrix(3 * LANES // 8, LANES // 8, 0)
    settle(0, True)
    conduct_one = assemble(0)
    conduct_two = restrict(conduct_one, matrix_two, 0.125)
    conduct_three = restrict(conduct_two, matrix_three, 0.125)
    faces_one, faces_two, faces_three = (
        coarse_faces(conduct) for conduct in (conduct_one, conduct_two, conduct_three))

    settle(1, True)
    solved, residual = smooth_planes(faces_one, assemble(1), None, False)
    for p in range(len(solved)):
        block = solved[p][0 : 2 * rows // 2]
        solved_one[p] = jnp.where(first_z, block[0 : rows // 2], block[rows // 2 : rows])
    out_one[...] = solved_one[pl.ds(2 * x, 2), :, 0 : LANES // 2]
    stores[1].start()
    solved, residual = smooth_planes(
        faces_two, restrict(residual, matrix_two, 0.25), None, False)
    for p in range(len(solved)):
        half = rows // 4
        out_two[p] = jnp.where(first_z, solved[p][0:half], solved[p][half : 2 * half])[:, 0 : LANES // 4]
    stores[2].start()
    solved, residual = smooth_planes(
        faces_three, restrict(residual, matrix_three, 0.25), None, False)
    for p in range(len(solved)):
        half = rows // 8
        for result, out in ((solved, out_three), (residual, out_rest)):
            out[p] = jnp.where(first_z, result[p][0:half], result[p][half : 2 * half])[:, 0 : LANES // 8]

    stores[3].start()
    stores[4].start()
    for entry in strips_sent + [entry for _, entry in faces]:
        wait_send(entry)
    settle_hop(0, False)
    settle(0, False)
    settle(1, False)
    for store in stores:
        store.wait()


def hand_over(*refs):
    count = len(refs) // 2
    copies = []
    for i in range(count):
        copies.append(pltpu.make_async_copy(refs[i], refs[count + i], refs[-1].at[i]))
        copies[-1].start()
    for copy in copies:
        copy.wait()


def fits(mesh, shape):
    return (
        mesh.shape["gz"] == 2
        and mesh.shape["gx"] <= 4
        and shape[0] == WIDTH * mesh.shape["gx"]
        and shape[1] == 32 * mesh.shape["gz"]
        and shape[2] == LANES * mesh.shape["gy"]
    )


def fused(mesh, conductivity, initial_guess, right_side):
    sizes = (mesh.shape["gx"], mesh.shape["gy"], mesh.shape["gz"])
    count_x, _, count_z = sizes
    planes, rows, lanes = conductivity.shape
    f32 = jnp.float32
    shapes = [
        (planes, rows, lanes),
        (planes // 2, rows // 2, lanes // 2),
        (count_x * planes // 4, rows // 4, lanes // 4),
        (count_x * planes // 8, rows // 8, lanes // 8),
        (count_x * planes // 8, rows // 8, lanes // 8),
    ]
    blocks_all = count_x * count_z
    dma = pltpu.SemaphoreType.DMA
    scratch = [pltpu.VMEM((3 * planes, rows + ROWS, 2 * LANES), f32)] * FIELDS + [
        pltpu.VMEM((2, rows // 2, LANES), f32),
        pltpu.VMEM((ROWS, LANES), f32),
        pltpu.VMEM((3, FIELDS * planes // 2, ROWS, LANES), f32),
        pltpu.VMEM((3, 2, rows // 2, LANES), f32),
        pltpu.VMEM((3, 2, ROWS, LANES), f32),
        pltpu.VMEM((3, FIELDS * planes // 2, ROWS, LANES), f32),
        pltpu.VMEM((2, rows // 2, LANES), f32),
        pltpu.VMEM((2, 2, ROWS, LANES), f32),
        pltpu.VMEM((2, 2, count_x, ROWS, LANES), f32),
        pltpu.VMEM((2, blocks_all, rows // 2, LANES), f32),
        pltpu.VMEM((2, 2, blocks_all, ROWS, LANES), f32),
        pltpu.VMEM((count_x, rows, LANES), f32),
        pltpu.VMEM((2 * count_x, rows // 2, LANES), f32),
        *[pltpu.VMEM(shape, f32) for shape in shapes],
        dma((3,)),
        dma((6,)), dma((6,)),
        dma((3,)), dma((3,)),
        dma((6,)), dma((6,)),
        dma((6,)), dma((6,)),
        dma((2, 3)), dma((2, 3)),
        dma((2,)), dma((2,)),
        dma((5,)),
    ]
    outside = pl.BlockSpec(memory_space=pltpu.HBM)
    out_shape = [jax.ShapeDtypeStruct(shape, f32) for shape in shapes]
    results = pl.pallas_call(
        functools.partial(kernel, sizes),
        out_shape=out_shape,
        in_specs=[outside] * 3,
        out_specs=[outside] * 5,
        scratch_shapes=scratch,
        compiler_params=pltpu.CompilerParams(
            collective_id=0, has_side_effects=True, vmem_limit_bytes=56 * 2**20),
    )(conductivity, initial_guess, right_side)
    return pl.pallas_call(
        hand_over,
        out_shape=out_shape,
        in_specs=[pl.BlockSpec(memory_space=pltpu.VMEM)] * 5,
        out_specs=[outside] * 5,
        scratch_shapes=[dma((5,))],
        compiler_params=pltpu.CompilerParams(vmem_limit_bytes=56 * 2**20),
    )(*results)


def solution(mesh):
    placed = (P("gx", "gz", "gy"), P("gx", "gz", "gy"), P("gx", "gz", "gy"))

    def whole(conductivity, initial_guess, right_side):
        local = shards
        if fits(mesh, conductivity.shape):
            local = functools.partial(fused, mesh)
        return jax.shard_map(
            local,
            mesh=mesh,
            in_specs=placed,
            out_specs=(
                P("gx", "gz", "gy"),
                P("gx", "gz", "gy"),
                P(None, "gz", "gy"),
                P(None, "gz", "gy"),
                P(None, "gz", "gy"),
            ),
            check_vma=False,
        )(conductivity, initial_guess, right_side)

    return whole
```

```python
import functools

import jax
import jax.numpy as jnp
from jax import lax
from jax.experimental import pallas as pl
from jax.experimental.pallas import tpu as pltpu
from jax.sharding import PartitionSpec as P

SWEEPS = 3


lower_bound = 0.25
upper_bound = 2.0


def with_halo(block, sides, width):
    for axis, dim in sides:
        count = lax.axis_size(axis)
        forward = [(i, i + 1) for i in range(count - 1)]
        backward = [(target, source) for source, target in forward]
        low = lax.ppermute(
            lax.slice_in_dim(block, block.shape[dim] - width, None, axis=dim), axis, forward
        )
        high = lax.ppermute(lax.slice_in_dim(block, 0, width, axis=dim), axis, backward)
        block = jnp.concatenate([low, block, high], axis=dim)
    return block


def extend(bundle):
    return with_halo(bundle, (("gx", 1), ("gy", 3), ("gz", 2)), 1)


def deep_extend(bundle, merged):
    if merged:
        grown = with_halo(bundle, (("gy", 3), ("gz", 2)), 4)
        return jnp.pad(grown, ((0, 0), (4, 4), (0, 0), (0, 0)))
    return with_halo(bundle, (("gx", 1), ("gy", 3), ("gz", 2)), 4)


def neighbours(padded):
    return [
        padded[:-2, 1:-1, 1:-1],
        padded[2:, 1:-1, 1:-1],
        padded[1:-1, :-2, 1:-1],
        padded[1:-1, 2:, 1:-1],
        padded[1:-1, 1:-1, :-2],
        padded[1:-1, 1:-1, 2:],
    ]


def face_terms(conduct):
    others = neighbours(extend(conduct[None])[0])
    weights = [0.5 * (conduct + other) for other in others]
    diagonal = weights[0] + weights[1] + weights[2] + weights[3] + weights[4] + weights[5]
    return (weights, diagonal)


def operate(field, weights, diagonal):
    others = neighbours(extend(field[None])[0])
    result = diagonal * field
    for face_index in range(6):
        result = result - weights[face_index] * others[face_index]
    return result


def smooth(source, conduct):
    theta = 0.5 * (upper_bound + lower_bound)
    delta = 0.5 * (upper_bound - lower_bound)
    sigma = theta / delta
    weights, diagonal = face_terms(conduct)
    solution = jnp.zeros_like(source)
    residual = source
    direction = residual / (theta * diagonal)
    ratio_now = 1.0 / sigma
    for sweep_index in range(SWEEPS):
        solution = solution + direction
        residual = residual - operate(direction, weights, diagonal)
        if sweep_index + 1 < SWEEPS:
            ratio_next = 1.0 / (2.0 * sigma - ratio_now)
            direction = (
                ratio_next * ratio_now * direction + 2.0 * ratio_next / delta * residual / diagonal
            )
            ratio_now = ratio_next
    return (solution, residual)


def local_operate(field, weights, diagonal):
    others = neighbours(jnp.pad(field, 1))
    result = diagonal * field
    for face_index in range(6):
        result = result - weights[face_index] * others[face_index]
    return result


def smooth_deep(source, start, conduct, merged):
    theta = 0.5 * (upper_bound + lower_bound)
    delta = 0.5 * (upper_bound - lower_bound)
    sigma = theta / delta
    members = [conduct, source, jnp.ones_like(source)]
    if start is not None:
        members.append(start)
    grown = deep_extend(jnp.stack(members), merged)
    padded_conduct = grown[0]
    padded_source = grown[1]
    inside = grown[2]
    others = neighbours(jnp.pad(padded_conduct, 1))
    weights = [0.5 * (padded_conduct + other) for other in others]
    diagonal = weights[0] + weights[1] + weights[2] + weights[3] + weights[4] + weights[5]
    safe_diagonal = jnp.where(inside > 0.5, diagonal, 1.0)
    if start is None:
        solution = jnp.zeros_like(padded_source)
        residual = padded_source
    else:
        solution = grown[3]
        residual = padded_source - local_operate(solution, weights, diagonal)
    direction = inside * (residual / (theta * safe_diagonal))
    ratio_now = 1.0 / sigma
    for sweep_index in range(SWEEPS):
        solution = solution + direction
        residual = residual - local_operate(direction, weights, diagonal)
        if sweep_index + 1 < SWEEPS:
            ratio_next = 1.0 / (2.0 * sigma - ratio_now)
            direction = inside * (
                ratio_next * ratio_now * direction
                + 2.0 * ratio_next / delta * residual / safe_diagonal
            )
            ratio_now = ratio_next
    return (solution[4:-4, 4:-4, 4:-4], residual[4:-4, 4:-4, 4:-4])


def level_smooth(source, start, conduct, merged):
    extents = source.shape[1:] if merged else source.shape
    if min(extents) >= 4:
        return smooth_deep(source, start, conduct, merged)
    return smooth(source, conduct)


def coarse_sum(field):
    first, second, third = field.shape
    blocks = field.reshape(first // 2, 2, second // 2, 2, third // 2, 2)
    return jnp.sum(blocks, axis=(1, 3, 5))


def shards(conductivity, initial_guess, right_side):
    fine_solution, residual_zero = level_smooth(right_side, initial_guess, conductivity, False)
    conduct_one = 0.125 * coarse_sum(conductivity)
    level_one_solution, residual_one = level_smooth(
        0.25 * coarse_sum(residual_zero), None, conduct_one, False
    )
    conduct_two = 0.125 * coarse_sum(conduct_one)
    source_two = 0.25 * coarse_sum(residual_one)
    bundle = jnp.stack([source_two, conduct_two])
    bundle = lax.all_gather(bundle, "gx", axis=1, tiled=True)
    level_two_solution, residual_two = level_smooth(bundle[0], None, bundle[1], True)
    conduct_three = 0.125 * coarse_sum(bundle[1])
    level_three_solution, level_three_residual = level_smooth(
        0.25 * coarse_sum(residual_two), None, conduct_three, True
    )
    return (
        fine_solution,
        level_one_solution,
        level_two_solution,
        level_three_solution,
        level_three_residual,
    )


FIELDS = 3
WIDTH = 4
ROWS = 8
LANES = 128


def in_range(index, count):
    return (index >= 0) & (index < count)


def shift(value, amount, axis):
    return pltpu.roll(value, amount % value.shape[axis], axis)


def face_planes(conduct, grown):
    count = len(conduct)
    edge = 1 if grown else 0
    weight_x = [None] * (count + 1)
    for i in range(1, count):
        weight_x[i] = 0.5 * (conduct[i - 1] + conduct[i])
    if not grown:
        weight_x[0] = 0.5 * conduct[0]
        weight_x[count] = 0.5 * conduct[count - 1]
    weight_z = [None] * count
    weight_y = [None] * count
    inverse = [None] * count
    for i in range(edge, count - edge):
        weight_z[i] = 0.5 * (conduct[i] + shift(conduct[i], -1, 0))
        weight_y[i] = 0.5 * (conduct[i] + shift(conduct[i], -1, 1))
        diagonal = weight_x[i] + weight_x[i + 1]
        diagonal = diagonal + (weight_z[i] + shift(weight_z[i], 1, 0))
        diagonal = diagonal + (weight_y[i] + shift(weight_y[i], 1, 1))
        inside = conduct[i] > 0.0
        inverse[i] = jnp.where(inside, 1.0 / jnp.where(inside, diagonal, 1.0), 0.0)
    return weight_x, weight_y, weight_z, inverse


def operate_planes(faces, field, low, high, keep=None):
    weight_x, weight_y, weight_z, _ = faces
    count = len(field)
    flux_x = [None] * (count + 1)
    for i in range(low, high + 1):
        if i == 0:
            flux_x[i] = weight_x[i] * field[i]
        elif i == count:
            flux_x[i] = -(weight_x[i] * field[i - 1])
        else:
            flux_x[i] = weight_x[i] * (field[i] - field[i - 1])
    result = [None] * count
    rows, lanes = keep if keep is not None else field[low].shape
    for i in range(low, high):
        flux_z = weight_z[i] * (field[i] - shift(field[i], -1, 0))
        flux_y = weight_y[i] * (field[i] - shift(field[i], -1, 1))
        flux_z, flux_y = flux_z[:, 0:lanes], flux_y[0:rows]
        result[i] = (
            (flux_x[i] - flux_x[i + 1])[0:rows, 0:lanes]
            + (flux_z - shift(flux_z, 1, 0))[0:rows]
            + (flux_y - shift(flux_y, 1, 1))[:, 0:lanes]
        )
    return result


def coarse_faces(conduct):
    count, length = len(conduct), conduct[0].shape[0]
    row = lax.broadcasted_iota(jnp.int32, conduct[0].shape, 0)
    first, last = row == 0, row == length - 1
    weights, diagonals, inverses = [], [], []
    for i in range(count):
        own = conduct[i]
        half = 0.5 * own
        below = 0.5 * (own + conduct[i - 1]) if i > 0 else half
        above = 0.5 * (own + conduct[i + 1]) if i + 1 < count else half
        before = jnp.where(first, half, 0.5 * (own + shift(own, 1, 0)))
        after = jnp.where(last, half, 0.5 * (own + shift(own, -1, 0)))
        left = 0.5 * (own + shift(own, 1, 1))
        right = 0.5 * (own + shift(own, -1, 1))
        diagonal = (below + above) + (before + after) + (left + right)
        inside = own > 0.0
        diagonals.append(diagonal)
        inverses.append(jnp.where(inside, 1.0 / jnp.where(inside, diagonal, 1.0), 0.0))
        before = jnp.where(first, 0.0, before)
        after = jnp.where(last, 0.0, after)
        weights.append((below, above, before, after, left, right))
    return weights, diagonals, None, inverses


def operate_coarse(faces, field):
    weights, diagonals = faces[0], faces[1]
    count = len(field)
    result = []
    for i in range(count):
        below, above, before, after, left, right = weights[i]
        own = field[i]
        value = diagonals[i] * own
        if i > 0:
            value = value - below * field[i - 1]
        if i + 1 < count:
            value = value - above * field[i + 1]
        rolled = before * shift(own, 1, 0) + after * shift(own, -1, 0)
        rolled = rolled + (left * shift(own, 1, 1) + right * shift(own, -1, 1))
        result.append(value - rolled)
    return result


def smooth_planes(faces, residual, start, grown, block=None):
    theta = 0.5 * (upper_bound + lower_bound)
    delta = 0.5 * (upper_bound - lower_bound)
    sigma = theta / delta
    inverse = faces[3]
    count = len(residual)
    edge = 1 if grown else 0
    low, high = edge, count - edge
    residual = list(residual)
    direction = [None] * count
    for i in range(low, high):
        direction[i] = residual[i] * (inverse[i] * (1.0 / theta))
    ratio_now = 1.0 / sigma
    solution = list(start) if start is not None else [None] * count
    for sweep_index in range(SWEEPS):
        for i in range(low, high):
            solution[i] = direction[i] if solution[i] is None else solution[i] + direction[i]
        low, high = low + edge, high - edge
        if grown:
            keep = block if sweep_index + 1 == SWEEPS else None
            applied = operate_planes(faces, direction, low, high, keep)
        else:
            applied = operate_coarse(faces, direction)
        for i in range(low, high):
            extent = applied[i].shape
            residual[i] = residual[i][0 : extent[0], 0 : extent[1]] - applied[i]
        if sweep_index + 1 < SWEEPS:
            ratio_next = 1.0 / (2.0 * sigma - ratio_now)
            turned = [None] * count
            for i in range(low, high):
                turned[i] = (ratio_next * ratio_now) * direction[i] + (
                    2.0 * ratio_next / delta
                ) * (residual[i] * inverse[i])
            direction = turned
            ratio_now = ratio_next
    return solution, residual


def split_dot(value, matrix):
    parts = []
    rest = value
    for _ in range(3):
        part = rest.astype(jnp.bfloat16)
        parts.append(part.astype(jnp.float32))
        rest = rest - parts[-1]
    rows = value.shape[0]
    stacked = jnp.concatenate(parts, axis=0).astype(jnp.bfloat16)
    product = jnp.dot(stacked, matrix, preferred_element_type=jnp.float32)
    return product[:rows] + product[rows : 2 * rows] + product[2 * rows :]


def pair_matrix(keep_low, keep_high, offset):
    source = lax.broadcasted_iota(jnp.int32, (LANES, LANES), 0)
    target = lax.broadcasted_iota(jnp.int32, (LANES, LANES), 1)
    low = (source < keep_low) & (target == offset + (source >> 1))
    high = (source >= LANES - keep_high) & (target == LANES // 2 + (source >> 1))
    return jnp.where(low | high, 1.0, 0.0).astype(jnp.bfloat16)


def pair_rows(value, hold, q):
    rows = value.shape[0]
    hold[q, 0:rows, :] = value
    even = hold[q, pl.ds(0, rows // 2, stride=2), :]
    return even + hold[q, pl.ds(1, rows // 2, stride=2), :]


def kernel(sizes, *refs):
    count_x, count_y, count_z = sizes
    inputs = refs[0:3]
    outs = refs[3:8]
    grown = refs[8:11]
    (pack_full, pack_edge, pack_rows, got_full, got_edge, got_rows, own_one, own_half, line_half, all_one,
     all_half, hold, solved_one, out_fine, out_one, out_two,
     out_three, out_rest, load_sem, face_send, face_recv, row_send, row_recv,
     full_send, full_recv, edge_send, edge_recv, one_send, one_recv, hop_send, hop_recv, store_sem) = refs[11:]
    kept = (out_fine, out_one, out_two, out_three, out_rest)
    stores = [pltpu.make_async_copy(kept[i], outs[i], store_sem.at[i]) for i in range(5)]
    planes, rows = inputs[0].shape[0], inputs[0].shape[1]
    x = lax.axis_index("gx")
    y = lax.axis_index("gy")
    z = lax.axis_index("gz")
    first_z = z == 0

    loads = []
    for f in range(FIELDS):
        loads.append(pltpu.make_async_copy(
            inputs[f], grown[f].at[planes : 2 * planes, 0:rows, 0:LANES], load_sem.at[f]))
        loads[-1].start()

    def other(step, turn, dy):
        return {"gx": lax.rem(x + step, count_x), "gy": y + dy, "gz": lax.rem(z + turn, count_z)}

    near = planes - WIDTH
    strip_list = [
        [(f, q) for f in range(FIELDS) for q in range(planes)
         if q > near + (1 if f == 2 else 0)],
        [(f, q) for f in range(FIELDS) for q in range(planes)],
        [(f, q) for f in range(FIELDS) for q in range(planes)
         if q < WIDTH - 1 - (1 if f == 2 else 0)],
    ]
    partners = [
        (step, turn, dy)
        for step in sorted(range(count_x), key=lambda step: -min(step, count_x - step))
        for turn in range(count_z)
        for dy in (0, -1, 1)
        if (step, turn, dy) != (0, 0, 0)
    ]
    barrier = pltpu.get_barrier_semaphore()
    for dy in (0, -1, 1):
        @pl.when(in_range(y + dy, count_y))
        def _():
            chosen = [p for p in partners if p[2] == dy]
            for step, turn, _dy in chosen:
                pl.semaphore_signal(
                    barrier, inc=1, device_id=other(step, turn, dy),
                    device_id_type=pl.DeviceIdType.MESH)

    for f in range(FIELDS):
        @pl.when(x == 0)
        def _():
            grown[f][0:planes, 0:rows, 0:LANES] = jnp.zeros((planes, rows, LANES), jnp.float32)

        @pl.when(x == count_x - 1)
        def _():
            grown[f][2 * planes : 3 * planes, 0:rows, 0:LANES] = jnp.zeros(
                (planes, rows, LANES), jnp.float32)

    for slot in range(3):
        for side in range(2):
            there = in_range(x + (slot - 1), count_x) & in_range(y + (2 * side - 1), count_y)

            @pl.when(jnp.logical_not(there))
            def _():
                got_full[slot, side] = jnp.zeros((rows // 2, LANES), jnp.float32)
                got_edge[slot, side] = jnp.zeros((ROWS, LANES), jnp.float32)

        if slot != 1:
            @pl.when(jnp.logical_not(in_range(x + (slot - 1), count_x)))
            def _():
                got_rows[slot] = jnp.zeros(got_rows.shape[1:], jnp.float32)

    for side in range(2):
        @pl.when(jnp.logical_not(in_range(y + (2 * side - 1), count_y)))
        def _():
            for part in range(2):
                all_half[part, side] = jnp.zeros(all_half.shape[2:], jnp.float32)

    for load in loads:
        load.wait()

    lane = lax.broadcasted_iota(jnp.int32, (rows, LANES), 1)
    row_index = lax.broadcasted_iota(jnp.int32, (ROWS, LANES), 0)
    low_lane = (lane[0 : rows // 2] & WIDTH) == 0
    leave = (row_index < WIDTH) == jnp.logical_not(first_z)
    strips = {}
    packed = jnp.zeros((rows, LANES), jnp.float32)
    for f in range(FIELDS):
        for q in range(planes):
            k = f * planes + q
            piece = grown[f][planes + q, 0:rows, 0:LANES]
            strips[f, q] = jnp.where(first_z, piece[rows - ROWS :], piece[0:ROWS])
            moved = shift(piece, 2 * WIDTH * k, 1)
            window = ((lane + (LANES + WIDTH - 2 * WIDTH * k)) & (LANES - 1)) < 2 * WIDTH
            packed = jnp.where(window, moved, packed)
    for slot in range(3):
        for t in range(len(strip_list[slot]) // 2):
            first, second = strip_list[slot][2 * t], strip_list[slot][2 * t + 1]
            pack_rows[slot, t] = jnp.where(
                leave, strips[first], shift(strips[second], WIDTH, 0))
    top, bottom = packed[0 : rows // 2], packed[rows // 2 : rows]
    pack_full[0] = jnp.where(low_lane, shift(bottom, -WIDTH, 1), top)
    pack_full[1] = jnp.where(low_lane, top, shift(bottom, WIDTH, 1))
    pack_edge[...] = jnp.where(first_z, packed[rows - ROWS :], packed[0:ROWS])

    wanted = (count_x * count_z - 1) + count_x * count_z * (
        jnp.where(y > 0, 1, 0) + jnp.where(y < count_y - 1, 1, 0))
    pl.semaphore_wait(barrier, wanted)

    def send(src, dst, send_sem, recv_sem, device, to, back):
        copy = pltpu.make_async_remote_copy(
            src_ref=src, dst_ref=dst, send_sem=send_sem, recv_sem=recv_sem,
            device_id=device, device_id_type=pl.DeviceIdType.MESH)
        if to is None:
            copy.start()
        else:
            pl.when(to)(copy.start)
        return copy, to, back

    def wait_recv(entry):
        copy, _, back = entry
        if back is None:
            copy.wait_recv()
        else:
            pl.when(back)(copy.wait_recv)

    def wait_send(entry):
        copy, to, _ = entry
        if to is None:
            copy.wait_send()
        else:
            pl.when(to)(copy.wait_send)

    faces = []
    strips_sent = []

    def send_face(f):
        for dx in (1, -1):
            to, back = in_range(x + dx, count_x), in_range(x - dx, count_x)
            low, high = 0, planes
            if f == 2:
                low, high = (1, planes) if dx == 1 else (0, planes - 1)
            base = 0 if dx == 1 else 2 * planes
            index = (dx + 1) // 2 * FIELDS + f
            faces.append((f, send(
                grown[f].at[planes + low : planes + high, 0:rows, 0:LANES],
                grown[f].at[base + low : base + high, 0:rows, 0:LANES],
                face_send.at[index], face_recv.at[index],
                {"gx": x + dx, "gy": y, "gz": z}, to, back)))

    send_face(0)
    for dx in (1, -1, 0):
        slot = 1 - dx
        to, back = (in_range(x + dx, count_x), in_range(x - dx, count_x)) if dx else (None, None)
        tiles = len(strip_list[slot]) // 2
        strips_sent.append(send(
            pack_rows.at[slot, 0:tiles], got_rows.at[slot, 0:tiles], row_send.at[slot],
            row_recv.at[slot], {"gx": x + dx, "gy": y, "gz": 1 - z}, to, back))
        for dy in (1, -1):
            side = (1 - dy) // 2
            to = in_range(x + dx, count_x) & in_range(y + dy, count_y)
            back = in_range(x - dx, count_x) & in_range(y - dy, count_y)
            strips_sent.append(send(
                pack_full.at[side], got_full.at[slot, side], full_send.at[slot * 2 + side],
                full_recv.at[slot * 2 + side], {"gx": x + dx, "gy": y + dy, "gz": z}, to, back))
            strips_sent.append(send(
                pack_edge, got_edge.at[slot, side], edge_send.at[slot * 2 + side],
                edge_recv.at[slot * 2 + side], {"gx": x + dx, "gy": y + dy, "gz": 1 - z}, to, back))
    send_face(1)
    send_face(2)

    to_one = [pair_matrix(LANES, 0, 0), pair_matrix(LANES, 0, LANES // 2)]
    matrix_one = jnp.concatenate(to_one, axis=0)
    quarter = (lax.broadcasted_iota(jnp.int32, (ROWS, LANES), 1) & (LANES // 4)) == 0

    def restrict_fine(blocks, scale):
        pairs = [pair_rows(blocks[2 * q] + blocks[2 * q + 1], hold, q) for q in range(planes // 2)]
        return scale * split_dot(jnp.concatenate(pairs, axis=1), matrix_one)

    hopped = (0,)
    here = z * count_x + x
    line = pl.ds(z * count_x, count_x)
    blocks_all = count_x * count_z

    def spread(part, value):
        own_one[part] = value
        top, bottom = value[0:ROWS], value[ROWS : 2 * ROWS]
        own_half[part, 0] = jnp.where(quarter, shift(bottom, -(LANES // 4), 1), top)
        own_half[part, 1] = jnp.where(quarter, top, shift(bottom, LANES // 4, 1))
        all_one[part, here] = value
        for dy in (0, 1, -1):
            side = (1 - dy) // 2

            def start():
                for step, turn, _dy in [p for p in partners if p[2] == dy]:
                    if dy == 0:
                        source, target = own_one.at[part], all_one.at[part, here]
                    else:
                        source, target = own_half.at[part, side], all_half.at[part, side, here]
                    pltpu.make_async_remote_copy(
                        src_ref=source, dst_ref=target, send_sem=one_send.at[part, dy + 1],
                        recv_sem=one_recv.at[part, dy + 1], device_id=other(step, turn, dy),
                        device_id_type=pl.DeviceIdType.MESH).start()

            if dy == 0:
                start()
            else:
                pl.when(in_range(y + dy, count_y))(start)

    def remote(source, target, send_sem, recv_sem, device):
        return pltpu.make_async_remote_copy(
            src_ref=source, dst_ref=target, send_sem=send_sem, recv_sem=recv_sem,
            device_id=device, device_id_type=pl.DeviceIdType.MESH)

    def first_hop(part, value):
        own_one[part] = value
        all_one[part, here] = value
        for step in range(1, count_x):
            remote(own_one.at[part], all_one.at[part, here], hop_send.at[part],
                   hop_recv.at[part], other(step, 0, 0)).start()

    def settle_hop(part, received):
        bytes_of = all_one.at[part, 0 : count_x - 1]
        copy = remote(bytes_of, bytes_of, hop_send.at[part], hop_recv.at[part], other(1, 0, 0))
        copy.wait_recv() if received else copy.wait_send()

    def line_copies(part, dy):
        side = (1 - dy) // 2
        sems = (one_send.at[part, dy + 1], one_recv.at[part, dy + 1])
        if dy == 0:
            return [remote(all_one.at[part, line], all_one.at[part, line], *sems, other(0, 1, 0))]
        return [
            remote(line_half.at[part, side], all_half.at[part, side, line], *sems,
                   other(0, turn, dy))
            for turn in range(count_z)
        ]

    def second_hop(part):
        for from_x in range(count_x):
            value = all_one[part, z * count_x + from_x]
            top, bottom = value[0:ROWS], value[ROWS : 2 * ROWS]
            line_half[part, 0, from_x] = jnp.where(quarter, shift(bottom, -(LANES // 4), 1), top)
            line_half[part, 1, from_x] = jnp.where(quarter, top, shift(bottom, LANES // 4, 1))
        for dy in (0, 1, -1):
            def start():
                for copy in line_copies(part, dy):
                    copy.start()

            if dy == 0:
                start()
            else:
                pl.when(in_range(y + dy, count_y))(start)

    def settle(part, received):
        for dy in (0, 1, -1):
            side = (1 - dy) // 2
            if dy == 0:
                extent = count_x if part in hopped else blocks_all - 1
                bytes_of = all_one.at[part, 0:extent]
            else:
                bytes_of = all_half.at[part, side]
            copy = remote(bytes_of, bytes_of, one_send.at[part, dy + 1],
                          one_recv.at[part, dy + 1], other(1, 0, 0))
            finish = copy.wait_recv if received else copy.wait_send
            if dy == 0:
                finish()
            else:
                pl.when(in_range(y - dy if received else y + dy, count_y))(finish)

    coarse_conduct = restrict_fine(
        [grown[0][planes + q, 0:rows, 0:LANES] for q in range(planes)], 0.125)
    first_hop(0, coarse_conduct)

    for entry in strips_sent:
        wait_recv(entry)
    row_keep = (row_index < WIDTH) == first_z
    lane_edge = lax.broadcasted_iota(jnp.int32, (rows + ROWS, LANES), 1)
    lane_keep = (lane_edge < WIDTH) | (lane_edge >= LANES - WIDTH)
    low_edge = low_lane[0:ROWS]
    joined = []
    for slot in range(3):
        low, high = got_full[slot, 1], got_full[slot, 0]
        joined.append(jnp.concatenate([
            jnp.where(low_lane, low, high),
            jnp.where(low_lane, shift(low, -WIDTH, 1), shift(high, WIDTH, 1)),
            jnp.where(row_keep, jnp.where(low_edge, got_edge[slot, 1], got_edge[slot, 0]), 0.0),
        ], axis=0))
    for f in range(FIELDS):
        for slot in range(3):
            for q in range(planes):
                p = slot * planes + q
                strip = jnp.zeros((ROWS, LANES), jnp.float32)
                if (f, q) in strip_list[slot]:
                    index = strip_list[slot].index((f, q))
                    strip = got_rows[slot, index // 2]
                    if index % 2 == 1:
                        strip = shift(strip, WIDTH, 0)
                    strip = jnp.where(row_keep, strip, 0.0)
                grown[f][p, rows : rows + ROWS, 0:LANES] = strip
                grown[f][p, :, LANES : 2 * LANES] = jnp.where(
                    lane_keep, shift(joined[slot], -2 * WIDTH * (f * planes + q), 1), 0.0)

    def wait_face(f):
        for index, entry in faces:
            if index == f:
                wait_recv(entry)

    wait_face(0)
    faces_fine = face_planes([grown[0][p] for p in range(3 * planes)], True)
    wait_face(1)
    start = [grown[1][p] for p in range(3 * planes)]
    applied = operate_planes(faces_fine, start, 1, 3 * planes - 1)
    wait_face(2)
    residual = [None] * (3 * planes)
    for p in range(1, 3 * planes - 1):
        residual[p] = grown[2][p] - applied[p]
    solved, residual = smooth_planes(
        faces_fine, residual, start, True, (rows, LANES))
    spread(
        1, restrict_fine([residual[planes + q] for q in range(planes)], 0.25))
    settle_hop(0, True)
    second_hop(0)
    for q in range(planes):
        out_fine[q] = solved[planes + q][0:rows, 0:LANES]
    stores[0].start()

    lane_one = lax.broadcasted_iota(jnp.int32, (2 * ROWS, LANES), 1)
    lower = lane_one < LANES // 2

    def assemble(part):
        level = []
        for from_x in range(count_x):
            blocks = [[], []]
            for from_z in range(count_z):
                block = from_z * count_x + from_x
                own = all_one[part, block]
                low, high = all_half[part, 0, block], all_half[part, 1, block]
                beside = jnp.concatenate(
                    [jnp.where(quarter, high, low),
                     jnp.where(quarter, shift(high, -(LANES // 4), 1), shift(low, LANES // 4, 1))],
                    axis=0)
                blocks[0].append(jnp.where(lower, own, shift(beside, LANES // 2, 1)))
                blocks[1].append(jnp.where(lower, shift(own, LANES // 2, 1), beside))
            for q in range(2):
                level.append(jnp.concatenate(blocks[q], axis=0))
        return level

    def restrict(level, matrix, scale):
        length = level[0].shape[0]
        summed = []
        for q in range(len(level) // 2):
            both = level[2 * q] + level[2 * q + 1]
            summed.append(pair_rows(both, hold, q))
        joined = scale * split_dot(jnp.concatenate(summed, axis=0), matrix)
        half = length // 2
        return [joined[q * half : (q + 1) * half] for q in range(len(summed))]

    matrix_two = pair_matrix(3 * LANES // 4, LANES // 4, 0)
    matrix_three = pair_matrix(3 * LANES // 8, LANES // 8, 0)
    settle(0, True)
    conduct_one = assemble(0)
    conduct_two = restrict(conduct_one, matrix_two, 0.125)
    conduct_three = restrict(conduct_two, matrix_three, 0.125)
    faces_one, faces_two, faces_three = (
        coarse_faces(conduct) for conduct in (conduct_one, conduct_two, conduct_three))

    settle(1, True)
    solved, residual = smooth_planes(faces_one, assemble(1), None, False)
    for p in range(len(solved)):
        block = solved[p][0 : 2 * rows // 2]
        solved_one[p] = jnp.where(first_z, block[0 : rows // 2], block[rows // 2 : rows])
    out_one[...] = solved_one[pl.ds(2 * x, 2), :, 0 : LANES // 2]
    stores[1].start()
    solved, residual = smooth_planes(
        faces_two, restrict(residual, matrix_two, 0.25), None, False)
    for p in range(len(solved)):
        half = rows // 4
        out_two[p] = jnp.where(first_z, solved[p][0:half], solved[p][half : 2 * half])[:, 0 : LANES // 4]
    stores[2].start()
    solved, residual = smooth_planes(
        faces_three, restrict(residual, matrix_three, 0.25), None, False)
    for p in range(len(solved)):
        half = rows // 8
        for result, out in ((solved, out_three), (residual, out_rest)):
            out[p] = jnp.where(first_z, result[p][0:half], result[p][half : 2 * half])[:, 0 : LANES // 8]

    stores[3].start()
    stores[4].start()
    for entry in strips_sent + [entry for _, entry in faces]:
        wait_send(entry)
    settle_hop(0, False)
    settle(0, False)
    settle(1, False)
    for store in stores:
        store.wait()


def hand_over(*refs):
    count = len(refs) // 2
    copies = []
    for i in range(count):
        copies.append(pltpu.make_async_copy(refs[i], refs[count + i], refs[-1].at[i]))
        copies[-1].start()
    for copy in copies:
        copy.wait()


def fits(mesh, shape):
    return (
        mesh.shape["gz"] == 2
        and mesh.shape["gx"] <= 4
        and shape[0] == WIDTH * mesh.shape["gx"]
        and shape[1] == 32 * mesh.shape["gz"]
        and shape[2] == LANES * mesh.shape["gy"]
    )


def fused(mesh, conductivity, initial_guess, right_side):
    sizes = (mesh.shape["gx"], mesh.shape["gy"], mesh.shape["gz"])
    count_x, _, count_z = sizes
    planes, rows, lanes = conductivity.shape
    f32 = jnp.float32
    shapes = [
        (planes, rows, lanes),
        (planes // 2, rows // 2, lanes // 2),
        (count_x * planes // 4, rows // 4, lanes // 4),
        (count_x * planes // 8, rows // 8, lanes // 8),
        (count_x * planes // 8, rows // 8, lanes // 8),
    ]
    blocks_all = count_x * count_z
    dma = pltpu.SemaphoreType.DMA
    scratch = [pltpu.VMEM((3 * planes, rows + ROWS, 2 * LANES), f32)] * FIELDS + [
        pltpu.VMEM((2, rows // 2, LANES), f32),
        pltpu.VMEM((ROWS, LANES), f32),
        pltpu.VMEM((3, FIELDS * planes // 2, ROWS, LANES), f32),
        pltpu.VMEM((3, 2, rows // 2, LANES), f32),
        pltpu.VMEM((3, 2, ROWS, LANES), f32),
        pltpu.VMEM((3, FIELDS * planes // 2, ROWS, LANES), f32),
        pltpu.VMEM((2, rows // 2, LANES), f32),
        pltpu.VMEM((2, 2, ROWS, LANES), f32),
        pltpu.VMEM((2, 2, count_x, ROWS, LANES), f32),
        pltpu.VMEM((2, blocks_all, rows // 2, LANES), f32),
        pltpu.VMEM((2, 2, blocks_all, ROWS, LANES), f32),
        pltpu.VMEM((count_x, rows, LANES), f32),
        pltpu.VMEM((2 * count_x, rows // 2, LANES), f32),
        *[pltpu.VMEM(shape, f32) for shape in shapes],
        dma((3,)),
        dma((6,)), dma((6,)),
        dma((3,)), dma((3,)),
        dma((6,)), dma((6,)),
        dma((6,)), dma((6,)),
        dma((2, 3)), dma((2, 3)),
        dma((2,)), dma((2,)),
        dma((5,)),
    ]
    outside = pl.BlockSpec(memory_space=pltpu.HBM)
    out_shape = [jax.ShapeDtypeStruct(shape, f32) for shape in shapes]
    results = pl.pallas_call(
        functools.partial(kernel, sizes),
        out_shape=out_shape,
        in_specs=[outside] * 3,
        out_specs=[outside] * 5,
        scratch_shapes=scratch,
        compiler_params=pltpu.CompilerParams(
            collective_id=0, has_side_effects=True, vmem_limit_bytes=56 * 2**20),
    )(conductivity, initial_guess, right_side)
    return pl.pallas_call(
        hand_over,
        out_shape=out_shape,
        in_specs=[pl.BlockSpec(memory_space=pltpu.VMEM)] * 5,
        out_specs=[outside] * 5,
        scratch_shapes=[dma((5,))],
        compiler_params=pltpu.CompilerParams(vmem_limit_bytes=56 * 2**20),
    )(*results)


def solution(mesh):
    placed = (P("gx", "gz", "gy"), P("gx", "gz", "gy"), P("gx", "gz", "gy"))

    def whole(conductivity, initial_guess, right_side):
        local = shards
        if fits(mesh, conductivity.shape):
            local = functools.partial(fused, mesh)
        return jax.shard_map(
            local,
            mesh=mesh,
            in_specs=placed,
            out_specs=(
                P("gx", "gz", "gy"),
                P("gx", "gz", "gy"),
                P(None, "gz", "gy"),
                P(None, "gz", "gy"),
                P(None, "gz", "gy"),
            ),
            check_vma=False,
        )(conductivity, initial_guess, right_side)

    return whole
```

```python
import functools

import jax
import jax.numpy as jnp
from jax import lax
from jax.experimental import pallas as pl
from jax.experimental.pallas import tpu as pltpu
from jax.sharding import PartitionSpec as P

SWEEPS = 3


lower_bound = 0.25
upper_bound = 2.0


def with_halo(block, sides, width):
    for axis, dim in sides:
        count = lax.axis_size(axis)
        forward = [(i, i + 1) for i in range(count - 1)]
        backward = [(target, source) for source, target in forward]
        low = lax.ppermute(
            lax.slice_in_dim(block, block.shape[dim] - width, None, axis=dim), axis, forward
        )
        high = lax.ppermute(lax.slice_in_dim(block, 0, width, axis=dim), axis, backward)
        block = jnp.concatenate([low, block, high], axis=dim)
    return block


def extend(bundle):
    return with_halo(bundle, (("gx", 1), ("gy", 3), ("gz", 2)), 1)


def deep_extend(bundle, merged):
    if merged:
        grown = with_halo(bundle, (("gy", 3), ("gz", 2)), 4)
        return jnp.pad(grown, ((0, 0), (4, 4), (0, 0), (0, 0)))
    return with_halo(bundle, (("gx", 1), ("gy", 3), ("gz", 2)), 4)


def neighbours(padded):
    return [
        padded[:-2, 1:-1, 1:-1],
        padded[2:, 1:-1, 1:-1],
        padded[1:-1, :-2, 1:-1],
        padded[1:-1, 2:, 1:-1],
        padded[1:-1, 1:-1, :-2],
        padded[1:-1, 1:-1, 2:],
    ]


def face_terms(conduct):
    others = neighbours(extend(conduct[None])[0])
    weights = [0.5 * (conduct + other) for other in others]
    diagonal = weights[0] + weights[1] + weights[2] + weights[3] + weights[4] + weights[5]
    return (weights, diagonal)


def operate(field, weights, diagonal):
    others = neighbours(extend(field[None])[0])
    result = diagonal * field
    for face_index in range(6):
        result = result - weights[face_index] * others[face_index]
    return result


def smooth(source, conduct):
    theta = 0.5 * (upper_bound + lower_bound)
    delta = 0.5 * (upper_bound - lower_bound)
    sigma = theta / delta
    weights, diagonal = face_terms(conduct)
    solution = jnp.zeros_like(source)
    residual = source
    direction = residual / (theta * diagonal)
    ratio_now = 1.0 / sigma
    for sweep_index in range(SWEEPS):
        solution = solution + direction
        residual = residual - operate(direction, weights, diagonal)
        if sweep_index + 1 < SWEEPS:
            ratio_next = 1.0 / (2.0 * sigma - ratio_now)
            direction = (
                ratio_next * ratio_now * direction + 2.0 * ratio_next / delta * residual / diagonal
            )
            ratio_now = ratio_next
    return (solution, residual)


def local_operate(field, weights, diagonal):
    others = neighbours(jnp.pad(field, 1))
    result = diagonal * field
    for face_index in range(6):
        result = result - weights[face_index] * others[face_index]
    return result


def smooth_deep(source, start, conduct, merged):
    theta = 0.5 * (upper_bound + lower_bound)
    delta = 0.5 * (upper_bound - lower_bound)
    sigma = theta / delta
    members = [conduct, source, jnp.ones_like(source)]
    if start is not None:
        members.append(start)
    grown = deep_extend(jnp.stack(members), merged)
    padded_conduct = grown[0]
    padded_source = grown[1]
    inside = grown[2]
    others = neighbours(jnp.pad(padded_conduct, 1))
    weights = [0.5 * (padded_conduct + other) for other in others]
    diagonal = weights[0] + weights[1] + weights[2] + weights[3] + weights[4] + weights[5]
    safe_diagonal = jnp.where(inside > 0.5, diagonal, 1.0)
    if start is None:
        solution = jnp.zeros_like(padded_source)
        residual = padded_source
    else:
        solution = grown[3]
        residual = padded_source - local_operate(solution, weights, diagonal)
    direction = inside * (residual / (theta * safe_diagonal))
    ratio_now = 1.0 / sigma
    for sweep_index in range(SWEEPS):
        solution = solution + direction
        residual = residual - local_operate(direction, weights, diagonal)
        if sweep_index + 1 < SWEEPS:
            ratio_next = 1.0 / (2.0 * sigma - ratio_now)
            direction = inside * (
                ratio_next * ratio_now * direction
                + 2.0 * ratio_next / delta * residual / safe_diagonal
            )
            ratio_now = ratio_next
    return (solution[4:-4, 4:-4, 4:-4], residual[4:-4, 4:-4, 4:-4])


def level_smooth(source, start, conduct, merged):
    extents = source.shape[1:] if merged else source.shape
    if min(extents) >= 4:
        return smooth_deep(source, start, conduct, merged)
    return smooth(source, conduct)


def coarse_sum(field):
    first, second, third = field.shape
    blocks = field.reshape(first // 2, 2, second // 2, 2, third // 2, 2)
    return jnp.sum(blocks, axis=(1, 3, 5))


def shards(conductivity, initial_guess, right_side):
    fine_solution, residual_zero = level_smooth(right_side, initial_guess, conductivity, False)
    conduct_one = 0.125 * coarse_sum(conductivity)
    level_one_solution, residual_one = level_smooth(
        0.25 * coarse_sum(residual_zero), None, conduct_one, False
    )
    conduct_two = 0.125 * coarse_sum(conduct_one)
    source_two = 0.25 * coarse_sum(residual_one)
    bundle = jnp.stack([source_two, conduct_two])
    bundle = lax.all_gather(bundle, "gx", axis=1, tiled=True)
    level_two_solution, residual_two = level_smooth(bundle[0], None, bundle[1], True)
    conduct_three = 0.125 * coarse_sum(bundle[1])
    level_three_solution, level_three_residual = level_smooth(
        0.25 * coarse_sum(residual_two), None, conduct_three, True
    )
    return (
        fine_solution,
        level_one_solution,
        level_two_solution,
        level_three_solution,
        level_three_residual,
    )


FIELDS = 3
WIDTH = 4
ROWS = 8
LANES = 128


def in_range(index, count):
    return (index >= 0) & (index < count)


def shift(value, amount, axis):
    return pltpu.roll(value, amount % value.shape[axis], axis)


def face_planes(conduct, grown):
    count = len(conduct)
    edge = 1 if grown else 0
    weight_x = [None] * (count + 1)
    for i in range(1, count):
        weight_x[i] = 0.5 * (conduct[i - 1] + conduct[i])
    if not grown:
        weight_x[0] = 0.5 * conduct[0]
        weight_x[count] = 0.5 * conduct[count - 1]
    weight_z = [None] * count
    weight_y = [None] * count
    inverse = [None] * count
    for i in range(edge, count - edge):
        weight_z[i] = 0.5 * (conduct[i] + shift(conduct[i], -1, 0))
        weight_y[i] = 0.5 * (conduct[i] + shift(conduct[i], -1, 1))
        diagonal = weight_x[i] + weight_x[i + 1]
        diagonal = diagonal + (weight_z[i] + shift(weight_z[i], 1, 0))
        diagonal = diagonal + (weight_y[i] + shift(weight_y[i], 1, 1))
        inside = conduct[i] > 0.0
        inverse[i] = jnp.where(inside, 1.0 / jnp.where(inside, diagonal, 1.0), 0.0)
    return weight_x, weight_y, weight_z, inverse


def operate_planes(faces, field, low, high, keep=None):
    weight_x, weight_y, weight_z, _ = faces
    count = len(field)
    flux_x = [None] * (count + 1)
    for i in range(low, high + 1):
        if i == 0:
            flux_x[i] = weight_x[i] * field[i]
        elif i == count:
            flux_x[i] = -(weight_x[i] * field[i - 1])
        else:
            flux_x[i] = weight_x[i] * (field[i] - field[i - 1])
    result = [None] * count
    rows, lanes = keep if keep is not None else field[low].shape
    for i in range(low, high):
        flux_z = weight_z[i] * (field[i] - shift(field[i], -1, 0))
        flux_y = weight_y[i] * (field[i] - shift(field[i], -1, 1))
        flux_z, flux_y = flux_z[:, 0:lanes], flux_y[0:rows]
        result[i] = (
            (flux_x[i] - flux_x[i + 1])[0:rows, 0:lanes]
            + (flux_z - shift(flux_z, 1, 0))[0:rows]
            + (flux_y - shift(flux_y, 1, 1))[:, 0:lanes]
        )
    return result


def coarse_faces(conduct):
    count, length = len(conduct), conduct[0].shape[0]
    row = lax.broadcasted_iota(jnp.int32, conduct[0].shape, 0)
    first, last = row == 0, row == length - 1
    weights, diagonals, inverses = [], [], []
    for i in range(count):
        own = conduct[i]
        half = 0.5 * own
        below = 0.5 * (own + conduct[i - 1]) if i > 0 else half
        above = 0.5 * (own + conduct[i + 1]) if i + 1 < count else half
        before = jnp.where(first, half, 0.5 * (own + shift(own, 1, 0)))
        after = jnp.where(last, half, 0.5 * (own + shift(own, -1, 0)))
        left = 0.5 * (own + shift(own, 1, 1))
        right = 0.5 * (own + shift(own, -1, 1))
        diagonal = (below + above) + (before + after) + (left + right)
        inside = own > 0.0
        diagonals.append(diagonal)
        inverses.append(jnp.where(inside, 1.0 / jnp.where(inside, diagonal, 1.0), 0.0))
        before = jnp.where(first, 0.0, before)
        after = jnp.where(last, 0.0, after)
        weights.append((below, above, before, after, left, right))
    return weights, diagonals, None, inverses


def operate_coarse(faces, field):
    weights, diagonals = faces[0], faces[1]
    count = len(field)
    result = []
    for i in range(count):
        below, above, before, after, left, right = weights[i]
        own = field[i]
        value = diagonals[i] * own
        if i > 0:
            value = value - below * field[i - 1]
        if i + 1 < count:
            value = value - above * field[i + 1]
        rolled = before * shift(own, 1, 0) + after * shift(own, -1, 0)
        rolled = rolled + (left * shift(own, 1, 1) + right * shift(own, -1, 1))
        result.append(value - rolled)
    return result


def smooth_planes(faces, residual, start, grown, block=None):
    theta = 0.5 * (upper_bound + lower_bound)
    delta = 0.5 * (upper_bound - lower_bound)
    sigma = theta / delta
    inverse = faces[3]
    count = len(residual)
    edge = 1 if grown else 0
    low, high = edge, count - edge
    residual = list(residual)
    direction = [None] * count
    for i in range(low, high):
        direction[i] = residual[i] * (inverse[i] * (1.0 / theta))
    ratio_now = 1.0 / sigma
    solution = list(start) if start is not None else [None] * count
    for sweep_index in range(SWEEPS):
        for i in range(low, high):
            solution[i] = direction[i] if solution[i] is None else solution[i] + direction[i]
        low, high = low + edge, high - edge
        if grown:
            keep = block if sweep_index + 1 == SWEEPS else None
            applied = operate_planes(faces, direction, low, high, keep)
        else:
            applied = operate_coarse(faces, direction)
        for i in range(low, high):
            extent = applied[i].shape
            residual[i] = residual[i][0 : extent[0], 0 : extent[1]] - applied[i]
        if sweep_index + 1 < SWEEPS:
            ratio_next = 1.0 / (2.0 * sigma - ratio_now)
            turned = [None] * count
            for i in range(low, high):
                turned[i] = (ratio_next * ratio_now) * direction[i] + (
                    2.0 * ratio_next / delta
                ) * (residual[i] * inverse[i])
            direction = turned
            ratio_now = ratio_next
    return solution, residual


def split_dot(value, matrix):
    parts = []
    rest = value
    for _ in range(3):
        part = rest.astype(jnp.bfloat16)
        parts.append(part.astype(jnp.float32))
        rest = rest - parts[-1]
    rows = value.shape[0]
    stacked = jnp.concatenate(parts, axis=0).astype(jnp.bfloat16)
    product = jnp.dot(stacked, matrix, preferred_element_type=jnp.float32)
    return product[:rows] + product[rows : 2 * rows] + product[2 * rows :]


def pair_matrix(keep_low, keep_high, offset):
    source = lax.broadcasted_iota(jnp.int32, (LANES, LANES), 0)
    target = lax.broadcasted_iota(jnp.int32, (LANES, LANES), 1)
    low = (source < keep_low) & (target == offset + (source >> 1))
    high = (source >= LANES - keep_high) & (target == LANES // 2 + (source >> 1))
    return jnp.where(low | high, 1.0, 0.0).astype(jnp.bfloat16)


def pair_rows(value, hold, q):
    rows = value.shape[0]
    hold[q, 0:rows, :] = value
    even = hold[q, pl.ds(0, rows // 2, stride=2), :]
    return even + hold[q, pl.ds(1, rows // 2, stride=2), :]


def kernel(sizes, *refs):
    count_x, count_y, count_z = sizes
    inputs = refs[0:3]
    outs = refs[3:8]
    grown = refs[8:11]
    (pack_full, pack_edge, pack_rows, got_full, got_edge, got_rows, own_one, own_half, line_half, all_one,
     all_half, hold, solved_one, out_fine, out_one, out_two,
     out_three, out_rest, load_sem, face_send, face_recv, row_send, row_recv,
     full_send, full_recv, edge_send, edge_recv, one_send, one_recv, hop_send, hop_recv, store_sem) = refs[11:]
    kept = (out_fine, out_one, out_two, out_three, out_rest)
    stores = [pltpu.make_async_copy(kept[i], outs[i], store_sem.at[i]) for i in range(5)]
    planes, rows = inputs[0].shape[0], inputs[0].shape[1]
    x = lax.axis_index("gx")
    y = lax.axis_index("gy")
    z = lax.axis_index("gz")
    first_z = z == 0

    loads = []
    for f in range(FIELDS):
        loads.append(pltpu.make_async_copy(
            inputs[f], grown[f].at[planes : 2 * planes, 0:rows, 0:LANES], load_sem.at[f]))
        loads[-1].start()

    def other(step, turn, dy):
        return {"gx": lax.rem(x + step, count_x), "gy": y + dy, "gz": lax.rem(z + turn, count_z)}

    near = planes - WIDTH
    strip_list = [
        [(f, q) for f in range(FIELDS) for q in range(planes)
         if q > near + (1 if f == 2 else 0)],
        [(f, q) for f in range(FIELDS) for q in range(planes)],
        [(f, q) for f in range(FIELDS) for q in range(planes)
         if q < WIDTH - 1 - (1 if f == 2 else 0)],
    ]
    partners = [
        (step, turn, dy)
        for step in sorted(range(count_x), key=lambda step: -min(step, count_x - step))
        for turn in range(count_z)
        for dy in (0, -1, 1)
        if (step, turn, dy) != (0, 0, 0)
    ]
    barrier = pltpu.get_barrier_semaphore()
    for dy in (0, -1, 1):
        @pl.when(in_range(y + dy, count_y))
        def _():
            chosen = [p for p in partners if p[2] == dy]
            for step, turn, _dy in chosen:
                pl.semaphore_signal(
                    barrier, inc=1, device_id=other(step, turn, dy),
                    device_id_type=pl.DeviceIdType.MESH)

    for f in range(FIELDS):
        @pl.when(x == 0)
        def _():
            grown[f][0:planes, 0:rows, 0:LANES] = jnp.zeros((planes, rows, LANES), jnp.float32)

        @pl.when(x == count_x - 1)
        def _():
            grown[f][2 * planes : 3 * planes, 0:rows, 0:LANES] = jnp.zeros(
                (planes, rows, LANES), jnp.float32)

    for slot in range(3):
        for side in range(2):
            there = in_range(x + (slot - 1), count_x) & in_range(y + (2 * side - 1), count_y)

            @pl.when(jnp.logical_not(there))
            def _():
                got_full[slot, side] = jnp.zeros((rows // 2, LANES), jnp.float32)
                got_edge[slot, side] = jnp.zeros((ROWS, LANES), jnp.float32)

        if slot != 1:
            @pl.when(jnp.logical_not(in_range(x + (slot - 1), count_x)))
            def _():
                got_rows[slot] = jnp.zeros(got_rows.shape[1:], jnp.float32)

    for side in range(2):
        @pl.when(jnp.logical_not(in_range(y + (2 * side - 1), count_y)))
        def _():
            for part in range(2):
                all_half[part, side] = jnp.zeros(all_half.shape[2:], jnp.float32)

    for load in loads:
        load.wait()

    lane = lax.broadcasted_iota(jnp.int32, (rows, LANES), 1)
    row_index = lax.broadcasted_iota(jnp.int32, (ROWS, LANES), 0)
    low_lane = (lane[0 : rows // 2] & WIDTH) == 0
    leave = (row_index < WIDTH) == jnp.logical_not(first_z)
    strips = {}
    packed = jnp.zeros((rows, LANES), jnp.float32)
    for f in range(FIELDS):
        for q in range(planes):
            k = f * planes + q
            piece = grown[f][planes + q, 0:rows, 0:LANES]
            strips[f, q] = jnp.where(first_z, piece[rows - ROWS :], piece[0:ROWS])
            moved = shift(piece, 2 * WIDTH * k, 1)
            window = ((lane + (LANES + WIDTH - 2 * WIDTH * k)) & (LANES - 1)) < 2 * WIDTH
            packed = jnp.where(window, moved, packed)
    for slot in range(3):
        for t in range(len(strip_list[slot]) // 2):
            first, second = strip_list[slot][2 * t], strip_list[slot][2 * t + 1]
            pack_rows[slot, t] = jnp.where(
                leave, strips[first], shift(strips[second], WIDTH, 0))
    top, bottom = packed[0 : rows // 2], packed[rows // 2 : rows]
    pack_full[0] = jnp.where(low_lane, shift(bottom, -WIDTH, 1), top)
    pack_full[1] = jnp.where(low_lane, top, shift(bottom, WIDTH, 1))
    pack_edge[...] = jnp.where(first_z, packed[rows - ROWS :], packed[0:ROWS])

    wanted = (count_x * count_z - 1) + count_x * count_z * (
        jnp.where(y > 0, 1, 0) + jnp.where(y < count_y - 1, 1, 0))
    pl.semaphore_wait(barrier, wanted)

    def send(src, dst, send_sem, recv_sem, device, to, back):
        copy = pltpu.make_async_remote_copy(
            src_ref=src, dst_ref=dst, send_sem=send_sem, recv_sem=recv_sem,
            device_id=device, device_id_type=pl.DeviceIdType.MESH)
        if to is None:
            copy.start()
        else:
            pl.when(to)(copy.start)
        return copy, to, back

    def wait_recv(entry):
        copy, _, back = entry
        if back is None:
            copy.wait_recv()
        else:
            pl.when(back)(copy.wait_recv)

    def wait_send(entry):
        copy, to, _ = entry
        if to is None:
            copy.wait_send()
        else:
            pl.when(to)(copy.wait_send)

    faces = []
    strips_sent = []

    def send_face(f):
        for dx in (1, -1):
            to, back = in_range(x + dx, count_x), in_range(x - dx, count_x)
            low, high = 0, planes
            if f == 2:
                low, high = (1, planes) if dx == 1 else (0, planes - 1)
            base = 0 if dx == 1 else 2 * planes
            index = (dx + 1) // 2 * FIELDS + f
            faces.append((f, send(
                grown[f].at[planes + low : planes + high, 0:rows, 0:LANES],
                grown[f].at[base + low : base + high, 0:rows, 0:LANES],
                face_send.at[index], face_recv.at[index],
                {"gx": x + dx, "gy": y, "gz": z}, to, back)))

    for dx in (1, -1, 0):
        slot = 1 - dx
        to, back = (in_range(x + dx, count_x), in_range(x - dx, count_x)) if dx else (None, None)
        tiles = len(strip_list[slot]) // 2
        strips_sent.append(send(
            pack_rows.at[slot, 0:tiles], got_rows.at[slot, 0:tiles], row_send.at[slot],
            row_recv.at[slot], {"gx": x + dx, "gy": y, "gz": 1 - z}, to, back))
        for dy in (1, -1):
            side = (1 - dy) // 2
            to = in_range(x + dx, count_x) & in_range(y + dy, count_y)
            back = in_range(x - dx, count_x) & in_range(y - dy, count_y)
            strips_sent.append(send(
                pack_full.at[side], got_full.at[slot, side], full_send.at[slot * 2 + side],
                full_recv.at[slot * 2 + side], {"gx": x + dx, "gy": y + dy, "gz": z}, to, back))
            strips_sent.append(send(
                pack_edge, got_edge.at[slot, side], edge_send.at[slot * 2 + side],
                edge_recv.at[slot * 2 + side], {"gx": x + dx, "gy": y + dy, "gz": 1 - z}, to, back))
    send_face(0)
    send_face(1)
    send_face(2)

    to_one = [pair_matrix(LANES, 0, 0), pair_matrix(LANES, 0, LANES // 2)]
    matrix_one = jnp.concatenate(to_one, axis=0)
    quarter = (lax.broadcasted_iota(jnp.int32, (ROWS, LANES), 1) & (LANES // 4)) == 0

    def restrict_fine(blocks, scale):
        pairs = [pair_rows(blocks[2 * q] + blocks[2 * q + 1], hold, q) for q in range(planes // 2)]
        return scale * split_dot(jnp.concatenate(pairs, axis=1), matrix_one)

    hopped = (0,)
    here = z * count_x + x
    line = pl.ds(z * count_x, count_x)
    blocks_all = count_x * count_z

    def spread(part, value):
        own_one[part] = value
        top, bottom = value[0:ROWS], value[ROWS : 2 * ROWS]
        own_half[part, 0] = jnp.where(quarter, shift(bottom, -(LANES // 4), 1), top)
        own_half[part, 1] = jnp.where(quarter, top, shift(bottom, LANES // 4, 1))
        all_one[part, here] = value
        for dy in (0, 1, -1):
            side = (1 - dy) // 2

            def start():
                for step, turn, _dy in [p for p in partners if p[2] == dy]:
                    if dy == 0:
                        source, target = own_one.at[part], all_one.at[part, here]
                    else:
                        source, target = own_half.at[part, side], all_half.at[part, side, here]
                    pltpu.make_async_remote_copy(
                        src_ref=source, dst_ref=target, send_sem=one_send.at[part, dy + 1],
                        recv_sem=one_recv.at[part, dy + 1], device_id=other(step, turn, dy),
                        device_id_type=pl.DeviceIdType.MESH).start()

            if dy == 0:
                start()
            else:
                pl.when(in_range(y + dy, count_y))(start)

    def remote(source, target, send_sem, recv_sem, device):
        return pltpu.make_async_remote_copy(
            src_ref=source, dst_ref=target, send_sem=send_sem, recv_sem=recv_sem,
            device_id=device, device_id_type=pl.DeviceIdType.MESH)

    def first_hop(part, value):
        own_one[part] = value
        all_one[part, here] = value
        for step in range(1, count_x):
            remote(own_one.at[part], all_one.at[part, here], hop_send.at[part],
                   hop_recv.at[part], other(step, 0, 0)).start()

    def settle_hop(part, received):
        bytes_of = all_one.at[part, 0 : count_x - 1]
        copy = remote(bytes_of, bytes_of, hop_send.at[part], hop_recv.at[part], other(1, 0, 0))
        copy.wait_recv() if received else copy.wait_send()

    def line_copies(part, dy):
        side = (1 - dy) // 2
        sems = (one_send.at[part, dy + 1], one_recv.at[part, dy + 1])
        if dy == 0:
            return [remote(all_one.at[part, line], all_one.at[part, line], *sems, other(0, 1, 0))]
        return [
            remote(line_half.at[part, side], all_half.at[part, side, line], *sems,
                   other(0, turn, dy))
            for turn in range(count_z)
        ]

    def second_hop(part):
        for from_x in range(count_x):
            value = all_one[part, z * count_x + from_x]
            top, bottom = value[0:ROWS], value[ROWS : 2 * ROWS]
            line_half[part, 0, from_x] = jnp.where(quarter, shift(bottom, -(LANES // 4), 1), top)
            line_half[part, 1, from_x] = jnp.where(quarter, top, shift(bottom, LANES // 4, 1))
        for dy in (0, 1, -1):
            def start():
                for copy in line_copies(part, dy):
                    copy.start()

            if dy == 0:
                start()
            else:
                pl.when(in_range(y + dy, count_y))(start)

    def settle(part, received):
        for dy in (0, 1, -1):
            side = (1 - dy) // 2
            if dy == 0:
                extent = count_x if part in hopped else blocks_all - 1
                bytes_of = all_one.at[part, 0:extent]
            else:
                bytes_of = all_half.at[part, side]
            copy = remote(bytes_of, bytes_of, one_send.at[part, dy + 1],
                          one_recv.at[part, dy + 1], other(1, 0, 0))
            finish = copy.wait_recv if received else copy.wait_send
            if dy == 0:
                finish()
            else:
                pl.when(in_range(y - dy if received else y + dy, count_y))(finish)

    coarse_conduct = restrict_fine(
        [grown[0][planes + q, 0:rows, 0:LANES] for q in range(planes)], 0.125)
    first_hop(0, coarse_conduct)

    for entry in strips_sent:
        wait_recv(entry)
    row_keep = (row_index < WIDTH) == first_z
    lane_edge = lax.broadcasted_iota(jnp.int32, (rows + ROWS, LANES), 1)
    lane_keep = (lane_edge < WIDTH) | (lane_edge >= LANES - WIDTH)
    low_edge = low_lane[0:ROWS]
    joined = []
    for slot in range(3):
        low, high = got_full[slot, 1], got_full[slot, 0]
        joined.append(jnp.concatenate([
            jnp.where(low_lane, low, high),
            jnp.where(low_lane, shift(low, -WIDTH, 1), shift(high, WIDTH, 1)),
            jnp.where(row_keep, jnp.where(low_edge, got_edge[slot, 1], got_edge[slot, 0]), 0.0),
        ], axis=0))
    for f in range(FIELDS):
        for slot in range(3):
            for q in range(planes):
                p = slot * planes + q
                strip = jnp.zeros((ROWS, LANES), jnp.float32)
                if (f, q) in strip_list[slot]:
                    index = strip_list[slot].index((f, q))
                    strip = got_rows[slot, index // 2]
                    if index % 2 == 1:
                        strip = shift(strip, WIDTH, 0)
                    strip = jnp.where(row_keep, strip, 0.0)
                grown[f][p, rows : rows + ROWS, 0:LANES] = strip
                grown[f][p, :, LANES : 2 * LANES] = jnp.where(
                    lane_keep, shift(joined[slot], -2 * WIDTH * (f * planes + q), 1), 0.0)

    def wait_face(f):
        for index, entry in faces:
            if index == f:
                wait_recv(entry)

    wait_face(0)
    faces_fine = face_planes([grown[0][p] for p in range(3 * planes)], True)
    wait_face(1)
    start = [grown[1][p] for p in range(3 * planes)]
    applied = operate_planes(faces_fine, start, 1, 3 * planes - 1)
    wait_face(2)
    residual = [None] * (3 * planes)
    for p in range(1, 3 * planes - 1):
        residual[p] = grown[2][p] - applied[p]
    solved, residual = smooth_planes(
        faces_fine, residual, start, True, (rows, LANES))
    spread(
        1, restrict_fine([residual[planes + q] for q in range(planes)], 0.25))
    settle_hop(0, True)
    second_hop(0)
    for q in range(planes):
        out_fine[q] = solved[planes + q][0:rows, 0:LANES]
    stores[0].start()

    lane_one = lax.broadcasted_iota(jnp.int32, (2 * ROWS, LANES), 1)
    lower = lane_one < LANES // 2

    def assemble(part):
        level = []
        for from_x in range(count_x):
            blocks = [[], []]
            for from_z in range(count_z):
                block = from_z * count_x + from_x
                own = all_one[part, block]
                low, high = all_half[part, 0, block], all_half[part, 1, block]
                beside = jnp.concatenate(
                    [jnp.where(quarter, high, low),
                     jnp.where(quarter, shift(high, -(LANES // 4), 1), shift(low, LANES // 4, 1))],
                    axis=0)
                blocks[0].append(jnp.where(lower, own, shift(beside, LANES // 2, 1)))
                blocks[1].append(jnp.where(lower, shift(own, LANES // 2, 1), beside))
            for q in range(2):
                level.append(jnp.concatenate(blocks[q], axis=0))
        return level

    def restrict(level, matrix, scale):
        length = level[0].shape[0]
        summed = []
        for q in range(len(level) // 2):
            both = level[2 * q] + level[2 * q + 1]
            summed.append(pair_rows(both, hold, q))
        joined = scale * split_dot(jnp.concatenate(summed, axis=0), matrix)
        half = length // 2
        return [joined[q * half : (q + 1) * half] for q in range(len(summed))]

    matrix_two = pair_matrix(3 * LANES // 4, LANES // 4, 0)
    matrix_three = pair_matrix(3 * LANES // 8, LANES // 8, 0)
    settle(0, True)
    conduct_one = assemble(0)
    conduct_two = restrict(conduct_one, matrix_two, 0.125)
    conduct_three = restrict(conduct_two, matrix_three, 0.125)
    faces_one, faces_two, faces_three = (
        coarse_faces(conduct) for conduct in (conduct_one, conduct_two, conduct_three))

    settle(1, True)
    solved, residual = smooth_planes(faces_one, assemble(1), None, False)
    for p in range(len(solved)):
        block = solved[p][0 : 2 * rows // 2]
        solved_one[p] = jnp.where(first_z, block[0 : rows // 2], block[rows // 2 : rows])
    out_one[...] = solved_one[pl.ds(2 * x, 2), :, 0 : LANES // 2]
    stores[1].start()
    solved, residual = smooth_planes(
        faces_two, restrict(residual, matrix_two, 0.25), None, False)
    for p in range(len(solved)):
        half = rows // 4
        out_two[p] = jnp.where(first_z, solved[p][0:half], solved[p][half : 2 * half])[:, 0 : LANES // 4]
    stores[2].start()
    solved, residual = smooth_planes(
        faces_three, restrict(residual, matrix_three, 0.25), None, False)
    for p in range(len(solved)):
        half = rows // 8
        for result, out in ((solved, out_three), (residual, out_rest)):
            out[p] = jnp.where(first_z, result[p][0:half], result[p][half : 2 * half])[:, 0 : LANES // 8]

    stores[3].start()
    stores[4].start()
    for entry in strips_sent + [entry for _, entry in faces]:
        wait_send(entry)
    settle_hop(0, False)
    settle(0, False)
    settle(1, False)
    for store in stores:
        store.wait()


def hand_over(*refs):
    count = len(refs) // 2
    copies = []
    for i in range(count):
        copies.append(pltpu.make_async_copy(refs[i], refs[count + i], refs[-1].at[i]))
        copies[-1].start()
    for copy in copies:
        copy.wait()


def fits(mesh, shape):
    return (
        mesh.shape["gz"] == 2
        and mesh.shape["gx"] <= 4
        and shape[0] == WIDTH * mesh.shape["gx"]
        and shape[1] == 32 * mesh.shape["gz"]
        and shape[2] == LANES * mesh.shape["gy"]
    )


def fused(mesh, conductivity, initial_guess, right_side):
    sizes = (mesh.shape["gx"], mesh.shape["gy"], mesh.shape["gz"])
    count_x, _, count_z = sizes
    planes, rows, lanes = conductivity.shape
    f32 = jnp.float32
    shapes = [
        (planes, rows, lanes),
        (planes // 2, rows // 2, lanes // 2),
        (count_x * planes // 4, rows // 4, lanes // 4),
        (count_x * planes // 8, rows // 8, lanes // 8),
        (count_x * planes // 8, rows // 8, lanes // 8),
    ]
    blocks_all = count_x * count_z
    dma = pltpu.SemaphoreType.DMA
    scratch = [pltpu.VMEM((3 * planes, rows + ROWS, 2 * LANES), f32)] * FIELDS + [
        pltpu.VMEM((2, rows // 2, LANES), f32),
        pltpu.VMEM((ROWS, LANES), f32),
        pltpu.VMEM((3, FIELDS * planes // 2, ROWS, LANES), f32),
        pltpu.VMEM((3, 2, rows // 2, LANES), f32),
        pltpu.VMEM((3, 2, ROWS, LANES), f32),
        pltpu.VMEM((3, FIELDS * planes // 2, ROWS, LANES), f32),
        pltpu.VMEM((2, rows // 2, LANES), f32),
        pltpu.VMEM((2, 2, ROWS, LANES), f32),
        pltpu.VMEM((2, 2, count_x, ROWS, LANES), f32),
        pltpu.VMEM((2, blocks_all, rows // 2, LANES), f32),
        pltpu.VMEM((2, 2, blocks_all, ROWS, LANES), f32),
        pltpu.VMEM((count_x, rows, LANES), f32),
        pltpu.VMEM((2 * count_x, rows // 2, LANES), f32),
        *[pltpu.VMEM(shape, f32) for shape in shapes],
        dma((3,)),
        dma((6,)), dma((6,)),
        dma((3,)), dma((3,)),
        dma((6,)), dma((6,)),
        dma((6,)), dma((6,)),
        dma((2, 3)), dma((2, 3)),
        dma((2,)), dma((2,)),
        dma((5,)),
    ]
    outside = pl.BlockSpec(memory_space=pltpu.HBM)
    out_shape = [jax.ShapeDtypeStruct(shape, f32) for shape in shapes]
    results = pl.pallas_call(
        functools.partial(kernel, sizes),
        out_shape=out_shape,
        in_specs=[outside] * 3,
        out_specs=[outside] * 5,
        scratch_shapes=scratch,
        compiler_params=pltpu.CompilerParams(
            collective_id=0, has_side_effects=True, vmem_limit_bytes=56 * 2**20),
    )(conductivity, initial_guess, right_side)
    return pl.pallas_call(
        hand_over,
        out_shape=out_shape,
        in_specs=[pl.BlockSpec(memory_space=pltpu.VMEM)] * 5,
        out_specs=[outside] * 5,
        scratch_shapes=[dma((5,))],
        compiler_params=pltpu.CompilerParams(vmem_limit_bytes=56 * 2**20),
    )(*results)


def solution(mesh):
    placed = (P("gx", "gz", "gy"), P("gx", "gz", "gy"), P("gx", "gz", "gy"))

    def whole(conductivity, initial_guess, right_side):
        local = shards
        if fits(mesh, conductivity.shape):
            local = functools.partial(fused, mesh)
        return jax.shard_map(
            local,
            mesh=mesh,
            in_specs=placed,
            out_specs=(
                P("gx", "gz", "gy"),
                P("gx", "gz", "gy"),
                P(None, "gz", "gy"),
                P(None, "gz", "gy"),
                P(None, "gz", "gy"),
            ),
            check_vma=False,
        )(conductivity, initial_guess, right_side)

    return whole
```
